256 devices in a mesh: gx: 8 (over z), gy: 8 (over y, core), gz: 4 (over x).
Axes of the slice: x: 4, y: 4, z: 8, core: 2. Of those that a mesh axis runs over, the one named last changes fastest.
Arguments:
- source: float32 [32, 256, 1024], P('gz', 'gx', 'gy'), may hold values from -8 to 8
- permeability: float32 [32, 256, 1024], P('gz', 'gx', 'gy'), may hold values from 0.01 to 100
- storage: float32 [32, 256, 1024], P('gz', 'gx', 'gy'), may hold values from 0.01 to 0.2
- column_depth: int32 [256, 1024], P('gx', 'gy'), may hold values from 16 to 32
Outputs:
- pressure: float32 [32, 256, 1024], P('gz', 'gx', 'gy')
- history: float32 [3], replicated
The draws below stay inside these ranges and needn't reach their ends.
Inputs may be any that keep to these rules, and one draw needn't show every extreme that they name: A cell (z, x, y) is active when z < column_depth[x, y].
All inputs are finite; a program needn't handle non-finite values.
Results may differ from the reference program's by a relative error of at most 0.0001.
Values sent between devices are 32-bit elements; how exact they have to be, the bound alone decides.
A program may use at most 64 MiB of HBM per device.

```python
import math
import jax
import jax.numpy as jnp
from jax import lax

CZ = 8
CX = 32
CY = 128
ITERS = 3
SWEEPS = 4
NZ = 32
NX = 256
NY = 1024
N_GX = 8
N_GY = 8
N_GZ = 4


def place_ends(values, key, low, largest):
    shape = values.shape
    spot = [jax.random.randint(jax.random.fold_in(key, axis), (), 0, shape[axis]) for axis in range(len(shape))]
    values = values.at[tuple(spot)].set(low)
    longest = shape.index(max(shape))
    spot[longest] = (spot[longest] + 1) % shape[longest]
    return values.at[tuple(spot)].set(largest)


def shard_levels(key, shape, split, low, high):
    def one(dim, blocks):
        draws = jax.random.uniform(jax.random.fold_in(jax.random.fold_in(key, 6), dim), (blocks,), jnp.float32, low / len(split), high / len(split))
        return jnp.repeat(jnp.exp(draws), shape[dim] // blocks).reshape((-1,) + (1,) * (len(shape) - dim - 1))

    factor_of = one(*split[0])
    for cut in split[1:]:
        factor_of = factor_of * one(*cut)
    return factor_of


def scatter_about(own_key, shape, scale, most, cuts=(), kind=jnp.bfloat16):
    gain = shard_levels(own_key, shape, cuts, -0.22, 0.18) if cuts else 1.0
    array = jax.random.normal(own_key, shape, jnp.float32) * scale * gain
    return jnp.minimum(jnp.maximum(array, -most), most).astype(kind)


def setup_inputs(seed: int = 0) -> dict:
    streams_of = jax.random.split(jax.random.key(seed), 5)
    return {
        "source": scatter_about(streams_of[0], (NZ, NX, NY), 1.0, 8.0, ((0, 4), (1, 8), (2, 8)), jnp.float32),
        "permeability": jnp.clip(jnp.exp(math.log(100.0) - 9.2103404 * jax.random.uniform(streams_of[1], (NZ, NX, NY), jnp.float32) ** shard_levels(streams_of[1], (NZ, NX, NY), ((0, 4), (1, 8), (2, 8)), -0.2, 0.2)), 0.01, 100.0),
        "storage": jnp.clip(jnp.exp(math.log(0.2) - 2.9957323 * jax.random.uniform(streams_of[2], (NZ, NX, NY), jnp.float32) ** shard_levels(streams_of[2], (NZ, NX, NY), ((0, 4), (1, 8), (2, 8)), -0.2, 0.2)), 0.01, 0.2),
        "column_depth": place_ends(jax.random.randint(streams_of[3], (NX, NY), NZ // 2, NZ + 1), jax.random.fold_in(streams_of[3], 1), NZ // 2, NZ).astype(jnp.int32),
    }


RELAXATION = 0.9
NEIGHBOURS = ((slice(0, -2), slice(1, -1), slice(1, -1)), (slice(2, None), slice(1, -1), slice(1, -1)), (slice(1, -1), slice(0, -2), slice(1, -1)), (slice(1, -1), slice(2, None), slice(1, -1)), (slice(1, -1), slice(1, -1), slice(0, -2)), (slice(1, -1), slice(1, -1), slice(2, None)))

def prepare(widened):
    perm_all = widened[0]
    active_all = widened[1]
    centre_perm = perm_all[1:-1, 1:-1, 1:-1]
    centre_active = active_all[1:-1, 1:-1, 1:-1]
    couplings = []
    for neighbour in NEIGHBOURS:
        other_perm = perm_all[neighbour]
        other_active = active_all[neighbour]
        couplings.append(centre_active * other_active * 2.0 * centre_perm * other_perm / (centre_perm + other_perm + (1.0 - centre_active) + (1.0 - other_active)))
    diagonal = widened[2][1:-1, 1:-1, 1:-1] + (1.0 - centre_active)
    for coupling in couplings:
        diagonal = diagonal + coupling
    return (couplings, diagonal)

def apply_operator(field_wide, couplings, diagonal):
    result = diagonal * field_wide[1:-1, 1:-1, 1:-1]
    for coupling, neighbour in zip(couplings, NEIGHBOURS):
        result = result - coupling * field_wide[neighbour]
    return result

def local_solve(couplings, diagonal, residual_block):
    correction = jnp.zeros_like(residual_block)
    for sweep_step in range(SWEEPS):
        widened = jnp.pad(correction, 1)
        correction = correction + RELAXATION * (residual_block - apply_operator(widened, couplings, diagonal)) / diagonal
    return correction

def multiplicity(position, owner, owners, extent):
    lower_edge = jnp.logical_and(position < 2, owner > 0)
    upper_edge = jnp.logical_and(position >= extent - 2, owner < owners - 1)
    return 1.0 + lower_edge.astype(jnp.float32) + upper_edge.astype(jnp.float32)

def axis_count(total_cells, extent):
    cells = jnp.arange(total_cells, dtype=jnp.int32)
    return multiplicity(cells % extent, cells // extent, total_cells // extent, extent)

def reference(source, permeability, storage, column_depth):
    layers = jnp.arange(NZ, dtype=jnp.int32)
    active = (layers[:, None, None] < column_depth[None, :, :]).astype(jnp.float32)
    stacked = jnp.stack([permeability, active, storage, source])
    inner_couplings, inner_diagonal = prepare(jnp.pad(stacked, ((0, 0), (1, 1), (1, 1), (1, 1))))
    stacked_three = jnp.pad(stacked, ((0, 0), (3, 3), (3, 3), (3, 3)))
    covered = axis_count(NZ, CZ)[:, None, None] * axis_count(NX, CX)[None, :, None] * axis_count(NY, CY)[None, None, :]
    pressure = jnp.zeros_like(source)
    norm_terms = []
    for iteration in range(ITERS + 1):
        residual = active * (source - apply_operator(jnp.pad(pressure, 1), inner_couplings, inner_diagonal))
        norm_terms.append(jnp.sum(residual * residual))
        if iteration == ITERS:
            break
        residual_two = jnp.pad(residual, 2)

        def visit(visit_index, accumulated):
            visit_index = jnp.asarray(visit_index).astype(jnp.int32)
            slab_depth = visit_index // (N_GX * N_GY)
            slab_row = visit_index // N_GY % N_GX
            slab_column = visit_index % N_GY
            start_z = (slab_depth * CZ).astype(jnp.int32)
            start_x = (slab_row * CX).astype(jnp.int32)
            start_y = (slab_column * CY).astype(jnp.int32)
            widened = lax.dynamic_slice(stacked_three, (jnp.int32(0), start_z, start_x, start_y), (4, CZ + 6, CX + 6, CY + 6))
            block_couplings, block_diagonal = prepare(widened)
            residual_part = lax.dynamic_slice(residual_two, (start_z, start_x, start_y), (CZ + 4, CX + 4, CY + 4))
            correction = local_solve(block_couplings, block_diagonal, residual_part)
            current = lax.dynamic_slice(accumulated, (start_z, start_x, start_y), (CZ + 4, CX + 4, CY + 4))
            return lax.dynamic_update_slice(accumulated, current + correction, (start_z, start_x, start_y))
        accumulated = lax.fori_loop(0, N_GZ * N_GX * N_GY, visit, jnp.zeros((NZ + 4, NX + 4, NY + 4), jnp.float32))
        pressure = pressure + accumulated[2:-2, 2:-2, 2:-2] / covered
    squares = jnp.stack(norm_terms)
    history = jnp.sqrt(squares[1:] / squares[0])
    return (pressure, history)
```

```python
import functools

import jax
import jax.numpy as jnp
from jax import lax
from jax.experimental import pallas as pl
from jax.experimental.pallas import tpu as pltpu
from jax.sharding import PartitionSpec as P

MESH = pl.DeviceIdType.MESH
ITERS = 3
RELAX = 0.9

PLANES, ROWS, LANES, PAD = 14, 40, 128, 8
FLAT = PLANES * ROWS + 2 * PAD
SIDE = ROWS + 2 * PAD
DIRS = tuple(
    (sz, sx, sy)
    for sz in (-1, 0, 1)
    for sx in (-1, 0, 1)
    for sy in (-1, 0, 1)
    if (sz, sx, sy) != (0, 0, 0)
)
DIRS = tuple(sorted(DIRS, key=lambda s: -(abs(s[0]) + abs(s[1]) + abs(s[2]))))
MAIN_DIRS = tuple(s for s in DIRS if s[2] == 0)
SIDE_DIRS = tuple(s for s in DIRS if s[2] != 0)


def plane(z):
    return pl.ds(PAD + ROWS * z, ROWS)


def iota(axis, shape=(ROWS, LANES)):
    return lax.broadcasted_iota(jnp.int32, shape, axis)


def roll(x, shift):
    return pltpu.roll(x, shift % LANES, axis=x.ndim - 1)


def row_tile(sx):
    return {0: pl.ds(0, ROWS), 1: pl.ds(ROWS - 8, 8), -1: pl.ds(0, 8)}[sx]


def add_tiles(acc, first, last):
    return jnp.concatenate([acc[:8] + first, acc[8 : ROWS - 8], acc[ROWS - 8 :] + last], axis=0)


def kernel(
    sizes, src_hbm, perm_hbm, stor_hbm, depth_hbm, out_hbm, hist_ref,
    in_src, in_perm, in_stor, in_depth, out_buf,
    own, own_side, own_corner,
    rz_k, rz_s, rz_q, rx0, rzx0, ry0, rxy0, rzy0, rzxy0,
    send, send_side, rz, rx, rzx, ry, rxy,
    k_main, k_side, s_main, s_side,
    w_main, w_side, alpha, alpha_side, scale,
    r0_main, r0_side, r_main, r_side, a_main, a_side, b_main, b_side, p_main, p_side,
    part, part_in,
    load_sem, out_sem, send0, recv0, sends, recvs, ar_send, ar_recv,
):
    n_gx, n_gy, n_gz = sizes
    gx, gy, gz = lax.axis_index("gx"), lax.axis_index("gy"), lax.axis_index("gz")

    def device(s):
        return (
            lax.rem(gx + s[1] + n_gx, n_gx),
            lax.rem(gy + s[2] + n_gy, n_gy),
            lax.rem(gz + s[0] + n_gz, n_gz),
        )

    barrier = pltpu.get_barrier_semaphore()
    for s in DIRS:
        pl.semaphore_signal(barrier, inc=1, device_id=device(s), device_id_type=MESH)

    loads = [
        pltpu.make_async_copy(a, b, load_sem.at[i])
        for i, (a, b) in enumerate(
            ((depth_hbm, in_depth), (perm_hbm, in_perm), (stor_hbm, in_stor), (src_hbm, in_src))
        )
    ]
    for copy in loads:
        copy.start()

    zero_plane = jnp.zeros((ROWS, LANES), jnp.float32)
    own[...] = jnp.zeros(own.shape, jnp.float32)
    for ref in (k_main, s_main, r0_main, r_main, a_main, b_main, p_main):
        ref[0 : PAD + ROWS] = jnp.zeros((PAD + ROWS, LANES), jnp.float32)
        ref[FLAT - PAD - ROWS :] = jnp.zeros((PAD + ROWS, LANES), jnp.float32)
    for ref in (k_side, s_side, r0_side, r_side, a_side, b_side, p_side):
        ref[...] = jnp.zeros((SIDE, LANES), jnp.float32)

    lane = iota(1)
    row = iota(0)
    group = lane // 8
    j = lane % 8
    left = jnp.logical_and(j >= 4, j <= 6)
    right = jnp.logical_and(j >= 1, j <= 3)

    def gather_edges(acc, z, value):
        return jnp.where(group == z, roll(value, 8 * z + 4), acc)

    for copy in loads:
        copy.wait()

    depth = in_depth[...]
    edges = [zero_plane, zero_plane, zero_plane]
    for z in range(8):
        active = (gz * 8 + z) < depth
        for f, value in enumerate(
            (jnp.where(active, in_perm[z], 0.0), in_stor[z], in_src[z])
        ):
            own[f, z + 3, 4:36] = value
            edges[f] = gather_edges(edges[f], z + 3, own[f, z + 3])
    sides = []
    for f in range(3):
        to_right = jnp.where(left, roll(edges[f], 3), 0.0)
        to_left = jnp.where(right, roll(edges[f], -3), 0.0)
        own_side[0, f] = to_left
        own_side[1, f] = to_right
        sides.append((to_left, to_right))
    for d in range(2):
        for u, base in ((0, 24), (1, 64)):
            k, st, q = (sides[f][d] for f in range(3))
            moved_s, moved_q = roll(st, 24), roll(q, 48)
            in_k = jnp.logical_and(lane >= base, lane < base + 24)
            in_s = jnp.logical_and(lane >= base + 24, lane < base + 48)
            own_corner[u, d] = jnp.where(in_k, k, jnp.where(in_s, moved_s, moved_q))

    pl.semaphore_wait(barrier, len(DIRS))

    started = []
    exchange0 = []

    def post0(src, dst, s):
        i = len(exchange0)
        copy = pltpu.make_async_remote_copy(
            src_ref=src, dst_ref=dst, send_sem=send0.at[i], recv_sem=recv0.at[i],
            device_id=device(s), device_id_type=MESH,
        )
        copy.start()
        exchange0.append(copy)
        started.append(copy)

    side_of = lambda v: (v + 1) // 2
    for s in DIRS:
        sz, sx, sy = s
        u, v, d = side_of(sz), side_of(sx), side_of(sy)
        if sy == 0:
            if sz == 0:
                post0(own.at[:, pl.ds(3, 8), row_tile(sx)], rx0.at[v], s)
            elif sx == 0:
                post0(own.at[0, pl.ds(8 if sz > 0 else 3, 3)], rz_k.at[u], s)
                post0(own.at[1, pl.ds(9 if sz > 0 else 3, 2)], rz_s.at[u], s)
                post0(own.at[2, pl.ds(9 if sz > 0 else 3, 2)], rz_q.at[u], s)
            else:
                post0(own.at[:, pl.ds(8 if sz > 0 else 3, 3), row_tile(sx)], rzx0.at[u, v], s)
        elif sz == 0:
            if sx == 0:
                post0(own_side.at[d], ry0.at[d], s)
            else:
                post0(own_side.at[d, :, row_tile(sx)], rxy0.at[v, d], s)
        elif sx == 0:
            post0(own_corner.at[u, d], rzy0.at[u, d], s)
        else:
            post0(own_corner.at[u, d, row_tile(sx)], rzxy0.at[u, v, d], s)
    for copy in exchange0:
        copy.wait_recv()

    x = row - 4
    row_in = jnp.logical_and(
        jnp.logical_or(x >= 0, gx > 0), jnp.logical_or(x < 32, gx < n_gx - 1)
    )
    side_in = jnp.logical_or(
        jnp.logical_and(left, gy > 0), jnp.logical_and(right, gy < n_gy - 1)
    )
    group_in = jnp.logical_and(
        jnp.logical_or(group >= 3, gz > 0), jnp.logical_or(group < 11, gz < n_gz - 1)
    )
    side_in = jnp.logical_and(jnp.logical_and(side_in, group_in), row_in)

    def plane_in(z):
        if z < 3:
            return (gz > 0).astype(jnp.float32)
        if z > 10:
            return (gz < n_gz - 1).astype(jnp.float32)
        return jnp.float32(1.0)

    def first_main(f, z, rz_f, low):
        if 3 <= z <= 10:
            value = own[f, z]
            return add_tiles(value, rx0[1, f, z - 3], rx0[0, f, z - 3])
        if z < 3:
            value = rz_f[1, z - low] if z >= low else zero_plane
            return add_tiles(value, rzx0[1, 1, f, z], rzx0[1, 0, f, z])
        value = rz_f[0, z - 11] if z - 11 < 3 - low else zero_plane
        return add_tiles(value, rzx0[0, 1, f, z - 11], rzx0[0, 0, f, z - 11])

    def first_side(f):
        total = []
        for d in range(2):
            shift = 64 - 24 * f

            def corner(lower, upper):
                g = lax.broadcasted_iota(jnp.int32, lower.shape, 1) // 8
                return jnp.where(
                    g <= 2, roll(lower, shift),
                    jnp.where(jnp.logical_and(g >= 11, g <= 13), roll(upper, shift), 0.0),
                )

            value = ry0[d, f] + corner(rzy0[1, d], rzy0[0, d])
            first, last = (
                rxy0[v, d, f] + corner(rzxy0[1, v, d], rzxy0[0, v, d]) for v in (1, 0)
            )
            total.append(add_tiles(value, first, last))
        return jnp.where(left, total[1], 0.0) + jnp.where(right, total[0], 0.0)

    row_gain = row_in.astype(jnp.float32)
    k_edges = zero_plane
    for z in range(PLANES):
        value = first_main(0, z, rz_k, 0) * (row_gain * plane_in(z))
        k_main[plane(z)] = value
        k_edges = gather_edges(k_edges, z, value)
    k_side[pl.ds(PAD, ROWS)] = jnp.where(side_in, first_side(0), 0.0)

    def to_main(side):
        return jnp.where(j == 4, roll(side, -2), roll(side, 2))

    def main_neighbours(ref, z, centre, cross):
        base = PAD + ROWS * z
        moved = roll(cross, -(8 * z + 4))
        return (
            ref[pl.ds(base - ROWS, ROWS)],
            ref[pl.ds(base + ROWS, ROWS)],
            ref[pl.ds(base - 1, ROWS)],
            ref[pl.ds(base + 1, ROWS)],
            jnp.where(lane == 0, moved, roll(centre, 1)),
            jnp.where(lane == LANES - 1, moved, roll(centre, -1)),
        )

    def side_neighbours(ref, centre, edges):
        return (
            roll(centre, 8),
            roll(centre, -8),
            ref[pl.ds(PAD - 1, ROWS)],
            ref[pl.ds(PAD + 1, ROWS)],
            jnp.where(j == 1, roll(edges, -2), roll(centre, 1)),
            jnp.where(j == 6, roll(edges, 2), roll(centre, -1)),
        )

    def weights(centre, others, storage, source, keep):
        idle = jnp.where(centre > 0.0, 0.0, 1.0)
        diagonal = storage + idle
        couplings = []
        for other in others:
            other_idle = jnp.where(other > 0.0, 0.0, 1.0)
            c = (2.0 * centre) * other / ((centre + idle) + (other + other_idle))
            couplings.append(c)
            diagonal = diagonal + c
        gain = jnp.where(keep, RELAX / diagonal, 0.0)
        live = jnp.where(keep, 1.0 - idle, 0.0)
        return [c * gain for c in couplings], live * gain * source, live * RELAX, diagonal

    rows_kept = jnp.logical_and(row >= 2, row < 38)
    rows_own = jnp.logical_and(row >= 4, row < 36)
    cross = to_main(k_side[pl.ds(PAD, ROWS)])
    edges = zero_plane
    total = zero_plane
    for z in range(1, 13):
        centre = k_main[plane(z)]
        ws, r, al, diagonal = weights(
            centre, main_neighbours(k_main, z, centre, cross),
            first_main(1, z, rz_s, 1), first_main(2, z, rz_q, 1), rows_kept,
        )
        for i in range(6):
            w_main[i, z - 1] = ws[i]
        alpha[z - 1] = al
        r0_main[plane(z)] = r
        edges = gather_edges(edges, z, r)
        if 3 <= z <= 10:
            sc = jnp.where(rows_own, diagonal * (1.0 / RELAX), 0.0)
            scale[z - 3] = sc
            total = total + (r * sc) * (r * sc)
    side_kept = jnp.logical_and(
        jnp.logical_and(rows_kept, jnp.logical_and(group >= 1, group <= 12)),
        jnp.logical_or(jnp.logical_or(j == 1, j == 2), jnp.logical_or(j == 5, j == 6)),
    )
    centre = k_side[pl.ds(PAD, ROWS)]
    ws, r, al, _ = weights(
        centre, side_neighbours(k_side, centre, k_edges), first_side(1), first_side(2), side_kept
    )
    for i in range(6):
        w_side[i] = ws[i]
    alpha_side[...] = al
    r0_side[pl.ds(PAD, ROWS)] = r

    def half(flag):
        return jnp.where(flag, 0.5, 1.0)

    def axis_gain(position, extent, owner, owners):
        inner_low = jnp.logical_and(jnp.logical_and(position >= 0, position < 2), owner > 0)
        inner_high = jnp.logical_and(
            jnp.logical_and(position >= extent - 2, position < extent), owner < owners - 1
        )
        outer = jnp.logical_or(
            jnp.logical_and(position >= -2, position < 0),
            jnp.logical_and(position >= extent, position < extent + 2),
        )
        return half(jnp.logical_or(outer, jnp.logical_or(inner_low, inner_high)))

    x_gain = axis_gain(x, 32, gx, n_gx)
    main_gain = x_gain * axis_gain(lane, 128, gy, n_gy)
    side_gain = (
        x_gain * axis_gain(group - 3, 8, gz, n_gz)
        * half(jnp.logical_or(jnp.logical_or(j == 1, j == 2), jnp.logical_or(j == 5, j == 6)))
    )

    def z_gain(z):
        if z in (0, 13):
            return 1.0
        if z in (1, 2, 11, 12):
            return 0.5
        if z in (3, 4):
            return jnp.where(gz > 0, 0.5, 1.0)
        if z in (9, 10):
            return jnp.where(gz < n_gz - 1, 0.5, 1.0)
        return 1.0

    def sweep(src, src_side, edges, rhs, rhs_side, write_main, write_side):
        side = src_side[pl.ds(PAD, ROWS)]
        value = (1.0 - RELAX) * side + rhs_side[pl.ds(PAD, ROWS)]
        for i, other in enumerate(side_neighbours(src_side, side, edges)):
            value = value + w_side[i] * other
        write_side(value)
        cross = to_main(side)
        new_edges = zero_plane
        for z in range(1, 13):
            centre = src[plane(z)]
            value = (1.0 - RELAX) * centre + rhs[plane(z)]
            for i, other in enumerate(main_neighbours(src, z, centre, cross)):
                value = value + w_main[i, z - 1] * other
            write_main(z, value)
            new_edges = gather_edges(new_edges, z, value)
        return new_edges

    def into(ref):
        def write(z, value):
            ref[plane(z)] = value
        return write

    def into_side(ref):
        def write(value):
            ref[pl.ds(PAD, ROWS)] = value
        return write

    partials = [total]
    for k in range(ITERS):
        rhs, rhs_side = (r0_main, r0_side) if k == 0 else (r_main, r_side)
        edges = sweep(rhs, rhs_side, edges, rhs, rhs_side, into(a_main), into_side(a_side))
        edges = sweep(a_main, a_side, edges, rhs, rhs_side, into(b_main), into_side(b_side))

        def last_main(z, value):
            send[k, z] = value

        def last_side(value):
            send[k, 0] = value
            send[k, 13] = value

        edges = sweep(b_main, b_side, edges, rhs, rhs_side, last_main, last_side)
        side = send[k, 0]
        send_side[k, 1] = jnp.where(
            left, roll(edges, 3), jnp.where(jnp.logical_or(j == 1, j == 2), side, 0.0)
        )
        send_side[k, 0] = jnp.where(
            right, roll(edges, -3), jnp.where(jnp.logical_or(j == 5, j == 6), side, 0.0)
        )

        copies = []
        for i, s in enumerate(DIRS):
            sz, sx, sy = s
            u, v, d = side_of(sz), side_of(sx), side_of(sy)
            if sy == 0:
                planes = {0: pl.ds(0, 13), 1: pl.ds(8, 6), -1: pl.ds(0, 6)}[sz]
                source = send.at[k, planes, row_tile(sx)]
                if sz == 0:
                    target = rx.at[k, v]
                elif sx == 0:
                    target = rz.at[k, u]
                else:
                    target = rzx.at[k, u, v]
            else:
                source = send_side.at[k, d, row_tile(sx)]
                target = ry.at[k, sz + 1, d] if sx == 0 else rxy.at[k, sz + 1, v, d]
            copy = pltpu.make_async_remote_copy(
                src_ref=source, dst_ref=target, send_sem=sends.at[k, i], recv_sem=recvs.at[k, i],
                device_id=device(s), device_id_type=MESH,
            )
            copy.start()
            copies.append(copy)
            started.append(copy)
        for copy in copies:
            copy.wait_recv()

        def across(lower, upper):
            at = lax.broadcasted_iota(jnp.int32, lower.shape, 1)
            return roll(jnp.where(at >= 64, lower, jnp.where(at < 48, upper, 0.0)), 64)

        side_sum = add_tiles(
            side + across(rz[k, 1, 5], rz[k, 0, 0]),
            rx[k, 1, 0] + across(rzx[k, 1, 1, 5], rzx[k, 0, 1, 0]),
            rx[k, 0, 0] + across(rzx[k, 1, 0, 5], rzx[k, 0, 0, 0]),
        )
        beside = [
            add_tiles(
                ry[k, 1, d] + across(ry[k, 2, d], ry[k, 0, d]),
                rxy[k, 1, 1, d] + across(rxy[k, 2, 1, d], rxy[k, 0, 1, d]),
                rxy[k, 1, 0, d] + across(rxy[k, 2, 0, d], rxy[k, 0, 0, d]),
            )
            for d in range(2)
        ]
        side_sum = side_sum + jnp.where(left, beside[1], 0.0) + jnp.where(right, beside[0], 0.0)
        inward = jnp.where(
            jnp.logical_or(j == 4, j == 5), roll(beside[1], 3), roll(beside[0], -3)
        )
        outermost = jnp.logical_or(lane < 2, lane >= LANES - 2)
        new_side = p_side[pl.ds(PAD, ROWS)] + side_sum * side_gain
        p_side[pl.ds(PAD, ROWS)] = new_side
        p_edges = zero_plane
        for z in range(PLANES):
            value = send[k, z] if 1 <= z <= 12 else zero_plane
            first = rx[k, 1, z] if 1 <= z <= 12 else jnp.zeros((8, LANES), jnp.float32)
            last = rx[k, 0, z] if 1 <= z <= 12 else jnp.zeros((8, LANES), jnp.float32)
            if z <= 4:
                value = value + rz[k, 1, z]
                first = first + rzx[k, 1, 1, z]
                last = last + rzx[k, 1, 0, z]
            if z >= 9:
                value = value + rz[k, 0, z - 8]
                first = first + rzx[k, 0, 1, z - 8]
                last = last + rzx[k, 0, 0, z - 8]
            value = add_tiles(value, first, last)
            value = value + jnp.where(outermost, roll(inward, -(8 * z + 4)), 0.0)
            value = value * (main_gain * z_gain(z))
            if k > 0:
                value = p_main[plane(z)] + value
            p_main[plane(z)] = value
            p_edges = gather_edges(p_edges, z, value)

        cross = to_main(new_side)
        edges = zero_plane
        total = zero_plane
        last_one = k == ITERS - 1
        for z in range(3, 11) if last_one else range(1, 13):
            centre = p_main[plane(z)]
            value = r0_main[plane(z)] - alpha[z - 1] * centre
            for i, other in enumerate(main_neighbours(p_main, z, centre, cross)):
                value = value + w_main[i, z - 1] * other
            if not last_one:
                r_main[plane(z)] = value
                edges = gather_edges(edges, z, value)
            if 3 <= z <= 10:
                value = value * scale[z - 3]
                total = total + value * value
        if not last_one:
            value = r0_side[pl.ds(PAD, ROWS)] - alpha_side[...] * new_side
            for i, other in enumerate(side_neighbours(p_side, new_side, p_edges)):
                value = value + w_side[i] * other
            r_side[pl.ds(PAD, ROWS)] = value
        partials.append(total)

    for z in range(8):
        out_buf[z] = p_main[pl.ds(PAD + ROWS * (z + 3) + 4, 32)]
    out_copy = pltpu.make_async_copy(out_buf, out_hbm, out_sem)
    out_copy.start()

    row8 = iota(0, (8, LANES))
    mine = jnp.zeros((8, LANES), jnp.float32)
    for i, value in enumerate(partials):
        mine = jnp.where(row8 == i, jnp.sum(value, axis=0, keepdims=True), mine)
    pair = gy + 1 - 2 * lax.rem(gy, 2)
    rounds = (
        [
            (lax.rem(gx + i, n_gx), gy if h == 0 else pair, gz)
            for i in range(n_gx)
            for h in range(2)
            if (i, h) != (0, 0)
        ],
        [
            (gx, lax.rem(gy + 2 * i, n_gy), lax.rem(gz + h, n_gz))
            for i in range(n_gy // 2)
            for h in range(n_gz)
            if (i, h) != (0, 0)
        ],
    )
    for n, targets in enumerate(rounds):
        part[n] = mine
        copies = []
        for i, target in enumerate(targets):
            copy = pltpu.make_async_remote_copy(
                src_ref=part.at[n], dst_ref=part_in.at[n, i],
                send_sem=ar_send.at[n, i], recv_sem=ar_recv.at[n, i],
                device_id=target, device_id_type=MESH,
            )
            copy.start()
            copies.append(copy)
            started.append(copy)
        for copy in copies:
            copy.wait_recv()
        terms = [mine] + [part_in[n, i] for i in range(len(targets))]
        while len(terms) > 1:
            terms = [sum(terms[i : i + 2]) for i in range(0, len(terms), 2)]
        mine = terms[0]
    squares = jnp.sum(mine, axis=1, keepdims=True)
    ratio = jnp.sqrt(squares / squares[0:1])
    for i in range(ITERS):
        hist_ref[i] = jnp.sum(ratio[i + 1 : i + 2, :])
    out_copy.wait()
    for copy in started:
        copy.wait_send()


def solution(mesh):
    sizes = (mesh.shape["gx"], mesh.shape["gy"], mesh.shape["gz"])
    f32 = jnp.float32

    def vmem(*shape):
        return pltpu.VMEM(shape, f32)

    n_dirs = len(DIRS)
    n_first = n_dirs + 4
    scratch = [
        vmem(8, 32, LANES), vmem(8, 32, LANES), vmem(8, 32, LANES),
        pltpu.VMEM((32, LANES), jnp.int32), vmem(8, 32, LANES),
        vmem(3, PLANES, ROWS, LANES), vmem(2, 3, ROWS, LANES), vmem(2, 2, ROWS, LANES),
        vmem(2, 3, ROWS, LANES), vmem(2, 2, ROWS, LANES), vmem(2, 2, ROWS, LANES),
        vmem(2, 3, 8, 8, LANES), vmem(2, 2, 3, 3, 8, LANES),
        vmem(2, 3, ROWS, LANES), vmem(2, 2, 3, 8, LANES),
        vmem(2, 2, ROWS, LANES), vmem(2, 2, 2, 8, LANES),
        vmem(ITERS, PLANES, ROWS, LANES), vmem(ITERS, 2, ROWS, LANES),
        vmem(ITERS, 2, 6, ROWS, LANES), vmem(ITERS, 2, 13, 8, LANES),
        vmem(ITERS, 2, 2, 6, 8, LANES),
        vmem(ITERS, 3, 2, ROWS, LANES), vmem(ITERS, 3, 2, 2, 8, LANES),
        vmem(FLAT, LANES), vmem(SIDE, LANES), vmem(FLAT, LANES), vmem(SIDE, LANES),
        vmem(6, 12, ROWS, LANES), vmem(6, ROWS, LANES),
        vmem(12, ROWS, LANES), vmem(ROWS, LANES), vmem(8, ROWS, LANES),
    ]
    for _ in range(5):
        scratch += [vmem(FLAT, LANES), vmem(SIDE, LANES)]
    scratch += [
        vmem(2, 8, LANES), vmem(2, 15, 8, LANES),
        pltpu.SemaphoreType.DMA((4,)), pltpu.SemaphoreType.DMA,
        pltpu.SemaphoreType.DMA((n_first,)), pltpu.SemaphoreType.DMA((n_first,)),
        pltpu.SemaphoreType.DMA((ITERS, n_dirs)), pltpu.SemaphoreType.DMA((ITERS, n_dirs)),
        pltpu.SemaphoreType.DMA((2, 15)), pltpu.SemaphoreType.DMA((2, 15)),
    ]

    def per_device(source, permeability, storage, column_depth):
        return pl.pallas_call(
            functools.partial(kernel, sizes),
            out_shape=(
                jax.ShapeDtypeStruct(source.shape, f32),
                jax.ShapeDtypeStruct((ITERS,), f32),
            ),
            in_specs=[pl.BlockSpec(memory_space=pl.ANY)] * 4,
            out_specs=(
                pl.BlockSpec(memory_space=pl.ANY),
                pl.BlockSpec(memory_space=pltpu.SMEM),
            ),
            scratch_shapes=scratch,
            compiler_params=pltpu.CompilerParams(
                collective_id=0, has_side_effects=True, vmem_limit_bytes=40 * 2**20
            ),
            name="schwarz",
        )(source, permeability, storage, column_depth)

    placed = (P("gz", "gx", "gy"), P("gz", "gx", "gy"), P("gz", "gx", "gy"), P("gx", "gy"))
    return jax.shard_map(
        per_device,
        mesh=mesh,
        in_specs=placed,
        out_specs=(P("gz", "gx", "gy"), P()),
        check_vma=False,
    )
```

```python
import functools

import jax
import jax.numpy as jnp
from jax import lax
from jax.experimental import pallas as pl
from jax.experimental.pallas import tpu as pltpu
from jax.sharding import PartitionSpec as P

MESH = pl.DeviceIdType.MESH
ITERS = 3
RELAX = 0.9

PLANES, ROWS, LANES, PAD = 14, 40, 128, 8
FLAT = PLANES * ROWS + 2 * PAD
SIDE = ROWS + 2 * PAD
DIRS = tuple(
    (sz, sx, sy)
    for sz in (-1, 0, 1)
    for sx in (-1, 0, 1)
    for sy in (-1, 0, 1)
    if (sz, sx, sy) != (0, 0, 0)
)
DIRS = tuple(sorted(DIRS, key=lambda s: -(abs(s[0]) + abs(s[1]) + abs(s[2]))))
MAIN_DIRS = tuple(s for s in DIRS if s[2] == 0)
SIDE_DIRS = tuple(s for s in DIRS if s[2] != 0)


def plane(z):
    return pl.ds(PAD + ROWS * z, ROWS)


def iota(axis, shape=(ROWS, LANES)):
    return lax.broadcasted_iota(jnp.int32, shape, axis)


def roll(x, shift):
    return pltpu.roll(x, shift % LANES, axis=x.ndim - 1)


def row_tile(sx):
    return {0: pl.ds(0, ROWS), 1: pl.ds(ROWS - 8, 8), -1: pl.ds(0, 8)}[sx]


def add_tiles(acc, first, last):
    return jnp.concatenate([acc[:8] + first, acc[8 : ROWS - 8], acc[ROWS - 8 :] + last], axis=0)


def kernel(
    sizes, src_hbm, perm_hbm, stor_hbm, depth_hbm, out_hbm, hist_ref,
    in_src, in_perm, in_stor, in_depth, out_buf,
    own, own_side, own_corner,
    rz_k, rz_s, rz_q, rx0, rzx0, ry0, rxy0, rzy0, rzxy0,
    send, send_side, rz, rx, rzx, ry, rxy,
    k_main, k_side, s_main, s_side,
    w_main, w_side, alpha, alpha_side, scale,
    r0_main, r0_side, r_main, r_side, a_main, a_side, b_main, b_side, p_main, p_side,
    part, part_in,
    load_sem, out_sem, send0, recv0, sends, recvs, ar_send, ar_recv,
):
    n_gx, n_gy, n_gz = sizes
    gx, gy, gz = lax.axis_index("gx"), lax.axis_index("gy"), lax.axis_index("gz")

    def device(s):
        return (
            lax.rem(gx + s[1] + n_gx, n_gx),
            lax.rem(gy + s[2] + n_gy, n_gy),
            lax.rem(gz + s[0] + n_gz, n_gz),
        )

    barrier = pltpu.get_barrier_semaphore()
    for s in DIRS:
        pl.semaphore_signal(barrier, inc=1, device_id=device(s), device_id_type=MESH)

    loads = [
        pltpu.make_async_copy(a, b, load_sem.at[i])
        for i, (a, b) in enumerate(
            ((depth_hbm, in_depth), (perm_hbm, in_perm), (stor_hbm, in_stor), (src_hbm, in_src))
        )
    ]
    for copy in loads:
        copy.start()

    zero_plane = jnp.zeros((ROWS, LANES), jnp.float32)
    own[...] = jnp.zeros(own.shape, jnp.float32)
    for ref in (k_main, s_main, r0_main, r_main, a_main, b_main, p_main):
        ref[0 : PAD + ROWS] = jnp.zeros((PAD + ROWS, LANES), jnp.float32)
        ref[FLAT - PAD - ROWS :] = jnp.zeros((PAD + ROWS, LANES), jnp.float32)
    for ref in (k_side, s_side, r0_side, r_side, a_side, b_side, p_side):
        ref[...] = jnp.zeros((SIDE, LANES), jnp.float32)

    lane = iota(1)
    row = iota(0)
    group = lane // 8
    j = lane % 8
    left = jnp.logical_and(j >= 4, j <= 6)
    right = jnp.logical_and(j >= 1, j <= 3)

    def gather_edges(acc, z, value):
        return jnp.where(group == z, roll(value, 8 * z + 4), acc)

    for copy in loads:
        copy.wait()

    depth = in_depth[...]
    edges = [zero_plane, zero_plane, zero_plane]
    for z in range(8):
        active = (gz * 8 + z) < depth
        for f, value in enumerate(
            (jnp.where(active, in_perm[z], 0.0), in_stor[z], in_src[z])
        ):
            own[f, z + 3, 4:36] = value
            edges[f] = gather_edges(edges[f], z + 3, own[f, z + 3])
    sides = []
    for f in range(3):
        to_right = jnp.where(left, roll(edges[f], 3), 0.0)
        to_left = jnp.where(right, roll(edges[f], -3), 0.0)
        own_side[0, f] = to_left
        own_side[1, f] = to_right
        sides.append((to_left, to_right))
    for d in range(2):
        for u, base in ((0, 24), (1, 64)):
            k, st, q = (sides[f][d] for f in range(3))
            moved_s, moved_q = roll(st, 24), roll(q, 48)
            in_k = jnp.logical_and(lane >= base, lane < base + 24)
            in_s = jnp.logical_and(lane >= base + 24, lane < base + 48)
            own_corner[u, d] = jnp.where(in_k, k, jnp.where(in_s, moved_s, moved_q))

    pl.semaphore_wait(barrier, len(DIRS))

    started = []
    exchange0 = []

    def post0(src, dst, s):
        i = len(exchange0)
        copy = pltpu.make_async_remote_copy(
            src_ref=src, dst_ref=dst, send_sem=send0.at[i], recv_sem=recv0.at[i],
            device_id=device(s), device_id_type=MESH,
        )
        copy.start()
        exchange0.append(copy)
        started.append(copy)

    side_of = lambda v: (v + 1) // 2
    for s in DIRS:
        sz, sx, sy = s
        u, v, d = side_of(sz), side_of(sx), side_of(sy)
        if sy == 0:
            if sz == 0:
                post0(own.at[:, pl.ds(3, 8), row_tile(sx)], rx0.at[v], s)
            elif sx == 0:
                post0(own.at[0, pl.ds(8 if sz > 0 else 3, 3)], rz_k.at[u], s)
                post0(own.at[1, pl.ds(9 if sz > 0 else 3, 2)], rz_s.at[u], s)
                post0(own.at[2, pl.ds(9 if sz > 0 else 3, 2)], rz_q.at[u], s)
            else:
                post0(own.at[:, pl.ds(8 if sz > 0 else 3, 3), row_tile(sx)], rzx0.at[u, v], s)
        elif sz == 0:
            if sx == 0:
                post0(own_side.at[d], ry0.at[d], s)
            else:
                post0(own_side.at[d, :, row_tile(sx)], rxy0.at[v, d], s)
        elif sx == 0:
            post0(own_corner.at[u, d], rzy0.at[u, d], s)
        else:
            post0(own_corner.at[u, d, row_tile(sx)], rzxy0.at[u, v, d], s)
    for copy in exchange0:
        copy.wait_recv()

    x = row - 4
    row_in = jnp.logical_and(
        jnp.logical_or(x >= 0, gx > 0), jnp.logical_or(x < 32, gx < n_gx - 1)
    )
    side_in = jnp.logical_or(
        jnp.logical_and(left, gy > 0), jnp.logical_and(right, gy < n_gy - 1)
    )
    group_in = jnp.logical_and(
        jnp.logical_or(group >= 3, gz > 0), jnp.logical_or(group < 11, gz < n_gz - 1)
    )
    side_in = jnp.logical_and(jnp.logical_and(side_in, group_in), row_in)

    def plane_in(z):
        if z < 3:
            return (gz > 0).astype(jnp.float32)
        if z > 10:
            return (gz < n_gz - 1).astype(jnp.float32)
        return jnp.float32(1.0)

    def first_main(f, z, rz_f, low):
        if 3 <= z <= 10:
            value = own[f, z]
            return add_tiles(value, rx0[1, f, z - 3], rx0[0, f, z - 3])
        if z < 3:
            value = rz_f[1, z - low] if z >= low else zero_plane
            return add_tiles(value, rzx0[1, 1, f, z], rzx0[1, 0, f, z])
        value = rz_f[0, z - 11] if z - 11 < 3 - low else zero_plane
        return add_tiles(value, rzx0[0, 1, f, z - 11], rzx0[0, 0, f, z - 11])

    def first_side(f):
        total = []
        for d in range(2):
            shift = 64 - 24 * f

            def corner(lower, upper):
                g = lax.broadcasted_iota(jnp.int32, lower.shape, 1) // 8
                return jnp.where(
                    g <= 2, roll(lower, shift),
                    jnp.where(jnp.logical_and(g >= 11, g <= 13), roll(upper, shift), 0.0),
                )

            value = ry0[d, f] + corner(rzy0[1, d], rzy0[0, d])
            first, last = (
                rxy0[v, d, f] + corner(rzxy0[1, v, d], rzxy0[0, v, d]) for v in (1, 0)
            )
            total.append(add_tiles(value, first, last))
        return jnp.where(left, total[1], 0.0) + jnp.where(right, total[0], 0.0)

    row_gain = row_in.astype(jnp.float32)
    k_edges = zero_plane
    for z in range(PLANES):
        value = first_main(0, z, rz_k, 0) * (row_gain * plane_in(z))
        k_main[plane(z)] = value
        k_edges = gather_edges(k_edges, z, value)
    k_side[pl.ds(PAD, ROWS)] = jnp.where(side_in, first_side(0), 0.0)

    def to_main(side):
        return jnp.where(j == 4, roll(side, -2), roll(side, 2))

    def main_neighbours(ref, z, centre, cross):
        base = PAD + ROWS * z
        moved = roll(cross, -(8 * z + 4))
        return (
            ref[pl.ds(base - ROWS, ROWS)],
            ref[pl.ds(base + ROWS, ROWS)],
            ref[pl.ds(base - 1, ROWS)],
            ref[pl.ds(base + 1, ROWS)],
            jnp.where(lane == 0, moved, roll(centre, 1)),
            jnp.where(lane == LANES - 1, moved, roll(centre, -1)),
        )

    def side_neighbours(ref, centre, edges):
        return (
            roll(centre, 8),
            roll(centre, -8),
            ref[pl.ds(PAD - 1, ROWS)],
            ref[pl.ds(PAD + 1, ROWS)],
            jnp.where(j == 1, roll(edges, -2), roll(centre, 1)),
            jnp.where(j == 6, roll(edges, 2), roll(centre, -1)),
        )

    def weights(centre, others, storage, source, keep):
        idle = jnp.where(centre > 0.0, 0.0, 1.0)
        diagonal = storage + idle
        couplings = []
        for other in others:
            other_idle = jnp.where(other > 0.0, 0.0, 1.0)
            c = (2.0 * centre) * other / ((centre + idle) + (other + other_idle))
            couplings.append(c)
            diagonal = diagonal + c
        gain = jnp.where(keep, RELAX / diagonal, 0.0)
        live = jnp.where(keep, 1.0 - idle, 0.0)
        return [c * gain for c in couplings], live * gain * source, live * RELAX, diagonal

    rows_kept = jnp.logical_and(row >= 2, row < 38)
    rows_own = jnp.logical_and(row >= 4, row < 36)
    cross = to_main(k_side[pl.ds(PAD, ROWS)])
    edges = zero_plane
    total = zero_plane
    for z in range(1, 13):
        centre = k_main[plane(z)]
        ws, r, al, diagonal = weights(
            centre, main_neighbours(k_main, z, centre, cross),
            first_main(1, z, rz_s, 1), first_main(2, z, rz_q, 1), rows_kept,
        )
        for i in range(6):
            w_main[i, z - 1] = ws[i]
        alpha[z - 1] = al
        r0_main[plane(z)] = r
        edges = gather_edges(edges, z, r)
        if 3 <= z <= 10:
            sc = jnp.where(rows_own, diagonal * (1.0 / RELAX), 0.0)
            scale[z - 3] = sc
            total = total + (r * sc) * (r * sc)
    side_kept = jnp.logical_and(
        jnp.logical_and(rows_kept, jnp.logical_and(group >= 1, group <= 12)),
        jnp.logical_or(jnp.logical_or(j == 1, j == 2), jnp.logical_or(j == 5, j == 6)),
    )
    centre = k_side[pl.ds(PAD, ROWS)]
    ws, r, al, _ = weights(
        centre, side_neighbours(k_side, centre, k_edges), first_side(1), first_side(2), side_kept
    )
    for i in range(6):
        w_side[i] = ws[i]
    alpha_side[...] = al
    r0_side[pl.ds(PAD, ROWS)] = r

    def half(flag):
        return jnp.where(flag, 0.5, 1.0)

    def axis_gain(position, extent, owner, owners):
        inner_low = jnp.logical_and(jnp.logical_and(position >= 0, position < 2), owner > 0)
        inner_high = jnp.logical_and(
            jnp.logical_and(position >= extent - 2, position < extent), owner < owners - 1
        )
        outer = jnp.logical_or(
            jnp.logical_and(position >= -2, position < 0),
            jnp.logical_and(position >= extent, position < extent + 2),
        )
        return half(jnp.logical_or(outer, jnp.logical_or(inner_low, inner_high)))

    x_gain = axis_gain(x, 32, gx, n_gx)
    main_gain = x_gain * axis_gain(lane, 128, gy, n_gy)
    side_gain = (
        x_gain * axis_gain(group - 3, 8, gz, n_gz)
        * half(jnp.logical_or(jnp.logical_or(j == 1, j == 2), jnp.logical_or(j == 5, j == 6)))
    )

    def z_gain(z):
        if z in (0, 13):
            return 1.0
        if z in (1, 2, 11, 12):
            return 0.5
        if z in (3, 4):
            return jnp.where(gz > 0, 0.5, 1.0)
        if z in (9, 10):
            return jnp.where(gz < n_gz - 1, 0.5, 1.0)
        return 1.0

    def sweep(src, src_side, edges, rhs, rhs_side, write_main, write_side):
        side = src_side[pl.ds(PAD, ROWS)]
        value = (1.0 - RELAX) * side + rhs_side[pl.ds(PAD, ROWS)]
        for i, other in enumerate(side_neighbours(src_side, side, edges)):
            value = value + w_side[i] * other
        write_side(value)
        cross = to_main(side)
        new_edges = zero_plane
        for z in range(1, 13):
            centre = src[plane(z)]
            value = (1.0 - RELAX) * centre + rhs[plane(z)]
            for i, other in enumerate(main_neighbours(src, z, centre, cross)):
                value = value + w_main[i, z - 1] * other
            write_main(z, value)
            new_edges = gather_edges(new_edges, z, value)
        return new_edges

    def into(ref):
        def write(z, value):
            ref[plane(z)] = value
        return write

    def into_side(ref):
        def write(value):
            ref[pl.ds(PAD, ROWS)] = value
        return write

    partials = [total]
    for k in range(ITERS):
        rhs, rhs_side = (r0_main, r0_side) if k == 0 else (r_main, r_side)
        edges = sweep(rhs, rhs_side, edges, rhs, rhs_side, into(a_main), into_side(a_side))
        edges = sweep(a_main, a_side, edges, rhs, rhs_side, into(b_main), into_side(b_side))

        def last_main(z, value):
            send[k, z] = value

        def last_side(value):
            send[k, 0] = value
            send[k, 13] = value

        edges = sweep(b_main, b_side, edges, rhs, rhs_side, last_main, last_side)
        side = send[k, 0]
        send_side[k, 1] = jnp.where(
            left, roll(edges, 3), jnp.where(jnp.logical_or(j == 1, j == 2), side, 0.0)
        )
        send_side[k, 0] = jnp.where(
            right, roll(edges, -3), jnp.where(jnp.logical_or(j == 5, j == 6), side, 0.0)
        )

        copies = []
        for i, s in enumerate(DIRS):
            sz, sx, sy = s
            u, v, d = side_of(sz), side_of(sx), side_of(sy)
            if sy == 0:
                planes = {0: pl.ds(0, 13), 1: pl.ds(8, 6), -1: pl.ds(0, 6)}[sz]
                source = send.at[k, planes, row_tile(sx)]
                if sz == 0:
                    target = rx.at[k, v]
                elif sx == 0:
                    target = rz.at[k, u]
                else:
                    target = rzx.at[k, u, v]
            else:
                source = send_side.at[k, d, row_tile(sx)]
                target = ry.at[k, sz + 1, d] if sx == 0 else rxy.at[k, sz + 1, v, d]
            copy = pltpu.make_async_remote_copy(
                src_ref=source, dst_ref=target, send_sem=sends.at[k, i], recv_sem=recvs.at[k, i],
                device_id=device(s), device_id_type=MESH,
            )
            copy.start()
            copies.append(copy)
            started.append(copy)
        for copy in copies:
            copy.wait_recv()

        def across(lower, upper):
            at = lax.broadcasted_iota(jnp.int32, lower.shape, 1)
            return roll(jnp.where(at >= 64, lower, jnp.where(at < 48, upper, 0.0)), 64)

        side_sum = add_tiles(
            side + across(rz[k, 1, 5], rz[k, 0, 0]),
            rx[k, 1, 0] + across(rzx[k, 1, 1, 5], rzx[k, 0, 1, 0]),
            rx[k, 0, 0] + across(rzx[k, 1, 0, 5], rzx[k, 0, 0, 0]),
        )
        beside = [
            add_tiles(
                ry[k, 1, d] + across(ry[k, 2, d], ry[k, 0, d]),
                rxy[k, 1, 1, d] + across(rxy[k, 2, 1, d], rxy[k, 0, 1, d]),
                rxy[k, 1, 0, d] + across(rxy[k, 2, 0, d], rxy[k, 0, 0, d]),
            )
            for d in range(2)
        ]
        side_sum = side_sum + jnp.where(left, beside[1], 0.0) + jnp.where(right, beside[0], 0.0)
        inward = jnp.where(
            jnp.logical_or(j == 4, j == 5), roll(beside[1], 3), roll(beside[0], -3)
        )
        outermost = jnp.logical_or(lane < 2, lane >= LANES - 2)
        new_side = p_side[pl.ds(PAD, ROWS)] + side_sum * side_gain
        p_side[pl.ds(PAD, ROWS)] = new_side
        p_edges = zero_plane
        for z in range(PLANES):
            value = send[k, z] if 1 <= z <= 12 else zero_plane
            first = rx[k, 1, z] if 1 <= z <= 12 else jnp.zeros((8, LANES), jnp.float32)
            last = rx[k, 0, z] if 1 <= z <= 12 else jnp.zeros((8, LANES), jnp.float32)
            if z <= 4:
                value = value + rz[k, 1, z]
                first = first + rzx[k, 1, 1, z]
                last = last + rzx[k, 1, 0, z]
            if z >= 9:
                value = value + rz[k, 0, z - 8]
                first = first + rzx[k, 0, 1, z - 8]
                last = last + rzx[k, 0, 0, z - 8]
            value = add_tiles(value, first, last)
            value = value + jnp.where(outermost, roll(inward, -(8 * z + 4)), 0.0)
            value = value * (main_gain * z_gain(z))
            if k > 0:
                value = p_main[plane(z)] + value
            p_main[plane(z)] = value
            p_edges = gather_edges(p_edges, z, value)

        cross = to_main(new_side)
        edges = zero_plane
        total = zero_plane
        last_one = k == ITERS - 1
        for z in range(3, 11) if last_one else range(1, 13):
            centre = p_main[plane(z)]
            value = r0_main[plane(z)] - alpha[z - 1] * centre
            for i, other in enumerate(main_neighbours(p_main, z, centre, cross)):
                value = value + w_main[i, z - 1] * other
            if not last_one:
                r_main[plane(z)] = value
                edges = gather_edges(edges, z, value)
            if 3 <= z <= 10:
                value = value * scale[z - 3]
                total = total + value * value
        if not last_one:
            value = r0_side[pl.ds(PAD, ROWS)] - alpha_side[...] * new_side
            for i, other in enumerate(side_neighbours(p_side, new_side, p_edges)):
                value = value + w_side[i] * other
            r_side[pl.ds(PAD, ROWS)] = value
        partials.append(total)

    for z in range(8):
        out_buf[z] = p_main[pl.ds(PAD + ROWS * (z + 3) + 4, 32)]
    out_copy = pltpu.make_async_copy(out_buf, out_hbm, out_sem)
    out_copy.start()

    at = iota(1, (1, LANES)) // 32
    mine = jnp.zeros((1, LANES), jnp.float32)
    for i, value in enumerate(partials):
        value = jnp.sum(value, axis=0, keepdims=True)
        value = value + roll(value, 64)
        mine = jnp.where(at == i, value + roll(value, 32), mine)
    pair = gy + 1 - 2 * lax.rem(gy, 2)

    def ring(i, n):
        return min(i, n - i)

    rounds = (
        sorted(
            ((i, h) for i in range(n_gx) for h in range(2) if (i, h) != (0, 0)),
            key=lambda t: -ring(t[0], n_gx) - 0.3 * t[1],
        ),
        sorted(
            ((i, h) for i in range(n_gy // 2) for h in range(n_gz) if (i, h) != (0, 0)),
            key=lambda t: -ring(t[0], n_gy // 2) - ring(t[1], n_gz),
        ),
    )
    rounds = (
        [(lax.rem(gx + i, n_gx), gy if h == 0 else pair, gz) for i, h in rounds[0]],
        [(gx, lax.rem(gy + 2 * i, n_gy), lax.rem(gz + h, n_gz)) for i, h in rounds[1]],
    )
    slots = (gx * 2 + lax.rem(gy, 2), (gy // 2) * n_gz + gz)
    for n, targets in enumerate(rounds):
        here = part_in.at[n, slots[n], pl.ds(0, 1)]
        part[n, 0:1] = mine
        copies = []
        for i, target in enumerate(targets):
            copy = pltpu.make_async_remote_copy(
                src_ref=part.at[n, pl.ds(0, 1)], dst_ref=here,
                send_sem=ar_send.at[n, i], recv_sem=ar_recv.at[n, i],
                device_id=target, device_id_type=MESH,
            )
            copy.start()
            copies.append(copy)
            started.append(copy)
        here[...] = mine
        for copy in copies:
            copy.wait_recv()
        terms = [part_in[n, i, 0:1] for i in range(len(targets) + 1)]
        while len(terms) > 1:
            terms = [sum(terms[i + 1 : i + 2], terms[i]) for i in range(0, len(terms), 2)]
        mine = terms[0]
    squares = [
        jnp.sum(jnp.where(at == i, mine, 0.0), axis=1, keepdims=True) for i in range(ITERS + 1)
    ]
    for i in range(ITERS):
        hist_ref[i] = jnp.sum(jnp.sqrt(squares[i + 1] / squares[0]))
    out_copy.wait()
    for copy in started:
        copy.wait_send()


def solution(mesh):
    sizes = (mesh.shape["gx"], mesh.shape["gy"], mesh.shape["gz"])
    f32 = jnp.float32

    def vmem(*shape):
        return pltpu.VMEM(shape, f32)

    n_dirs = len(DIRS)
    n_first = n_dirs + 4
    scratch = [
        vmem(8, 32, LANES), vmem(8, 32, LANES), vmem(8, 32, LANES),
        pltpu.VMEM((32, LANES), jnp.int32), vmem(8, 32, LANES),
        vmem(3, PLANES, ROWS, LANES), vmem(2, 3, ROWS, LANES), vmem(2, 2, ROWS, LANES),
        vmem(2, 3, ROWS, LANES), vmem(2, 2, ROWS, LANES), vmem(2, 2, ROWS, LANES),
        vmem(2, 3, 8, 8, LANES), vmem(2, 2, 3, 3, 8, LANES),
        vmem(2, 3, ROWS, LANES), vmem(2, 2, 3, 8, LANES),
        vmem(2, 2, ROWS, LANES), vmem(2, 2, 2, 8, LANES),
        vmem(ITERS, PLANES, ROWS, LANES), vmem(ITERS, 2, ROWS, LANES),
        vmem(ITERS, 2, 6, ROWS, LANES), vmem(ITERS, 2, 13, 8, LANES),
        vmem(ITERS, 2, 2, 6, 8, LANES),
        vmem(ITERS, 3, 2, ROWS, LANES), vmem(ITERS, 3, 2, 2, 8, LANES),
        vmem(FLAT, LANES), vmem(SIDE, LANES), vmem(FLAT, LANES), vmem(SIDE, LANES),
        vmem(6, 12, ROWS, LANES), vmem(6, ROWS, LANES),
        vmem(12, ROWS, LANES), vmem(ROWS, LANES), vmem(8, ROWS, LANES),
    ]
    for _ in range(5):
        scratch += [vmem(FLAT, LANES), vmem(SIDE, LANES)]
    scratch += [
        vmem(2, 8, LANES), vmem(2, 16, 8, LANES),
        pltpu.SemaphoreType.DMA((4,)), pltpu.SemaphoreType.DMA,
        pltpu.SemaphoreType.DMA((n_first,)), pltpu.SemaphoreType.DMA((n_first,)),
        pltpu.SemaphoreType.DMA((ITERS, n_dirs)), pltpu.SemaphoreType.DMA((ITERS, n_dirs)),
        pltpu.SemaphoreType.DMA((2, 15)), pltpu.SemaphoreType.DMA((2, 15)),
    ]

    def per_device(source, permeability, storage, column_depth):
        return pl.pallas_call(
            functools.partial(kernel, sizes),
            out_shape=(
                jax.ShapeDtypeStruct(source.shape, f32),
                jax.ShapeDtypeStruct((ITERS,), f32),
            ),
            in_specs=[pl.BlockSpec(memory_space=pl.ANY)] * 4,
            out_specs=(
                pl.BlockSpec(memory_space=pl.ANY),
                pl.BlockSpec(memory_space=pltpu.SMEM),
            ),
            scratch_shapes=scratch,
            compiler_params=pltpu.CompilerParams(
                collective_id=0, has_side_effects=True, vmem_limit_bytes=60 * 2**20
            ),
            name="schwarz",
        )(source, permeability, storage, column_depth)

    placed = (P("gz", "gx", "gy"), P("gz", "gx", "gy"), P("gz", "gx", "gy"), P("gx", "gy"))
    return jax.shard_map(
        per_device,
        mesh=mesh,
        in_specs=placed,
        out_specs=(P("gz", "gx", "gy"), P()),
        check_vma=False,
    )
```

```python
import functools

import jax
import jax.numpy as jnp
from jax import lax
from jax.experimental import pallas as pl
from jax.experimental.pallas import tpu as pltpu
from jax.sharding import PartitionSpec as P

MESH = pl.DeviceIdType.MESH
ITERS = 3
RELAX = 0.9

PLANES, ROWS, LANES, PAD, STEP = 14, 40, 128, 8, 9
FLAT = PLANES * ROWS + 2 * PAD
SIDE = ROWS + 2 * PAD
DIRS = tuple(
    (sz, sx, sy)
    for sz in (-1, 0, 1)
    for sx in (-1, 0, 1)
    for sy in (-1, 0, 1)
    if (sz, sx, sy) != (0, 0, 0)
)
DIRS = tuple(sorted(DIRS, key=lambda s: -(abs(s[0]) + abs(s[1]) + abs(s[2]))))


def plane(z, count=1):
    return pl.ds(PAD + ROWS * z, ROWS * count)


MIDDLE = pl.ds(PAD, ROWS)


def iota(axis, shape=(ROWS, LANES)):
    return lax.broadcasted_iota(jnp.int32, shape, axis)


def roll(x, shift):
    return pltpu.roll(x, shift % LANES, axis=x.ndim - 1)


def both(*flags):
    return functools.reduce(jnp.logical_and, flags)


def either(*flags):
    return functools.reduce(jnp.logical_or, flags)


def between(x, low, high):
    return both(x >= low, x <= high)


def lanes_between(lane, low, high):
    if low < 0:
        return either(lane >= low + LANES, lane <= high)
    return between(lane, low, high)


def classes(shape, offset):
    u = lax.rem(iota(1, shape) + offset, LANES)
    z = (u * 57) >> 9
    return z, u - STEP * z


def row_tile(sx):
    return {0: pl.ds(0, ROWS), 1: pl.ds(ROWS - 8, 8), -1: pl.ds(0, 8)}[sx]


def add_tiles(acc, first, last):
    return jnp.concatenate([acc[:8] + first, acc[8 : ROWS - 8], acc[ROWS - 8 :] + last], axis=0)


def part_of(v):
    return (v + 1) // 2


def kernel(
    sizes, src_hbm, perm_hbm, stor_hbm, depth_hbm, out_hbm, hist_ref,
    in_src, in_perm, in_stor, in_depth, out_buf,
    own_rows, own_side, rz_k, rz_s, rz_q, rx0, rzx0, ry0, rxy0,
    send, rz, rx, rzx, ry, rxy,
    k_main, k_a, k_b, s_main, q_main,
    w_main, w_a, w_b, alpha, alpha_a, alpha_b, scale,
    r0_main, r0_a, r0_b, r_main, r_a, r_b, u_main, u_a, u_b, v_main, v_a, v_b, p_main, p_a, p_b,
    shifter, part, part_in,
    load_sem, out_sem, send0, recv0, sends, recvs, ar_send, ar_recv,
):
    n_gx, n_gy, n_gz = sizes
    gx, gy, gz = lax.axis_index("gx"), lax.axis_index("gy"), lax.axis_index("gz")

    def device(s):
        return (
            lax.rem(gx + s[1] + n_gx, n_gx),
            lax.rem(gy + s[2] + n_gy, n_gy),
            lax.rem(gz + s[0] + n_gz, n_gz),
        )

    barrier = pltpu.get_barrier_semaphore()
    for s in DIRS:
        pl.semaphore_signal(barrier, inc=1, device_id=device(s), device_id_type=MESH)

    loads = [
        pltpu.make_async_copy(a, b, load_sem.at[i])
        for i, (a, b) in enumerate(
            ((depth_hbm, in_depth), (perm_hbm, in_perm), (stor_hbm, in_stor), (src_hbm, in_src))
        )
    ]
    for copy in loads:
        copy.start()

    zero_plane = jnp.zeros((ROWS, LANES), jnp.float32)
    own_rows[...] = jnp.zeros(own_rows.shape, jnp.float32)
    own_side[...] = jnp.zeros(own_side.shape, jnp.float32)
    for ref in (k_main, s_main, q_main):
        ref[...] = jnp.zeros((FLAT, LANES), jnp.float32)
    for ref in (r0_main, r_main, u_main, v_main, p_main):
        ref[0 : PAD + ROWS] = jnp.zeros((PAD + ROWS, LANES), jnp.float32)
        ref[FLAT - PAD - ROWS :] = jnp.zeros((PAD + ROWS, LANES), jnp.float32)
    for ref in (k_a, k_b, r0_a, r0_b, r_a, r_b, u_a, u_b, v_a, v_b, p_a, p_b):
        ref[...] = jnp.zeros((SIDE, LANES), jnp.float32)

    at_in, at_out = iota(0, (2 * LANES, 2 * LANES)), iota(1, (2 * LANES, 2 * LANES))
    from_lane = lax.rem(at_out + jnp.where(at_out < LANES, LANES - 1, 1), LANES)
    shifter[...] = jnp.where(lax.rem(at_in, LANES) == from_lane, 1.0, 0.0).astype(jnp.bfloat16)

    lane, row = iota(1), iota(0)
    x = row - 4
    z_fa, y_fa = classes((ROWS, LANES), 0)
    z_fb, y_fb = classes((ROWS, LANES), 5)
    z_pa, y_pa = classes((ROWS, LANES), 1)
    z_pb, y_pb = classes((ROWS, LANES), 4)
    y_fa, y_fb, y_pa, y_pb = y_fa - 2, y_fb - 7, y_pa - 3, y_pb - 6

    def gather(accs, z, value):
        at = iota(1, value.shape)
        moved = roll(value, STEP * z + 2)
        return (
            jnp.where(lanes_between(at, STEP * z + 2, STEP * z + 8), moved, accs[0]),
            jnp.where(lanes_between(at, STEP * z - 5, STEP * z + 1), moved, accs[1]),
        )

    for copy in loads:
        copy.wait()

    depth = in_depth[...]
    zero_block = jnp.zeros((32, LANES), jnp.float32)
    edges = [(zero_block, zero_block)] * 3
    for z in range(8):
        in_perm[z] = jnp.where((gz * 8 + z) < depth, in_perm[z], 0.0)
        for f, ref in enumerate((in_perm, in_stor, in_src)):
            edges[f] = gather(edges[f], z + 3, ref[z])
        for v, low in ((0, 0), (1, 29)):
            own_rows[v, z, 0:3] = in_perm[z, low : low + 3]
            for i, ref in ((3, in_stor), (5, in_src)):
                own_rows[v, z, i : i + 2] = ref[z, low + v : low + v + 2]
    _, c = classes((32, LANES), 4)
    own_side[0, 4:36] = jnp.where(
        c >= 6, edges[0][0], jnp.where(c >= 3, roll(edges[1][0], -3), roll(edges[2][0], -6))
    )
    _, c = classes((32, LANES), 1)
    own_side[1, 4:36] = jnp.where(
        c < 3, edges[0][1], jnp.where(c < 6, roll(edges[1][1], 3), roll(edges[2][1], 6))
    )

    pl.semaphore_wait(barrier, len(DIRS))

    started = []
    exchange0 = []

    def post0(src, dst, s):
        i = len(exchange0)
        copy = pltpu.make_async_remote_copy(
            src_ref=src, dst_ref=dst, send_sem=send0.at[i], recv_sem=recv0.at[i],
            device_id=device(s), device_id_type=MESH,
        )
        copy.start()
        exchange0.append(copy)
        started.append(copy)

    for s in DIRS:
        sz, sx, sy = s
        u, v, d = part_of(sz), part_of(sx), part_of(sy)
        if sy == 0:
            if sz == 0:
                post0(own_rows.at[v], rx0.at[v], s)
            elif sx == 0:
                post0(in_perm.at[pl.ds(5 if sz > 0 else 0, 3)], rz_k.at[u], s)
                post0(in_stor.at[pl.ds(6 if sz > 0 else 0, 2)], rz_s.at[u], s)
                post0(in_src.at[pl.ds(6 if sz > 0 else 0, 2)], rz_q.at[u], s)
            else:
                post0(own_rows.at[v, pl.ds(5 if sz > 0 else 0, 3)], rzx0.at[u, v], s)
        elif sx == 0:
            post0(own_side.at[d], ry0.at[sz + 1, d], s)
        else:
            post0(own_side.at[d, row_tile(sx)], rxy0.at[sz + 1, v, d], s)
    for copy in exchange0:
        copy.wait_recv()

    def inside(flag):
        return flag.astype(jnp.float32)

    below, above = inside(gz > 0), inside(gz < n_gz - 1)
    before, after = inside(gx > 0), inside(gx < n_gx - 1)
    in_z = {z: below if z < 3 else above for z in (0, 1, 2, 11, 12, 13)}
    for z in range(PLANES):
        base = PAD + ROWS * z
        if 3 <= z <= 10:
            middle = in_perm[z - 3]
            low, high = rx0[1, z - 3], rx0[0, z - 3]
            gain = 1.0
            s_main[base + 4 : base + 36] = in_stor[z - 3]
            q_main[base + 4 : base + 36] = in_src[z - 3]
        else:
            u, i = (1, z) if z < 3 else (0, z - 11)
            middle = rz_k[u, i] * in_z[z]
            low, high = rzx0[u, 1, i], rzx0[u, 0, i]
            gain = in_z[z]
            if 1 <= z <= 12:
                i = z - 1 if z < 3 else z - 11
                s_main[base + 4 : base + 36] = rz_s[u, i]
                q_main[base + 4 : base + 36] = rz_q[u, i]
        k_main[base + 4 : base + 36] = middle
        k_main[base + 1 : base + 4] = low[0:3] * (before * gain)
        k_main[base + 36 : base + 39] = high[0:3] * (after * gain)
        s_main[base + 2 : base + 4] = low[3:5]
        s_main[base + 36 : base + 38] = high[3:5]
        q_main[base + 2 : base + 4] = low[5:7]
        q_main[base + 36 : base + 38] = high[5:7]

    def z_sum(here, lower, upper, offset, shift=0):
        z, _ = classes(here.shape, offset)
        moved = jnp.where(
            z <= 4, roll(lower, -8 * STEP - shift),
            jnp.where(both(z >= 9, z <= 13), roll(upper, 8 * STEP + shift), 0.0),
        )
        return here + moved

    def beside(y_ref, xy_ref, d):
        offset = 1 if d else 4
        return add_tiles(
            z_sum(y_ref(1, d), y_ref(2, d), y_ref(0, d), offset),
            z_sum(xy_ref(1, 1, d), xy_ref(2, 1, d), xy_ref(0, 1, d), offset),
            z_sum(xy_ref(1, 0, d), xy_ref(2, 0, d), xy_ref(0, 0, d), offset),
        )

    from_left, from_right = (
        beside(lambda i, d: ry0[i, d], lambda i, v, d: rxy0[i, v, d], d) for d in (1, 0)
    )

    def grid_z(z):
        return both(either(z >= 3, gz > 0), either(z <= 10, gz < n_gz - 1))

    row_in = both(either(x >= 0, gx > 0), either(x < 32, gx < n_gx - 1))
    gain_a = jnp.where(both(row_in, grid_z(z_pa), gy > 0), 1.0, 0.0)
    gain_b = jnp.where(both(row_in, grid_z(z_pb), gy < n_gy - 1), 1.0, 0.0)
    k_edges, s_edges, q_edges = ((zero_plane, zero_plane) for _ in range(3))
    for z in range(PLANES):
        k_edges = gather(k_edges, z, k_main[plane(z)])
        if 1 <= z <= 12:
            s_edges = gather(s_edges, z, s_main[plane(z)])
            q_edges = gather(q_edges, z, q_main[plane(z)])
    k_left, k_right = from_left * gain_a, from_right * gain_b
    k_fa = jnp.where(both(y_pa >= -2, y_pa <= -1), k_left, k_edges[0])
    k_fb = jnp.where(both(y_pb >= 0, y_pb <= 1), k_right, k_edges[1])
    k_pa = jnp.where(y_pa == -3, k_left, k_fa)
    k_pb = jnp.where(y_pb == 2, k_right, k_fb)
    k_a[MIDDLE] = k_fa
    k_b[MIDDLE] = k_fb
    s_a = jnp.where(both(y_pa >= -2, y_pa <= -1), roll(from_left, -3), s_edges[0])
    q_a = jnp.where(both(y_pa >= -2, y_pa <= -1), roll(from_left, -6), q_edges[0])
    s_b = jnp.where(both(y_pb >= 0, y_pb <= 1), roll(from_right, 3), s_edges[1])
    q_b = jnp.where(both(y_pb >= 0, y_pb <= 1), roll(from_right, 6), q_edges[1])

    def weights(centre, others, storage, source, keep):
        idle = jnp.where(centre > 0.0, 0.0, 1.0)
        diagonal = storage + idle
        couplings = []
        for other in others:
            other_idle = jnp.where(other > 0.0, 0.0, 1.0)
            c = (2.0 * centre) * other / ((centre + idle) + (other + other_idle))
            couplings.append(c)
            diagonal = diagonal + c
        gain = jnp.where(keep, RELAX / diagonal, 0.0)
        live = jnp.where(keep, 1.0 - idle, 0.0)
        return [c * gain for c in couplings], live * gain * source, live * RELAX, diagonal

    def around(ref, z, count=1):
        base, rows = PAD + ROWS * z, ROWS * count
        return (
            ref[pl.ds(base - ROWS, rows)],
            ref[pl.ds(base + ROWS, rows)],
            ref[pl.ds(base - 1, rows)],
            ref[pl.ds(base + 1, rows)],
        )

    def side_around(ref, centre):
        return (
            roll(centre, STEP), roll(centre, -STEP), ref[pl.ds(PAD - 1, ROWS)], ref[pl.ds(PAD + 1, ROWS)],
        )

    rows_kept, rows_own = between(row, 2, 37), between(row, 4, 35)
    inner = both(lane > 0, lane < LANES - 1)
    total = zero_plane
    r_edges = (zero_plane, zero_plane)
    for z in range(1, 13):
        centre = k_main[plane(z)]
        ws, r, al, diagonal = weights(
            centre, around(k_main, z) + (roll(centre, 1), roll(centre, -1)),
            s_main[plane(z)], q_main[plane(z)], rows_kept,
        )
        for i in range(6):
            w_main[i, plane(z)] = ws[i]
        alpha[plane(z)] = al
        r0_main[plane(z)] = r
        r_edges = gather(r_edges, z, r)
        if 3 <= z <= 10:
            sc = jnp.where(both(rows_own, inner), diagonal * (1.0 / RELAX), 0.0)
            scale[z - 3] = sc
            total = total + (r * sc) * (r * sc)
    scale_side = []
    for ref, k_f, left, right, st, q, z, y, low, high, w_ref, al_ref, r_ref, edge, own in (
        (k_a, k_fa, k_pa, k_fa, s_a, q_a, z_fa, y_fa, -2, 5, w_a, alpha_a, r0_a, r_edges[0], 0),
        (k_b, k_fb, k_fb, k_pb, s_b, q_b, z_fb, y_fb, -6, 1, w_b, alpha_b, r0_b, r_edges[1], -1),
    ):
        keep = both(rows_kept, between(z, 1, 12), between(y, low, high))
        ws, r, al, diagonal = weights(
            k_f, side_around(ref, k_f) + (roll(left, 1), roll(right, -1)), st, q, keep
        )
        for i in range(6):
            w_ref[i] = ws[i]
        if low == -2:
            w_ref[6] = jnp.where(y == -2, 0.0, ws[4])
        else:
            w_ref[6] = jnp.where(y == 1, 0.0, ws[5])
        al_ref[...] = al
        r_ref[MIDDLE] = jnp.where(y <= 0 if low == -2 else y >= -1, r, edge)
        sc = jnp.where(
            both(rows_own, between(z, 3, 10), y == own), diagonal * (1.0 / RELAX), 0.0
        )
        scale_side.append(sc)
        total = total + (r * sc) * (r * sc)

    def half(flag):
        return jnp.where(flag, 0.5, 1.0)

    def axis_gain(position, extent, owner, owners):
        inner_low = both(position >= 0, position < 2, owner > 0)
        inner_high = both(position >= extent - 2, position < extent, owner < owners - 1)
        outer = either(
            both(position >= -2, position < 0), both(position >= extent, position < extent + 2)
        )
        return half(either(outer, inner_low, inner_high))

    x_gain = axis_gain(x, 32, gx, n_gx)
    main_gain = x_gain * axis_gain(lane, 128, gy, n_gy)
    side_gain = (
        x_gain * axis_gain(z_pa - 3, 8, gz, n_gz) * axis_gain(y_pa, 128, gy, n_gy),
        x_gain * axis_gain(z_pb - 3, 8, gz, n_gz) * axis_gain(y_pb + 128, 128, gy, n_gy),
    )

    def z_gain(z):
        if z in (0, 13):
            return 1.0
        if z in (1, 2, 11, 12):
            return 0.5
        if z in (3, 4):
            return jnp.where(gz > 0, 0.5, 1.0)
        if z in (9, 10):
            return jnp.where(gz < n_gz - 1, 0.5, 1.0)
        return 1.0

    def side_sweep(ref, rhs, w_ref, last):
        value = ref[MIDDLE]
        others = side_around(ref, value) + (roll(value, 1), roll(value, -1))
        value = (1.0 - RELAX) * value + rhs[MIDDLE]
        for i, other in enumerate(others):
            value = value + w_ref[6 if i == last else i] * other
        return value

    def main_sweep(ref, rhs, z):
        value = ref[plane(z, 2)]
        hi = value.astype(jnp.bfloat16)
        lo = (value - hi.astype(jnp.float32)).astype(jnp.bfloat16)
        beside_y = jnp.dot(
            jnp.concatenate([hi, lo], axis=1), shifter[...], preferred_element_type=jnp.float32
        )
        others = around(ref, z, 2) + (beside_y[:, :LANES], beside_y[:, LANES:])
        value = (1.0 - RELAX) * value + rhs[plane(z, 2)]
        for i, other in enumerate(others):
            value = value + w_main[i, plane(z, 2)] * other
        return value

    partials = [total]
    for k in range(ITERS):
        rhs, rhs_a, rhs_b = (r0_main, r0_a, r0_b) if k == 0 else (r_main, r_a, r_b)
        copies = []

        def post(source, target, s):
            i = DIRS.index(s)
            copy = pltpu.make_async_remote_copy(
                src_ref=source, dst_ref=target, send_sem=sends.at[k, i], recv_sem=recvs.at[k, i],
                device_id=device(s), device_id_type=MESH,
            )
            copy.start()
            copies.append(copy)
            started.append(copy)

        for before_ref, after_ref in (((rhs_a, rhs_b), (u_a, u_b)), ((u_a, u_b), (v_a, v_b))):
            after_ref[0][MIDDLE] = side_sweep(before_ref[0], rhs_a, w_a, 4)
            after_ref[1][MIDDLE] = side_sweep(before_ref[1], rhs_b, w_b, 5)
        side_a = side_sweep(v_a, rhs_a, w_a, 4)
        side_b = side_sweep(v_b, rhs_b, w_b, 5)
        far_b = roll(side_b, 64)
        send[k, 0] = jnp.where(lane < 60, side_a, far_b)
        send[k, 13] = jnp.where(lane < 60, far_b, side_a)
        send[k, 14] = side_a
        send[k, 15] = side_b
        for s in DIRS:
            sz, sx, sy = s
            v, d = part_of(sx), part_of(sy)
            if sy != 0:
                source = send.at[k, 15 if sy > 0 else 14, row_tile(sx)]
                post(source, ry.at[k, sz + 1, d] if sx == 0 else rxy.at[k, sz + 1, v, d], s)

        for z in range(1, 13, 2):
            u_main[plane(z, 2)] = main_sweep(rhs, rhs, z)
        for z in range(1, 13, 2):
            v_main[plane(z, 2)] = main_sweep(u_main, rhs, z)
        for z in (1, 3, 5, 11, 9, 7):
            value = main_sweep(v_main, rhs, z)
            send[k, z] = value[:ROWS]
            send[k, z + 1] = value[ROWS:]
            if z in (5, 7):
                sz = -1 if z == 5 else 1
                planes = pl.ds(0 if z == 5 else 8, 6)
                for sx in (-1, 1):
                    post(
                        send.at[k, planes, row_tile(sx)],
                        rzx.at[k, part_of(sz), part_of(sx)], (sz, sx, 0),
                    )
                post(send.at[k, planes], rz.at[k, part_of(sz)], (sz, 0, 0))
        for sx in (-1, 1):
            post(send.at[k, pl.ds(1, 15), row_tile(sx)], rx.at[k, part_of(sx)], (0, sx, 0))
        for copy in copies:
            copy.wait_recv()

        new_p = []
        for own, d, offset, shift, y, low, high, outer_low, outer_high, ref in (
            (14, 1, 1, 0, y_pa, -2, 3, -3, 1, p_a),
            (15, 0, 4, 64, y_pb, -4, 1, -2, 2, p_b),
        ):
            here = add_tiles(
                z_sum(send[k, own], rz[k, 1, 5], rz[k, 0, 0], offset, shift),
                z_sum(rx[k, 1, own - 1], rzx[k, 1, 1, 5], rzx[k, 0, 1, 0], offset, shift),
                z_sum(rx[k, 0, own - 1], rzx[k, 1, 0, 5], rzx[k, 0, 0, 0], offset, shift),
            )
            other = beside(lambda i, d: ry[k, i, d], lambda i, v, d: rxy[k, i, v, d], d)
            value = jnp.where(between(y, low, high), here, 0.0) + jnp.where(
                between(y, outer_low, outer_high), other, 0.0
            )
            value = value * side_gain[1 - d]
            if k > 0:
                value = ref[MIDDLE] + value
            ref[MIDDLE] = value
            new_p.append(value)
        edges = jnp.where(between(y_pa, 0, 3), new_p[0], new_p[1])
        edge_lane = either(lane < 4, lane >= LANES - 4)
        for z in range(PLANES):
            solved = 1 <= z <= 12
            value = send[k, z] if solved else zero_plane
            first = rx[k, 1, z - 1] if solved else jnp.zeros((8, LANES), jnp.float32)
            last = rx[k, 0, z - 1] if solved else jnp.zeros((8, LANES), jnp.float32)
            if z <= 4:
                value = value + rz[k, 1, z]
                first = first + rzx[k, 1, 1, z]
                last = last + rzx[k, 1, 0, z]
            if z >= 9:
                value = value + rz[k, 0, z - 8]
                first = first + rzx[k, 0, 1, z - 8]
                last = last + rzx[k, 0, 0, z - 8]
            value = add_tiles(value, first, last) * (main_gain * z_gain(z))
            if k > 0:
                value = p_main[plane(z)] + value
            p_main[plane(z)] = jnp.where(edge_lane, roll(edges, -(STEP * z + 2)), value)

        total = zero_plane
        r_edges = (zero_plane, zero_plane)
        last_one = k == ITERS - 1
        for z in range(3, 11) if last_one else range(1, 13):
            centre = p_main[plane(z)]
            value = r0_main[plane(z)] - alpha[plane(z)] * centre
            for i, other in enumerate(
                around(p_main, z) + (roll(centre, 1), roll(centre, -1))
            ):
                value = value + w_main[i, plane(z)] * other
            if not last_one:
                r_main[plane(z)] = value
                r_edges = gather(r_edges, z, value)
            if 3 <= z <= 10:
                value = value * scale[z - 3]
                total = total + value * value
        for i, (ref, r0, al, w_ref, r_ref, p) in enumerate(
            ((p_a, r0_a, alpha_a, w_a, r_a, new_p[0]), (p_b, r0_b, alpha_b, w_b, r_b, new_p[1]))
        ):
            value = r0[MIDDLE] - al[...] * p
            for n, other in enumerate(side_around(ref, p) + (roll(p, 1), roll(p, -1))):
                value = value + w_ref[n] * other
            if not last_one:
                r_ref[MIDDLE] = jnp.where(y_fa <= 0 if i == 0 else y_fb >= -1, value, r_edges[i])
            value = value * scale_side[i]
            total = total + value * value
        partials.append(total)

    for z in range(8):
        out_buf[z] = p_main[pl.ds(PAD + ROWS * (z + 3) + 4, 32)]
    out_copy = pltpu.make_async_copy(out_buf, out_hbm, out_sem)
    out_copy.start()

    at = iota(1, (1, LANES)) // 32
    mine = jnp.zeros((1, LANES), jnp.float32)
    for i, value in enumerate(partials):
        value = jnp.sum(value, axis=0, keepdims=True)
        value = value + roll(value, 64)
        mine = jnp.where(at == i, value + roll(value, 32), mine)
    pair = gy + 1 - 2 * lax.rem(gy, 2)

    def ring(i, n):
        return min(i, n - i)

    rounds = (
        sorted(
            ((i, h) for i in range(n_gx) for h in range(2) if (i, h) != (0, 0)),
            key=lambda t: -ring(t[0], n_gx) - 0.3 * t[1],
        ),
        sorted(
            ((i, h) for i in range(n_gy // 2) for h in range(n_gz) if (i, h) != (0, 0)),
            key=lambda t: -ring(t[0], n_gy // 2) - ring(t[1], n_gz),
        ),
    )
    rounds = (
        [(lax.rem(gx + i, n_gx), gy if h == 0 else pair, gz) for i, h in rounds[0]],
        [(gx, lax.rem(gy + 2 * i, n_gy), lax.rem(gz + h, n_gz)) for i, h in rounds[1]],
    )
    slots = (gx * 2 + lax.rem(gy, 2), (gy // 2) * n_gz + gz)
    for n, targets in enumerate(rounds):
        here = part_in.at[n, slots[n], pl.ds(0, 1)]
        part[n, 0:1] = mine
        copies = []
        for i, target in enumerate(targets):
            copy = pltpu.make_async_remote_copy(
                src_ref=part.at[n, pl.ds(0, 1)], dst_ref=here,
                send_sem=ar_send.at[n, i], recv_sem=ar_recv.at[n, i],
                device_id=target, device_id_type=MESH,
            )
            copy.start()
            copies.append(copy)
            started.append(copy)
        here[...] = mine
        for copy in copies:
            copy.wait_recv()
        terms = [part_in[n, i, 0:1] for i in range(len(targets) + 1)]
        while len(terms) > 1:
            terms = [sum(terms[i + 1 : i + 2], terms[i]) for i in range(0, len(terms), 2)]
        mine = terms[0]
    squares = [
        jnp.sum(jnp.where(at == i, mine, 0.0), axis=1, keepdims=True) for i in range(ITERS + 1)
    ]
    for i in range(ITERS):
        hist_ref[i] = jnp.sum(jnp.sqrt(squares[i + 1] / squares[0]))
    out_copy.wait()
    for copy in started:
        copy.wait_send()


def solution(mesh):
    sizes = (mesh.shape["gx"], mesh.shape["gy"], mesh.shape["gz"])
    f32 = jnp.float32

    def vmem(*shape):
        return pltpu.VMEM(shape, f32)

    n_dirs = len(DIRS)
    n_first = n_dirs + 4
    scratch = [
        vmem(8, 32, LANES), vmem(8, 32, LANES), vmem(8, 32, LANES),
        pltpu.VMEM((32, LANES), jnp.int32), vmem(8, 32, LANES),
        vmem(2, 8, 8, LANES), vmem(2, ROWS, LANES),
        vmem(2, 3, 32, LANES), vmem(2, 2, 32, LANES), vmem(2, 2, 32, LANES),
        vmem(2, 8, 8, LANES), vmem(2, 2, 3, 8, LANES),
        vmem(3, 2, ROWS, LANES), vmem(3, 2, 2, 8, LANES),
        vmem(ITERS, 16, ROWS, LANES),
        vmem(ITERS, 2, 6, ROWS, LANES), vmem(ITERS, 2, 15, 8, LANES),
        vmem(ITERS, 2, 2, 6, 8, LANES),
        vmem(ITERS, 3, 2, ROWS, LANES), vmem(ITERS, 3, 2, 2, 8, LANES),
        vmem(FLAT, LANES), vmem(SIDE, LANES), vmem(SIDE, LANES), vmem(FLAT, LANES), vmem(FLAT, LANES),
        vmem(6, FLAT, LANES), vmem(7, ROWS, LANES), vmem(7, ROWS, LANES),
        vmem(FLAT, LANES), vmem(ROWS, LANES), vmem(ROWS, LANES), vmem(8, ROWS, LANES),
    ]
    for _ in range(5):
        scratch += [vmem(FLAT, LANES), vmem(SIDE, LANES), vmem(SIDE, LANES)]
    scratch += [
        pltpu.VMEM((2 * LANES, 2 * LANES), jnp.bfloat16),
        vmem(2, 8, LANES), vmem(2, 16, 8, LANES),
        pltpu.SemaphoreType.DMA((4,)), pltpu.SemaphoreType.DMA,
        pltpu.SemaphoreType.DMA((n_first,)), pltpu.SemaphoreType.DMA((n_first,)),
        pltpu.SemaphoreType.DMA((ITERS, n_dirs)), pltpu.SemaphoreType.DMA((ITERS, n_dirs)),
        pltpu.SemaphoreType.DMA((2, 15)), pltpu.SemaphoreType.DMA((2, 15)),
    ]

    def per_device(source, permeability, storage, column_depth):
        return pl.pallas_call(
            functools.partial(kernel, sizes),
            out_shape=(
                jax.ShapeDtypeStruct(source.shape, f32),
                jax.ShapeDtypeStruct((ITERS,), f32),
            ),
            in_specs=[pl.BlockSpec(memory_space=pl.ANY)] * 4,
            out_specs=(
                pl.BlockSpec(memory_space=pl.ANY),
                pl.BlockSpec(memory_space=pltpu.SMEM),
            ),
            scratch_shapes=scratch,
            compiler_params=pltpu.CompilerParams(
                collective_id=0, has_side_effects=True, vmem_limit_bytes=60 * 2**20
            ),
            name="schwarz",
        )(source, permeability, storage, column_depth)

    placed = (P("gz", "gx", "gy"), P("gz", "gx", "gy"), P("gz", "gx", "gy"), P("gx", "gy"))
    return jax.shard_map(
        per_device,
        mesh=mesh,
        in_specs=placed,
        out_specs=(P("gz", "gx", "gy"), P()),
        check_vma=False,
    )
```

```python
import functools

import jax
import jax.numpy as jnp
from jax import lax
from jax.experimental import pallas as pl
from jax.experimental.pallas import tpu as pltpu
from jax.sharding import PartitionSpec as P

MESH = pl.DeviceIdType.MESH
ITERS = 3
RELAX = 0.9

PLANES, ROWS, LANES, PAD, STEP = 14, 40, 128, 8, 9
FLAT = PLANES * ROWS + 2 * PAD
SIDE = ROWS + 2 * PAD
DIRS = tuple(
    (sz, sx, sy)
    for sz in (-1, 0, 1)
    for sx in (-1, 0, 1)
    for sy in (-1, 0, 1)
    if (sz, sx, sy) != (0, 0, 0)
)
DIRS = tuple(sorted(DIRS, key=lambda s: -(abs(s[0]) + abs(s[1]) + abs(s[2]))))


def plane(z, count=1):
    return pl.ds(PAD + ROWS * z, ROWS * count)


MIDDLE = pl.ds(PAD, ROWS)


def iota(axis, shape=(ROWS, LANES)):
    return lax.broadcasted_iota(jnp.int32, shape, axis)


def roll(x, shift):
    return pltpu.roll(x, shift % LANES, axis=x.ndim - 1)


def both(*flags):
    return functools.reduce(jnp.logical_and, flags)


def either(*flags):
    return functools.reduce(jnp.logical_or, flags)


def between(x, low, high):
    return both(x >= low, x <= high)


def lanes_between(lane, low, high):
    if low < 0:
        return either(lane >= low + LANES, lane <= high)
    return between(lane, low, high)


def classes(shape, offset):
    u = lax.rem(iota(1, shape) + offset, LANES)
    z = (u * 57) >> 9
    return z, u - STEP * z


def row_tile(sx):
    return {0: pl.ds(0, ROWS), 1: pl.ds(ROWS - 8, 8), -1: pl.ds(0, 8)}[sx]


def add_tiles(acc, first, last):
    return jnp.concatenate([acc[:8] + first, acc[8 : ROWS - 8], acc[ROWS - 8 :] + last], axis=0)


WIDTH = 43


def fold(side, first):
    t = [side[8 * i : 8 * i + 8] for i in range(5)]
    at = lax.rem(iota(1, (8, LANES)) + (LANES - first), LANES)
    one = jnp.where(
        at < WIDTH, t[0], jnp.where(at < 2 * WIDTH, roll(t[1], WIDTH), roll(t[2], 2 * WIDTH))
    )
    two = jnp.where(at < WIDTH, t[3], roll(t[4], WIDTH))
    return jnp.concatenate([one, two], axis=0)


def unfold(both_tiles, shift):
    return jnp.concatenate(
        [roll(both_tiles[8 * (i // 3) : 8 * (i // 3) + 8], shift - WIDTH * (i % 3)) for i in range(5)],
        axis=0,
    )


def part_of(v):
    return (v + 1) // 2


def kernel(
    sizes, src_hbm, perm_hbm, stor_hbm, depth_hbm, out_ref, hist_ref,
    in_src, in_perm, in_stor, in_depth,
    own_rows, own_side, own_fold, rz_k, rz_s, rz_q, rx0, rzx0, ry0, rzy0, rxy0,
    send, zx_out, fold_out, rz, rx, rzx, ry, rzy, rxy,
    k_main, k_a, k_b, s_main, q_main,
    w_main, w_a, w_b, alpha, alpha_a, alpha_b, scale,
    r0_main, r0_a, r0_b, r_main, r_a, r_b, u_main, u_a, u_b, v_main, v_a, v_b, p_main, p_a, p_b,
    shifter, part, part_in,
    load_sem, send0, recv0, sends, recvs, ar_send, ar_recv,
):
    n_gx, n_gy, n_gz = sizes
    gx, gy, gz = lax.axis_index("gx"), lax.axis_index("gy"), lax.axis_index("gz")

    def device(s):
        return (
            lax.rem(gx + s[1] + n_gx, n_gx),
            lax.rem(gy + s[2] + n_gy, n_gy),
            lax.rem(gz + s[0] + n_gz, n_gz),
        )

    barrier = pltpu.get_barrier_semaphore()
    for s in DIRS:
        pl.semaphore_signal(barrier, inc=1, device_id=device(s), device_id_type=MESH)

    loads = [
        pltpu.make_async_copy(a, b, load_sem.at[i])
        for i, (a, b) in enumerate(
            ((depth_hbm, in_depth), (perm_hbm, in_perm), (stor_hbm, in_stor), (src_hbm, in_src))
        )
    ]
    for copy in loads:
        copy.start()

    zero_plane = jnp.zeros((ROWS, LANES), jnp.float32)
    own_rows[...] = jnp.zeros(own_rows.shape, jnp.float32)
    own_side[...] = jnp.zeros(own_side.shape, jnp.float32)
    for ref in (k_main, s_main, q_main):
        ref[...] = jnp.zeros((FLAT, LANES), jnp.float32)
    for ref in (r0_main, r_main, u_main, v_main, p_main):
        ref[0 : PAD + ROWS] = jnp.zeros((PAD + ROWS, LANES), jnp.float32)
        ref[FLAT - PAD - ROWS :] = jnp.zeros((PAD + ROWS, LANES), jnp.float32)
    for ref in (k_a, k_b, r0_a, r0_b, r_a, r_b, u_a, u_b, v_a, v_b, p_a, p_b):
        ref[...] = jnp.zeros((SIDE, LANES), jnp.float32)

    at_in, at_out = iota(0, (2 * LANES, 2 * LANES)), iota(1, (2 * LANES, 2 * LANES))
    from_lane = lax.rem(at_out + jnp.where(at_out < LANES, LANES - 1, 1), LANES)
    shifter[...] = jnp.where(lax.rem(at_in, LANES) == from_lane, 1.0, 0.0).astype(jnp.bfloat16)

    lane, row = iota(1), iota(0)
    x = row - 4
    z_fa, y_fa = classes((ROWS, LANES), 0)
    z_fb, y_fb = classes((ROWS, LANES), 5)
    z_pa, y_pa = classes((ROWS, LANES), 1)
    z_pb, y_pb = classes((ROWS, LANES), 4)
    y_fa, y_fb, y_pa, y_pb = y_fa - 2, y_fb - 7, y_pa - 3, y_pb - 6

    def gather(accs, z, value):
        at = iota(1, value.shape)
        moved = roll(value, STEP * z + 2)
        return (
            jnp.where(lanes_between(at, STEP * z + 2, STEP * z + 8), moved, accs[0]),
            jnp.where(lanes_between(at, STEP * z - 5, STEP * z + 1), moved, accs[1]),
        )

    for copy in loads:
        copy.wait()

    depth = in_depth[...]
    for z in range(8):
        in_perm[z] = jnp.where((gz * 8 + z) < depth, in_perm[z], 0.0)

    pl.semaphore_wait(barrier, len(DIRS))

    started = []
    exchange0 = []

    def post0(src, dst, s):
        i = len(exchange0)
        copy = pltpu.make_async_remote_copy(
            src_ref=src, dst_ref=dst, send_sem=send0.at[i], recv_sem=recv0.at[i],
            device_id=device(s), device_id_type=MESH,
        )
        copy.start()
        exchange0.append(copy)
        started.append(copy)

    for sz in (-1, 1):
        u = part_of(sz)
        post0(in_perm.at[pl.ds(5 * u, 3)], rz_k.at[u], (sz, 0, 0))
        post0(in_stor.at[pl.ds(6 * u, 2)], rz_s.at[u], (sz, 0, 0))
        post0(in_src.at[pl.ds(6 * u, 2)], rz_q.at[u], (sz, 0, 0))
    zero_block = jnp.zeros((32, LANES), jnp.float32)
    edges = [(zero_block, zero_block)] * 3
    for z in range(8):
        for f, ref in enumerate((in_perm, in_stor, in_src)):
            edges[f] = gather(edges[f], z + 3, ref[z])
        for v, low in ((0, 0), (1, 29)):
            own_rows[v, z, 0:3] = in_perm[z, low : low + 3]
            for i, ref in ((3, in_stor), (5, in_src)):
                own_rows[v, z, i : i + 2] = ref[z, low + v : low + v + 2]
    _, c = classes((32, LANES), 4)
    own_side[0, 4:36] = jnp.where(
        c >= 6, edges[0][0], jnp.where(c >= 3, roll(edges[1][0], -3), roll(edges[2][0], -6))
    )
    _, c = classes((32, LANES), 1)
    own_side[1, 4:36] = jnp.where(
        c < 3, edges[0][1], jnp.where(c < 6, roll(edges[1][1], 3), roll(edges[2][1], 6))
    )
    for d in range(2):
        for u in range(2):
            own_fold[u, d] = fold(own_side[d], STEP * (8 if u else 3) - (1 if d else 4))
    for s in DIRS:
        sz, sx, sy = s
        u, v, d = part_of(sz), part_of(sx), part_of(sy)
        if sy == 0:
            if sz == 0:
                post0(own_rows.at[v], rx0.at[v], s)
            elif sx != 0:
                post0(own_rows.at[v, pl.ds(5 * u, 3)], rzx0.at[u, v], s)
        elif sx != 0:
            post0(own_side.at[d, row_tile(sx)], rxy0.at[sz + 1, v, d], s)
        elif sz != 0:
            post0(own_fold.at[u, d], rzy0.at[u, d], s)
        else:
            post0(own_side.at[d], ry0.at[d], s)
    for copy in exchange0:
        copy.wait_recv()

    def inside(flag):
        return flag.astype(jnp.float32)

    below, above = inside(gz > 0), inside(gz < n_gz - 1)
    before, after = inside(gx > 0), inside(gx < n_gx - 1)
    in_z = {z: below if z < 3 else above for z in (0, 1, 2, 11, 12, 13)}
    for z in range(PLANES):
        base = PAD + ROWS * z
        if 3 <= z <= 10:
            middle = in_perm[z - 3]
            low, high = rx0[1, z - 3], rx0[0, z - 3]
            gain = 1.0
            s_main[base + 4 : base + 36] = in_stor[z - 3]
            q_main[base + 4 : base + 36] = in_src[z - 3]
        else:
            u, i = (1, z) if z < 3 else (0, z - 11)
            middle = rz_k[u, i] * in_z[z]
            low, high = rzx0[u, 1, i], rzx0[u, 0, i]
            gain = in_z[z]
            if 1 <= z <= 12:
                i = z - 1 if z < 3 else z - 11
                s_main[base + 4 : base + 36] = rz_s[u, i]
                q_main[base + 4 : base + 36] = rz_q[u, i]
        k_main[base + 4 : base + 36] = middle
        k_main[base + 1 : base + 4] = low[0:3] * (before * gain)
        k_main[base + 36 : base + 39] = high[0:3] * (after * gain)
        s_main[base + 2 : base + 4] = low[3:5]
        s_main[base + 36 : base + 38] = high[3:5]
        q_main[base + 2 : base + 4] = low[5:7]
        q_main[base + 36 : base + 38] = high[5:7]

    def z_sum(here, lower, upper, offset, shift=0, move=roll, reach=5):
        z, _ = classes(here.shape, offset)
        moved = jnp.where(
            z < reach, move(lower, -8 * STEP - shift),
            jnp.where(between(z, 14 - reach, 13), move(upper, 8 * STEP + shift), 0.0),
        )
        return here + moved

    def beside(y, zy, xy, d, reach=5):
        offset = 1 if d else 4
        return add_tiles(
            z_sum(y[d], zy[1, d], zy[0, d], offset, move=unfold, reach=reach),
            z_sum(xy[1, 1, d], xy[2, 1, d], xy[0, 1, d], offset, reach=reach),
            z_sum(xy[1, 0, d], xy[2, 0, d], xy[0, 0, d], offset, reach=reach),
        )

    from_left, from_right = (beside(ry0, rzy0, rxy0, d, 3) for d in (1, 0))

    def grid_z(z):
        return both(either(z >= 3, gz > 0), either(z <= 10, gz < n_gz - 1))

    row_in = both(either(x >= 0, gx > 0), either(x < 32, gx < n_gx - 1))
    gain_a = jnp.where(both(row_in, grid_z(z_pa), gy > 0), 1.0, 0.0)
    gain_b = jnp.where(both(row_in, grid_z(z_pb), gy < n_gy - 1), 1.0, 0.0)
    k_edges, s_edges, q_edges = ((zero_plane, zero_plane) for _ in range(3))
    for z in range(PLANES):
        k_edges = gather(k_edges, z, k_main[plane(z)])
        if 1 <= z <= 12:
            s_edges = gather(s_edges, z, s_main[plane(z)])
            q_edges = gather(q_edges, z, q_main[plane(z)])
    k_left, k_right = from_left * gain_a, from_right * gain_b
    k_fa = jnp.where(both(y_pa >= -2, y_pa <= -1), k_left, k_edges[0])
    k_fb = jnp.where(both(y_pb >= 0, y_pb <= 1), k_right, k_edges[1])
    k_pa = jnp.where(y_pa == -3, k_left, k_fa)
    k_pb = jnp.where(y_pb == 2, k_right, k_fb)
    k_a[MIDDLE] = k_fa
    k_b[MIDDLE] = k_fb
    s_a = jnp.where(both(y_pa >= -2, y_pa <= -1), roll(from_left, -3), s_edges[0])
    q_a = jnp.where(both(y_pa >= -2, y_pa <= -1), roll(from_left, -6), q_edges[0])
    s_b = jnp.where(both(y_pb >= 0, y_pb <= 1), roll(from_right, 3), s_edges[1])
    q_b = jnp.where(both(y_pb >= 0, y_pb <= 1), roll(from_right, 6), q_edges[1])

    def weights(centre, others, storage, source, keep):
        idle = jnp.where(centre > 0.0, 0.0, 1.0)
        diagonal = storage + idle
        couplings = []
        for other in others:
            other_idle = jnp.where(other > 0.0, 0.0, 1.0)
            c = (2.0 * centre) * other / ((centre + idle) + (other + other_idle))
            couplings.append(c)
            diagonal = diagonal + c
        gain = jnp.where(keep, RELAX / diagonal, 0.0)
        live = jnp.where(keep, 1.0 - idle, 0.0)
        return [c * gain for c in couplings], live * gain * source, live * RELAX, diagonal

    def around(ref, z, count=1):
        base, rows = PAD + ROWS * z, ROWS * count
        return (
            ref[pl.ds(base - ROWS, rows)],
            ref[pl.ds(base + ROWS, rows)],
            ref[pl.ds(base - 1, rows)],
            ref[pl.ds(base + 1, rows)],
        )

    def side_around(ref, centre):
        return (
            roll(centre, STEP), roll(centre, -STEP), ref[pl.ds(PAD - 1, ROWS)], ref[pl.ds(PAD + 1, ROWS)],
        )

    rows_kept, rows_own = between(row, 2, 37), between(row, 4, 35)
    inner = both(lane > 0, lane < LANES - 1)
    total = zero_plane
    r_edges = (zero_plane, zero_plane)
    for z in range(1, 13):
        centre = k_main[plane(z)]
        ws, r, al, diagonal = weights(
            centre, around(k_main, z) + (roll(centre, 1), roll(centre, -1)),
            s_main[plane(z)], q_main[plane(z)], rows_kept,
        )
        for i in range(6):
            w_main[i, plane(z)] = ws[i]
        alpha[plane(z)] = al
        r0_main[plane(z)] = r
        r_edges = gather(r_edges, z, r)
        if 3 <= z <= 10:
            sc = jnp.where(both(rows_own, inner), diagonal * (1.0 / RELAX), 0.0)
            scale[z - 3] = sc
            total = total + (r * sc) * (r * sc)
    scale_side = []
    for ref, k_f, left, right, st, q, z, y, low, high, w_ref, al_ref, r_ref, edge, own in (
        (k_a, k_fa, k_pa, k_fa, s_a, q_a, z_fa, y_fa, -2, 5, w_a, alpha_a, r0_a, r_edges[0], 0),
        (k_b, k_fb, k_fb, k_pb, s_b, q_b, z_fb, y_fb, -6, 1, w_b, alpha_b, r0_b, r_edges[1], -1),
    ):
        keep = both(rows_kept, between(z, 1, 12), between(y, low, high))
        ws, r, al, diagonal = weights(
            k_f, side_around(ref, k_f) + (roll(left, 1), roll(right, -1)), st, q, keep
        )
        for i in range(6):
            w_ref[i] = ws[i]
        if low == -2:
            w_ref[6] = jnp.where(y == -2, 0.0, ws[4])
        else:
            w_ref[6] = jnp.where(y == 1, 0.0, ws[5])
        al_ref[...] = al
        r_ref[MIDDLE] = jnp.where(y <= 0 if low == -2 else y >= -1, r, edge)
        sc = jnp.where(
            both(rows_own, between(z, 3, 10), y == own), diagonal * (1.0 / RELAX), 0.0
        )
        scale_side.append(sc)
        total = total + (r * sc) * (r * sc)

    def half(flag):
        return jnp.where(flag, 0.5, 1.0)

    def axis_gain(position, extent, owner, owners):
        inner_low = both(position >= 0, position < 2, owner > 0)
        inner_high = both(position >= extent - 2, position < extent, owner < owners - 1)
        outer = either(
            both(position >= -2, position < 0), both(position >= extent, position < extent + 2)
        )
        return half(either(outer, inner_low, inner_high))

    x_gain = axis_gain(x, 32, gx, n_gx)
    main_gain = x_gain * axis_gain(lane, 128, gy, n_gy)
    side_gain = (
        x_gain * axis_gain(z_pa - 3, 8, gz, n_gz) * axis_gain(y_pa, 128, gy, n_gy),
        x_gain * axis_gain(z_pb - 3, 8, gz, n_gz) * axis_gain(y_pb + 128, 128, gy, n_gy),
    )

    def z_gain(z):
        if z in (0, 13):
            return 1.0
        if z in (1, 2, 11, 12):
            return 0.5
        if z in (3, 4):
            return jnp.where(gz > 0, 0.5, 1.0)
        if z in (9, 10):
            return jnp.where(gz < n_gz - 1, 0.5, 1.0)
        return 1.0

    def side_sweep(ref, rhs, w_ref, last):
        value = ref[MIDDLE]
        others = side_around(ref, value) + (roll(value, 1), roll(value, -1))
        value = (1.0 - RELAX) * value + rhs[MIDDLE]
        for i, other in enumerate(others):
            value = value + w_ref[6 if i == last else i] * other
        return value

    def main_sweep(ref, rhs, z):
        value = ref[plane(z, 2)]
        hi = value.astype(jnp.bfloat16)
        lo = (value - hi.astype(jnp.float32)).astype(jnp.bfloat16)
        beside_y = jnp.dot(
            jnp.concatenate([hi, lo], axis=1), shifter[...], preferred_element_type=jnp.float32
        )
        others = around(ref, z, 2) + (beside_y[:, :LANES], beside_y[:, LANES:])
        value = (1.0 - RELAX) * value + rhs[plane(z, 2)]
        for i, other in enumerate(others):
            value = value + w_main[i, plane(z, 2)] * other
        return value

    partials = [total]
    for k in range(ITERS):
        rhs, rhs_a, rhs_b = (r0_main, r0_a, r0_b) if k == 0 else (r_main, r_a, r_b)
        copies = []
        last_one = k == ITERS - 1

        def post(source, target, s):
            i = DIRS.index(s)
            copy = pltpu.make_async_remote_copy(
                src_ref=source, dst_ref=target, send_sem=sends.at[k, i], recv_sem=recvs.at[k, i],
                device_id=device(s), device_id_type=MESH,
            )
            copy.start()
            copies.append(copy)
            started.append(copy)

        for before_ref, after_ref in (((rhs_a, rhs_b), (u_a, u_b)), ((u_a, u_b), (v_a, v_b))):
            after_ref[0][MIDDLE] = side_sweep(before_ref[0], rhs_a, w_a, 4)
            after_ref[1][MIDDLE] = side_sweep(before_ref[1], rhs_b, w_b, 5)
        side_a = side_sweep(v_a, rhs_a, w_a, 4)
        side_b = side_sweep(v_b, rhs_b, w_b, 5)
        far_b = roll(side_b, 64)
        send[k, 0] = jnp.where(lane < 60, side_a, far_b)
        send[k, 13] = jnp.where(lane < 60, far_b, side_a)
        send[k, 14] = side_a
        send[k, 15] = side_b
        for d, value in ((0, side_a), (1, side_b)):
            for u in range(2):
                fold_out[k, u, d] = fold(value, STEP * (8 if u else 1) - d)
        for s in DIRS:
            sz, sx, sy = s
            u, v, d = part_of(sz), part_of(sx), part_of(sy)
            if sy != 0:
                if sx != 0:
                    post(send.at[k, 14 + d, row_tile(sx)], rxy.at[k, sz + 1, v, d], s)
                elif sz != 0:
                    post(fold_out.at[k, u, d], rzy.at[k, u, d], s)
                else:
                    post(send.at[k, 14 + d], ry.at[k, d], s)

        for z in range(1, 13, 2):
            u_main[plane(z, 2)] = main_sweep(rhs, rhs, z)
        for z in range(1, 13, 2):
            v_main[plane(z, 2)] = main_sweep(u_main, rhs, z)
        for z in (1, 3, 5, 11, 9, 7):
            value = main_sweep(v_main, rhs, z)
            send[k, z] = value[:ROWS]
            send[k, z + 1] = value[ROWS:]
            if z in (5, 7):
                sz = -1 if z == 5 else 1
                count = 4 if last_one else 6
                skip = 6 - count if sz > 0 else 0
                planes, places = pl.ds((8 if sz > 0 else 0) + skip, count), pl.ds(skip, count)
                u = part_of(sz)
                for v, low in ((0, 2), (1, 33)):
                    for i in range(6):
                        zx_out[k, u, v, 2 + 5 * i : 7 + 5 * i] = send[
                            k, (8 + i) if u else i, low : low + 5
                        ]
                    post(
                        zx_out.at[k, u, v], rzx.at[k, u, v, pl.ds(0, 32)], (sz, 2 * v - 1, 0)
                    )
                post(send.at[k, planes], rz.at[k, part_of(sz), places], (sz, 0, 0))
        for sx in (-1, 1):
            post(send.at[k, pl.ds(1, 15), row_tile(sx)], rx.at[k, part_of(sx)], (0, sx, 0))
        for copy in copies:
            copy.wait_recv()

        def edge_rows(u, v, i):
            at = iota(0, (8, LANES))
            tile = rzx[k, u, v, 5 * i + v : 5 * i + v + 8]
            return jnp.where(between(at, 2 - v, 6 - v), tile, 0.0)

        new_p = []
        for own, d, offset, shift, y, low, high, outer_low, outer_high, ref in (
            (14, 1, 1, 0, y_pa, -2, 3, -3, 1, p_a),
            (15, 0, 4, 64, y_pb, -4, 1, -2, 2, p_b),
        ):
            here = add_tiles(
                z_sum(send[k, own], rz[k, 1, 5], rz[k, 0, 0], offset, shift),
                z_sum(rx[k, 1, own - 1], edge_rows(1, 1, 5), edge_rows(0, 1, 0), offset, shift),
                z_sum(rx[k, 0, own - 1], edge_rows(1, 0, 5), edge_rows(0, 0, 0), offset, shift),
            )
            other = beside(ry.at[k], rzy.at[k], rxy.at[k], d)
            value = jnp.where(between(y, low, high), here, 0.0) + jnp.where(
                between(y, outer_low, outer_high), other, 0.0
            )
            value = value * side_gain[1 - d]
            if k > 0:
                value = ref[MIDDLE] + value
            ref[MIDDLE] = value
            new_p.append(value)
        edges = jnp.where(between(y_pa, 0, 3), new_p[0], new_p[1])
        edge_lane = either(lane < 4, lane >= LANES - 4)
        for z in range(2, 12) if last_one else range(PLANES):
            solved = 1 <= z <= 12
            value = send[k, z] if solved else zero_plane
            first = rx[k, 1, z - 1] if solved else jnp.zeros((8, LANES), jnp.float32)
            last = rx[k, 0, z - 1] if solved else jnp.zeros((8, LANES), jnp.float32)
            if z <= 4:
                value = value + rz[k, 1, z]
                first = first + edge_rows(1, 1, z)
                last = last + edge_rows(1, 0, z)
            if z >= 9:
                value = value + rz[k, 0, z - 8]
                first = first + edge_rows(0, 1, z - 8)
                last = last + edge_rows(0, 0, z - 8)
            value = add_tiles(value, first, last) * (main_gain * z_gain(z))
            if k > 0:
                value = p_main[plane(z)] + value
            p_main[plane(z)] = jnp.where(edge_lane, roll(edges, -(STEP * z + 2)), value)

        total = zero_plane
        r_edges = (zero_plane, zero_plane)
        for z in range(3, 11) if last_one else range(1, 13):
            centre = p_main[plane(z)]
            value = r0_main[plane(z)] - alpha[plane(z)] * centre
            for i, other in enumerate(
                around(p_main, z) + (roll(centre, 1), roll(centre, -1))
            ):
                value = value + w_main[i, plane(z)] * other
            if not last_one:
                r_main[plane(z)] = value
                r_edges = gather(r_edges, z, value)
            if 3 <= z <= 10:
                value = value * scale[z - 3]
                total = total + value * value
        for i, (ref, r0, al, w_ref, r_ref, p) in enumerate(
            ((p_a, r0_a, alpha_a, w_a, r_a, new_p[0]), (p_b, r0_b, alpha_b, w_b, r_b, new_p[1]))
        ):
            value = r0[MIDDLE] - al[...] * p
            for n, other in enumerate(side_around(ref, p) + (roll(p, 1), roll(p, -1))):
                value = value + w_ref[n] * other
            if not last_one:
                r_ref[MIDDLE] = jnp.where(y_fa <= 0 if i == 0 else y_fb >= -1, value, r_edges[i])
            value = value * scale_side[i]
            total = total + value * value
        partials.append(total)

    for z in range(8):
        out_ref[z] = p_main[pl.ds(PAD + ROWS * (z + 3) + 4, 32)]

    at = iota(1, (1, LANES)) // 32
    mine = jnp.zeros((1, LANES), jnp.float32)
    for i, value in enumerate(partials):
        value = jnp.sum(value, axis=0, keepdims=True)
        value = value + roll(value, 64)
        mine = jnp.where(at == i, value + roll(value, 32), mine)
    pair = gy + 1 - 2 * lax.rem(gy, 2)

    def ring(i, n):
        return min(i, n - i)

    rounds = (
        sorted(
            ((i, h) for i in range(n_gx) for h in range(2) if (i, h) != (0, 0)),
            key=lambda t: -ring(t[0], n_gx) - 0.3 * t[1],
        ),
        sorted(
            ((i, h) for i in range(n_gy // 2) for h in range(n_gz) if (i, h) != (0, 0)),
            key=lambda t: -ring(t[0], n_gy // 2) - ring(t[1], n_gz),
        ),
    )
    rounds = (
        [(lax.rem(gx + i, n_gx), gy if h == 0 else pair, gz) for i, h in rounds[0]],
        [(gx, lax.rem(gy + 2 * i, n_gy), lax.rem(gz + h, n_gz)) for i, h in rounds[1]],
    )
    slots = (gx * 2 + lax.rem(gy, 2), (gy // 2) * n_gz + gz)
    for n, targets in enumerate(rounds):
        here = part_in.at[n, slots[n], pl.ds(0, 1)]
        part[n, 0:1] = mine
        copies = []
        for i, target in enumerate(targets):
            copy = pltpu.make_async_remote_copy(
                src_ref=part.at[n, pl.ds(0, 1)], dst_ref=here,
                send_sem=ar_send.at[n, i], recv_sem=ar_recv.at[n, i],
                device_id=target, device_id_type=MESH,
            )
            copy.start()
            copies.append(copy)
            started.append(copy)
        here[...] = mine
        for copy in copies:
            copy.wait_recv()
        terms = [part_in[n, i, 0:1] for i in range(len(targets) + 1)]
        while len(terms) > 1:
            terms = [sum(terms[i + 1 : i + 2], terms[i]) for i in range(0, len(terms), 2)]
        mine = terms[0]
    squares = [
        jnp.sum(jnp.where(at == i, mine, 0.0), axis=1, keepdims=True) for i in range(ITERS + 1)
    ]
    for i in range(ITERS):
        hist_ref[i] = jnp.sum(jnp.sqrt(squares[i + 1] / squares[0]))
    for copy in started:
        copy.wait_send()


def solution(mesh):
    sizes = (mesh.shape["gx"], mesh.shape["gy"], mesh.shape["gz"])
    f32 = jnp.float32

    def vmem(*shape):
        return pltpu.VMEM(shape, f32)

    n_dirs = len(DIRS)
    n_first = n_dirs + 4
    scratch = [
        vmem(8, 32, LANES), vmem(8, 32, LANES), vmem(8, 32, LANES),
        pltpu.VMEM((32, LANES), jnp.int32),
        vmem(2, 8, 8, LANES), vmem(2, ROWS, LANES), vmem(2, 2, 16, LANES),
        vmem(2, 3, 32, LANES), vmem(2, 2, 32, LANES), vmem(2, 2, 32, LANES),
        vmem(2, 8, 8, LANES), vmem(2, 2, 3, 8, LANES),
        vmem(2, ROWS, LANES), vmem(2, 2, 16, LANES), vmem(3, 2, 2, 8, LANES),
        vmem(ITERS, 16, ROWS, LANES), vmem(ITERS, 2, 2, 32, LANES), vmem(ITERS, 2, 2, 16, LANES),
        vmem(ITERS, 2, 6, ROWS, LANES), vmem(ITERS, 2, 15, 8, LANES),
        vmem(ITERS, 2, 2, 40, LANES),
        vmem(ITERS, 2, ROWS, LANES), vmem(ITERS, 2, 2, 16, LANES), vmem(ITERS, 3, 2, 2, 8, LANES),
        vmem(FLAT, LANES), vmem(SIDE, LANES), vmem(SIDE, LANES), vmem(FLAT, LANES), vmem(FLAT, LANES),
        vmem(6, FLAT, LANES), vmem(7, ROWS, LANES), vmem(7, ROWS, LANES),
        vmem(FLAT, LANES), vmem(ROWS, LANES), vmem(ROWS, LANES), vmem(8, ROWS, LANES),
    ]
    for _ in range(5):
        scratch += [vmem(FLAT, LANES), vmem(SIDE, LANES), vmem(SIDE, LANES)]
    scratch += [
        pltpu.VMEM((2 * LANES, 2 * LANES), jnp.bfloat16),
        vmem(2, 8, LANES), vmem(2, 16, 8, LANES),
        pltpu.SemaphoreType.DMA((4,)),
        pltpu.SemaphoreType.DMA((n_first,)), pltpu.SemaphoreType.DMA((n_first,)),
        pltpu.SemaphoreType.DMA((ITERS, n_dirs)), pltpu.SemaphoreType.DMA((ITERS, n_dirs)),
        pltpu.SemaphoreType.DMA((2, 15)), pltpu.SemaphoreType.DMA((2, 15)),
    ]

    def per_device(source, permeability, storage, column_depth):
        return pl.pallas_call(
            functools.partial(kernel, sizes),
            out_shape=(
                jax.ShapeDtypeStruct(source.shape, f32),
                jax.ShapeDtypeStruct((ITERS,), f32),
            ),
            in_specs=[pl.BlockSpec(memory_space=pl.ANY)] * 4,
            out_specs=(
                pl.BlockSpec(memory_space=pltpu.VMEM),
                pl.BlockSpec(memory_space=pltpu.SMEM),
            ),
            scratch_shapes=scratch,
            compiler_params=pltpu.CompilerParams(
                collective_id=0, has_side_effects=True, vmem_limit_bytes=55056 * 2**10
            ),
            name="schwarz",
        )(source, permeability, storage, column_depth)

    placed = (P("gz", "gx", "gy"), P("gz", "gx", "gy"), P("gz", "gx", "gy"), P("gx", "gy"))
    return jax.shard_map(
        per_device,
        mesh=mesh,
        in_specs=placed,
        out_specs=(P("gz", "gx", "gy"), P()),
        check_vma=False,
    )
```

```python
import functools
import math

import jax
import jax.numpy as jnp
from jax import lax
from jax.experimental import pallas as pl
from jax.experimental.pallas import tpu as pltpu
from jax.sharding import PartitionSpec as P

MESH = pl.DeviceIdType.MESH
ITERS = 3
RELAX = 0.9

PLANES, ROWS, LANES, PAD, STEP = 14, 40, 128, 8, 9
FLAT = PLANES * ROWS + 2 * PAD
SIDE = ROWS + 2 * PAD
DIRS = tuple(
    (sz, sx, sy)
    for sz in (-1, 0, 1)
    for sx in (-1, 0, 1)
    for sy in (-1, 0, 1)
    if (sz, sx, sy) != (0, 0, 0)
)
DIRS = tuple(sorted(DIRS, key=lambda s: -(abs(s[0]) + abs(s[1]) + abs(s[2]))))


def plane(z, count=1):
    return pl.ds(PAD + ROWS * z, ROWS * count)


MIDDLE = pl.ds(PAD, ROWS)


def iota(axis, shape=(ROWS, LANES)):
    return lax.broadcasted_iota(jnp.int32, shape, axis)


def roll(x, shift):
    return pltpu.roll(x, shift % LANES, axis=x.ndim - 1)


def both(*flags):
    return functools.reduce(jnp.logical_and, flags)


def either(*flags):
    return functools.reduce(jnp.logical_or, flags)


def between(x, low, high):
    return both(x >= low, x <= high)


def lanes_between(lane, low, high):
    if low < 0:
        return either(lane >= low + LANES, lane <= high)
    return between(lane, low, high)


def classes(shape, offset):
    u = lax.rem(iota(1, shape) + offset, LANES)
    z = (u * 57) >> 9
    return z, u - STEP * z


def row_tile(sx):
    return {0: pl.ds(0, ROWS), 1: pl.ds(ROWS - 8, 8), -1: pl.ds(0, 8)}[sx]


def add_tiles(acc, first, last):
    return jnp.concatenate([acc[:8] + first, acc[8 : ROWS - 8], acc[ROWS - 8 :] + last], axis=0)


WIDTH = 43


def fold(side, first):
    t = [side[8 * i : 8 * i + 8] for i in range(5)]
    at = lax.rem(iota(1, (8, LANES)) + (LANES - first), LANES)
    one = jnp.where(
        at < WIDTH, t[0], jnp.where(at < 2 * WIDTH, roll(t[1], WIDTH), roll(t[2], 2 * WIDTH))
    )
    two = jnp.where(at < WIDTH, t[3], roll(t[4], WIDTH))
    return jnp.concatenate([one, two], axis=0)


def unfold(both_tiles, shift):
    return jnp.concatenate(
        [roll(both_tiles[8 * (i // 3) : 8 * (i // 3) + 8], shift - WIDTH * (i % 3)) for i in range(5)],
        axis=0,
    )


def part_of(v):
    return (v + 1) // 2


def kernel(
    sizes, src_hbm, perm_hbm, stor_hbm, depth_hbm, out_ref, hist_ref,
    in_src, in_perm, in_stor, in_depth,
    own_rows, own_side, own_fold, rz_k, rz_s, rz_q, rx0, rzx0, ry0, rzy0, rxy0,
    send, zx_out, fold_out, rz, rx, rzx, ry, rzy, rxy,
    k_main, k_a, k_b, s_main, q_main,
    w_main, w_a, w_b, alpha, alpha_a, alpha_b, scale,
    r0_main, r0_a, r0_b, r_main, r_a, r_b, u_main, u_a, u_b, v_main, v_a, v_b, p_main, p_a, p_b,
    shifter, part, part_in, tally,
    load_sem, send0, recv0, sends, recvs, ar_send, ar_recv,
):
    n_gx, n_gy, n_gz = sizes
    gx, gy, gz = lax.axis_index("gx"), lax.axis_index("gy"), lax.axis_index("gz")

    def device(s):
        return (
            lax.rem(gx + s[1] + n_gx, n_gx),
            lax.rem(gy + s[2] + n_gy, n_gy),
            lax.rem(gz + s[0] + n_gz, n_gz),
        )

    def wait_rows(sem, rows):
        span = tally.at[pl.ds(0, rows)]
        pltpu.make_async_copy(span, span, sem).wait()

    def rows_of(ref):
        return math.prod(ref.shape[:-1])

    barrier = pltpu.get_barrier_semaphore()
    for s in DIRS:
        pl.semaphore_signal(barrier, inc=1, device_id=device(s), device_id_type=MESH)

    loads = [
        pltpu.make_async_copy(a, b, load_sem)
        for a, b in (
            (depth_hbm, in_depth), (perm_hbm, in_perm), (stor_hbm, in_stor), (src_hbm, in_src)
        )
    ]
    for copy in loads:
        copy.start()

    zero_plane = jnp.zeros((ROWS, LANES), jnp.float32)
    own_rows[...] = jnp.zeros(own_rows.shape, jnp.float32)
    own_side[...] = jnp.zeros(own_side.shape, jnp.float32)
    for ref in (k_main, s_main, q_main):
        ref[...] = jnp.zeros((FLAT, LANES), jnp.float32)
    for ref in (r0_main, r_main, u_main, v_main, p_main):
        ref[0 : PAD + ROWS] = jnp.zeros((PAD + ROWS, LANES), jnp.float32)
        ref[FLAT - PAD - ROWS :] = jnp.zeros((PAD + ROWS, LANES), jnp.float32)
    for ref in (k_a, k_b, r0_a, r0_b, r_a, r_b, u_a, u_b, v_a, v_b, p_a, p_b):
        ref[...] = jnp.zeros((SIDE, LANES), jnp.float32)

    at_in, at_out = iota(0, (2 * LANES, 2 * LANES)), iota(1, (2 * LANES, 2 * LANES))
    from_lane = lax.rem(at_out + jnp.where(at_out < LANES, LANES - 1, 1), LANES)
    shifter[...] = jnp.where(lax.rem(at_in, LANES) == from_lane, 1.0, 0.0).astype(jnp.bfloat16)

    lane, row = iota(1), iota(0)
    x = row - 4
    z_fa, y_fa = classes((ROWS, LANES), 0)
    z_fb, y_fb = classes((ROWS, LANES), 5)
    z_pa, y_pa = classes((ROWS, LANES), 1)
    z_pb, y_pb = classes((ROWS, LANES), 4)
    y_fa, y_fb, y_pa, y_pb = y_fa - 2, y_fb - 7, y_pa - 3, y_pb - 6

    def gather(accs, z, value):
        at = iota(1, value.shape)
        moved = roll(value, STEP * z + 2)
        return (
            jnp.where(lanes_between(at, STEP * z + 2, STEP * z + 8), moved, accs[0]),
            jnp.where(lanes_between(at, STEP * z - 5, STEP * z + 1), moved, accs[1]),
        )

    wait_rows(load_sem, 3 * 8 * 32 + 32)

    depth = in_depth[...]
    for z in range(8):
        in_perm[z] = jnp.where((gz * 8 + z) < depth, in_perm[z], 0.0)

    pl.semaphore_wait(barrier, len(DIRS))

    rows0 = []

    def post0(src, dst, s):
        pltpu.make_async_remote_copy(
            src_ref=src, dst_ref=dst, send_sem=send0, recv_sem=recv0,
            device_id=device(s), device_id_type=MESH,
        ).start()
        rows0.append(rows_of(src))

    for sz in (-1, 1):
        u = part_of(sz)
        post0(in_perm.at[pl.ds(5 * u, 3)], rz_k.at[u], (sz, 0, 0))
        post0(in_stor.at[pl.ds(6 * u, 2)], rz_s.at[u], (sz, 0, 0))
        post0(in_src.at[pl.ds(6 * u, 2)], rz_q.at[u], (sz, 0, 0))
    zero_block = jnp.zeros((32, LANES), jnp.float32)
    edges = [(zero_block, zero_block)] * 3
    for z in range(8):
        for f, ref in enumerate((in_perm, in_stor, in_src)):
            edges[f] = gather(edges[f], z + 3, ref[z])
        for v, low in ((0, 0), (1, 29)):
            own_rows[v, z, 0:3] = in_perm[z, low : low + 3]
            for i, ref in ((3, in_stor), (5, in_src)):
                own_rows[v, z, i : i + 2] = ref[z, low + v : low + v + 2]
    _, c = classes((32, LANES), 4)
    own_side[0, 4:36] = jnp.where(
        c >= 6, edges[0][0], jnp.where(c >= 3, roll(edges[1][0], -3), roll(edges[2][0], -6))
    )
    _, c = classes((32, LANES), 1)
    own_side[1, 4:36] = jnp.where(
        c < 3, edges[0][1], jnp.where(c < 6, roll(edges[1][1], 3), roll(edges[2][1], 6))
    )
    for d in range(2):
        for u in range(2):
            own_fold[u, d] = fold(own_side[d], STEP * (8 if u else 3) - (1 if d else 4))
    for s in DIRS:
        sz, sx, sy = s
        u, v, d = part_of(sz), part_of(sx), part_of(sy)
        if sy == 0:
            if sz == 0:
                post0(own_rows.at[v], rx0.at[v], s)
            elif sx != 0:
                post0(own_rows.at[v, pl.ds(5 * u, 3)], rzx0.at[u, v], s)
        elif sx != 0:
            post0(own_side.at[d, row_tile(sx)], rxy0.at[sz + 1, v, d], s)
        elif sz != 0:
            post0(own_fold.at[u, d], rzy0.at[u, d], s)
        else:
            post0(own_side.at[d], ry0.at[d], s)
    wait_rows(recv0, sum(rows0))

    def inside(flag):
        return flag.astype(jnp.float32)

    below, above = inside(gz > 0), inside(gz < n_gz - 1)
    before, after = inside(gx > 0), inside(gx < n_gx - 1)
    in_z = {z: below if z < 3 else above for z in (0, 1, 2, 11, 12, 13)}
    for z in range(PLANES):
        base = PAD + ROWS * z
        if 3 <= z <= 10:
            middle = in_perm[z - 3]
            low, high = rx0[1, z - 3], rx0[0, z - 3]
            gain = 1.0
            s_main[base + 4 : base + 36] = in_stor[z - 3]
            q_main[base + 4 : base + 36] = in_src[z - 3]
        else:
            u, i = (1, z) if z < 3 else (0, z - 11)
            middle = rz_k[u, i] * in_z[z]
            low, high = rzx0[u, 1, i], rzx0[u, 0, i]
            gain = in_z[z]
            if 1 <= z <= 12:
                i = z - 1 if z < 3 else z - 11
                s_main[base + 4 : base + 36] = rz_s[u, i]
                q_main[base + 4 : base + 36] = rz_q[u, i]
        k_main[base + 4 : base + 36] = middle
        k_main[base + 1 : base + 4] = low[0:3] * (before * gain)
        k_main[base + 36 : base + 39] = high[0:3] * (after * gain)
        s_main[base + 2 : base + 4] = low[3:5]
        s_main[base + 36 : base + 38] = high[3:5]
        q_main[base + 2 : base + 4] = low[5:7]
        q_main[base + 36 : base + 38] = high[5:7]

    def z_sum(here, lower, upper, offset, shift=0, move=roll, reach=5):
        z, _ = classes(here.shape, offset)
        moved = jnp.where(
            z < reach, move(lower, -8 * STEP - shift),
            jnp.where(between(z, 14 - reach, 13), move(upper, 8 * STEP + shift), 0.0),
        )
        return here + moved

    def beside(y, zy, xy, d, reach=5):
        offset = 1 if d else 4
        return add_tiles(
            z_sum(y[d], zy[1, d], zy[0, d], offset, move=unfold, reach=reach),
            z_sum(xy[1, 1, d], xy[2, 1, d], xy[0, 1, d], offset, reach=reach),
            z_sum(xy[1, 0, d], xy[2, 0, d], xy[0, 0, d], offset, reach=reach),
        )

    from_left, from_right = (beside(ry0, rzy0, rxy0, d, 3) for d in (1, 0))

    def grid_z(z):
        return both(either(z >= 3, gz > 0), either(z <= 10, gz < n_gz - 1))

    row_in = both(either(x >= 0, gx > 0), either(x < 32, gx < n_gx - 1))
    gain_a = jnp.where(both(row_in, grid_z(z_pa), gy > 0), 1.0, 0.0)
    gain_b = jnp.where(both(row_in, grid_z(z_pb), gy < n_gy - 1), 1.0, 0.0)
    k_edges, s_edges, q_edges = ((zero_plane, zero_plane) for _ in range(3))
    for z in range(PLANES):
        k_edges = gather(k_edges, z, k_main[plane(z)])
        if 1 <= z <= 12:
            s_edges = gather(s_edges, z, s_main[plane(z)])
            q_edges = gather(q_edges, z, q_main[plane(z)])
    k_left, k_right = from_left * gain_a, from_right * gain_b
    k_fa = jnp.where(both(y_pa >= -2, y_pa <= -1), k_left, k_edges[0])
    k_fb = jnp.where(both(y_pb >= 0, y_pb <= 1), k_right, k_edges[1])
    k_pa = jnp.where(y_pa == -3, k_left, k_fa)
    k_pb = jnp.where(y_pb == 2, k_right, k_fb)
    k_a[MIDDLE] = k_fa
    k_b[MIDDLE] = k_fb
    s_a = jnp.where(both(y_pa >= -2, y_pa <= -1), roll(from_left, -3), s_edges[0])
    q_a = jnp.where(both(y_pa >= -2, y_pa <= -1), roll(from_left, -6), q_edges[0])
    s_b = jnp.where(both(y_pb >= 0, y_pb <= 1), roll(from_right, 3), s_edges[1])
    q_b = jnp.where(both(y_pb >= 0, y_pb <= 1), roll(from_right, 6), q_edges[1])

    def weights(centre, others, storage, source, keep):
        idle = jnp.where(centre > 0.0, 0.0, 1.0)
        diagonal = storage + idle
        couplings = []
        for other in others:
            other_idle = jnp.where(other > 0.0, 0.0, 1.0)
            c = (2.0 * centre) * other / ((centre + idle) + (other + other_idle))
            couplings.append(c)
            diagonal = diagonal + c
        gain = jnp.where(keep, RELAX / diagonal, 0.0)
        live = jnp.where(keep, 1.0 - idle, 0.0)
        return [c * gain for c in couplings], live * gain * source, live * RELAX, diagonal

    def around(ref, z, count=1):
        base, rows = PAD + ROWS * z, ROWS * count
        return (
            ref[pl.ds(base - ROWS, rows)],
            ref[pl.ds(base + ROWS, rows)],
            ref[pl.ds(base - 1, rows)],
            ref[pl.ds(base + 1, rows)],
        )

    def side_around(ref, centre):
        return (
            roll(centre, STEP), roll(centre, -STEP), ref[pl.ds(PAD - 1, ROWS)], ref[pl.ds(PAD + 1, ROWS)],
        )

    rows_kept, rows_own = between(row, 2, 37), between(row, 4, 35)
    inner = both(lane > 0, lane < LANES - 1)
    total = zero_plane
    r_edges = (zero_plane, zero_plane)
    for z in range(1, 13):
        centre = k_main[plane(z)]
        ws, r, al, diagonal = weights(
            centre, around(k_main, z) + (roll(centre, 1), roll(centre, -1)),
            s_main[plane(z)], q_main[plane(z)], rows_kept,
        )
        for i in range(6):
            w_main[i, plane(z)] = ws[i]
        alpha[plane(z)] = al
        r0_main[plane(z)] = r
        r_edges = gather(r_edges, z, r)
        if 3 <= z <= 10:
            sc = jnp.where(both(rows_own, inner), diagonal * (1.0 / RELAX), 0.0)
            scale[z - 3] = sc
            total = total + (r * sc) * (r * sc)
    scale_side = []
    for ref, k_f, left, right, st, q, z, y, low, high, w_ref, al_ref, r_ref, edge, own in (
        (k_a, k_fa, k_pa, k_fa, s_a, q_a, z_fa, y_fa, -2, 5, w_a, alpha_a, r0_a, r_edges[0], 0),
        (k_b, k_fb, k_fb, k_pb, s_b, q_b, z_fb, y_fb, -6, 1, w_b, alpha_b, r0_b, r_edges[1], -1),
    ):
        keep = both(rows_kept, between(z, 1, 12), between(y, low, high))
        ws, r, al, diagonal = weights(
            k_f, side_around(ref, k_f) + (roll(left, 1), roll(right, -1)), st, q, keep
        )
        for i in range(6):
            w_ref[i] = ws[i]
        if low == -2:
            w_ref[6] = jnp.where(y == -2, 0.0, ws[4])
        else:
            w_ref[6] = jnp.where(y == 1, 0.0, ws[5])
        al_ref[...] = al
        r_ref[MIDDLE] = jnp.where(y <= 0 if low == -2 else y >= -1, r, edge)
        sc = jnp.where(
            both(rows_own, between(z, 3, 10), y == own), diagonal * (1.0 / RELAX), 0.0
        )
        scale_side.append(sc)
        total = total + (r * sc) * (r * sc)

    def half(flag):
        return jnp.where(flag, 0.5, 1.0)

    def axis_gain(position, extent, owner, owners):
        inner_low = both(position >= 0, position < 2, owner > 0)
        inner_high = both(position >= extent - 2, position < extent, owner < owners - 1)
        outer = either(
            both(position >= -2, position < 0), both(position >= extent, position < extent + 2)
        )
        return half(either(outer, inner_low, inner_high))

    x_gain = axis_gain(x, 32, gx, n_gx)
    main_gain = x_gain * axis_gain(lane, 128, gy, n_gy)
    side_gain = (
        x_gain * axis_gain(z_pa - 3, 8, gz, n_gz) * axis_gain(y_pa, 128, gy, n_gy),
        x_gain * axis_gain(z_pb - 3, 8, gz, n_gz) * axis_gain(y_pb + 128, 128, gy, n_gy),
    )

    def z_gain(z):
        if z in (0, 13):
            return 1.0
        if z in (1, 2, 11, 12):
            return 0.5
        if z in (3, 4):
            return jnp.where(gz > 0, 0.5, 1.0)
        if z in (9, 10):
            return jnp.where(gz < n_gz - 1, 0.5, 1.0)
        return 1.0

    def side_sweep(ref, rhs, w_ref, last):
        value = ref[MIDDLE]
        others = side_around(ref, value) + (roll(value, 1), roll(value, -1))
        value = (1.0 - RELAX) * value + rhs[MIDDLE]
        for i, other in enumerate(others):
            value = value + w_ref[6 if i == last else i] * other
        return value

    def main_sweep(ref, rhs, z):
        value = ref[plane(z, 2)]
        hi = value.astype(jnp.bfloat16)
        lo = (value - hi.astype(jnp.float32)).astype(jnp.bfloat16)
        beside_y = jnp.dot(
            jnp.concatenate([hi, lo], axis=1), shifter[...], preferred_element_type=jnp.float32
        )
        others = around(ref, z, 2) + (beside_y[:, :LANES], beside_y[:, LANES:])
        value = (1.0 - RELAX) * value + rhs[plane(z, 2)]
        for i, other in enumerate(others):
            value = value + w_main[i, plane(z, 2)] * other
        return value

    partials = [total]
    sent = [(send0, sum(rows0))]
    for k in range(ITERS):
        rhs, rhs_a, rhs_b = (r0_main, r0_a, r0_b) if k == 0 else (r_main, r_a, r_b)
        rows = []
        last_one = k == ITERS - 1

        def post(source, target, s):
            pltpu.make_async_remote_copy(
                src_ref=source, dst_ref=target, send_sem=sends.at[k], recv_sem=recvs.at[k],
                device_id=device(s), device_id_type=MESH,
            ).start()
            rows.append(rows_of(source))

        for before_ref, after_ref in (((rhs_a, rhs_b), (u_a, u_b)), ((u_a, u_b), (v_a, v_b))):
            after_ref[0][MIDDLE] = side_sweep(before_ref[0], rhs_a, w_a, 4)
            after_ref[1][MIDDLE] = side_sweep(before_ref[1], rhs_b, w_b, 5)
        side_a = side_sweep(v_a, rhs_a, w_a, 4)
        side_b = side_sweep(v_b, rhs_b, w_b, 5)
        far_b = roll(side_b, 64)
        send[k, 0] = jnp.where(lane < 60, side_a, far_b)
        send[k, 13] = jnp.where(lane < 60, far_b, side_a)
        send[k, 14] = side_a
        send[k, 15] = side_b
        for d, value in ((0, side_a), (1, side_b)):
            for u in range(2):
                fold_out[k, u, d] = fold(value, STEP * (8 if u else 1) - d)
        for s in DIRS:
            sz, sx, sy = s
            u, v, d = part_of(sz), part_of(sx), part_of(sy)
            if sy != 0:
                if sx != 0:
                    post(send.at[k, 14 + d, row_tile(sx)], rxy.at[k, sz + 1, v, d], s)
                elif sz != 0:
                    post(fold_out.at[k, u, d], rzy.at[k, u, d], s)
                else:
                    post(send.at[k, 14 + d], ry.at[k, d], s)

        for z in range(1, 13, 2):
            u_main[plane(z, 2)] = main_sweep(rhs, rhs, z)
        for z in range(1, 13, 2):
            v_main[plane(z, 2)] = main_sweep(u_main, rhs, z)
        for z in (1, 3, 5, 11, 9, 7):
            value = main_sweep(v_main, rhs, z)
            send[k, z] = value[:ROWS]
            send[k, z + 1] = value[ROWS:]
            if z in (5, 7):
                sz = -1 if z == 5 else 1
                count = 4 if last_one else 6
                skip = 6 - count if sz > 0 else 0
                planes, places = pl.ds((8 if sz > 0 else 0) + skip, count), pl.ds(skip, count)
                u = part_of(sz)
                for v, low in ((0, 2), (1, 33)):
                    for i in range(6):
                        zx_out[k, u, v, 2 + 5 * i : 7 + 5 * i] = send[
                            k, (8 + i) if u else i, low : low + 5
                        ]
                    post(
                        zx_out.at[k, u, v], rzx.at[k, u, v, pl.ds(0, 32)], (sz, 2 * v - 1, 0)
                    )
                post(send.at[k, planes], rz.at[k, part_of(sz), places], (sz, 0, 0))
        for sx in (-1, 1):
            post(send.at[k, pl.ds(1, 15), row_tile(sx)], rx.at[k, part_of(sx)], (0, sx, 0))
        wait_rows(recvs.at[k], sum(rows))
        sent.append((sends.at[k], sum(rows)))

        def edge_rows(u, v, i):
            at = iota(0, (8, LANES))
            tile = rzx[k, u, v, 5 * i + v : 5 * i + v + 8]
            return jnp.where(between(at, 2 - v, 6 - v), tile, 0.0)

        new_p = []
        for own, d, offset, shift, y, low, high, outer_low, outer_high, ref in (
            (14, 1, 1, 0, y_pa, -2, 3, -3, 1, p_a),
            (15, 0, 4, 64, y_pb, -4, 1, -2, 2, p_b),
        ):
            here = add_tiles(
                z_sum(send[k, own], rz[k, 1, 5], rz[k, 0, 0], offset, shift),
                z_sum(rx[k, 1, own - 1], edge_rows(1, 1, 5), edge_rows(0, 1, 0), offset, shift),
                z_sum(rx[k, 0, own - 1], edge_rows(1, 0, 5), edge_rows(0, 0, 0), offset, shift),
            )
            other = beside(ry.at[k], rzy.at[k], rxy.at[k], d)
            value = jnp.where(between(y, low, high), here, 0.0) + jnp.where(
                between(y, outer_low, outer_high), other, 0.0
            )
            value = value * side_gain[1 - d]
            if k > 0:
                value = ref[MIDDLE] + value
            ref[MIDDLE] = value
            new_p.append(value)
        edges = jnp.where(between(y_pa, 0, 3), new_p[0], new_p[1])
        edge_lane = either(lane < 4, lane >= LANES - 4)
        for z in range(2, 12) if last_one else range(PLANES):
            solved = 1 <= z <= 12
            value = send[k, z] if solved else zero_plane
            first = rx[k, 1, z - 1] if solved else jnp.zeros((8, LANES), jnp.float32)
            last = rx[k, 0, z - 1] if solved else jnp.zeros((8, LANES), jnp.float32)
            if z <= 4:
                value = value + rz[k, 1, z]
                first = first + edge_rows(1, 1, z)
                last = last + edge_rows(1, 0, z)
            if z >= 9:
                value = value + rz[k, 0, z - 8]
                first = first + edge_rows(0, 1, z - 8)
                last = last + edge_rows(0, 0, z - 8)
            value = add_tiles(value, first, last) * (main_gain * z_gain(z))
            if k > 0:
                value = p_main[plane(z)] + value
            p_main[plane(z)] = jnp.where(edge_lane, roll(edges, -(STEP * z + 2)), value)

        total = zero_plane
        r_edges = (zero_plane, zero_plane)
        for z in range(3, 11) if last_one else range(1, 13):
            centre = p_main[plane(z)]
            value = r0_main[plane(z)] - alpha[plane(z)] * centre
            for i, other in enumerate(
                around(p_main, z) + (roll(centre, 1), roll(centre, -1))
            ):
                value = value + w_main[i, plane(z)] * other
            if not last_one:
                r_main[plane(z)] = value
                r_edges = gather(r_edges, z, value)
            if 3 <= z <= 10:
                value = value * scale[z - 3]
                total = total + value * value
        for i, (ref, r0, al, w_ref, r_ref, p) in enumerate(
            ((p_a, r0_a, alpha_a, w_a, r_a, new_p[0]), (p_b, r0_b, alpha_b, w_b, r_b, new_p[1]))
        ):
            value = r0[MIDDLE] - al[...] * p
            for n, other in enumerate(side_around(ref, p) + (roll(p, 1), roll(p, -1))):
                value = value + w_ref[n] * other
            if not last_one:
                r_ref[MIDDLE] = jnp.where(y_fa <= 0 if i == 0 else y_fb >= -1, value, r_edges[i])
            value = value * scale_side[i]
            total = total + value * value
        partials.append(total)

    for z in range(8):
        out_ref[z] = p_main[pl.ds(PAD + ROWS * (z + 3) + 4, 32)]

    at = iota(1, (1, LANES)) // 32
    mine = jnp.zeros((1, LANES), jnp.float32)
    for i, value in enumerate(partials):
        value = jnp.sum(value, axis=0, keepdims=True)
        value = value + roll(value, 64)
        mine = jnp.where(at == i, value + roll(value, 32), mine)
    pair = gy + 1 - 2 * lax.rem(gy, 2)

    def ring(i, n):
        return min(i, n - i)

    rounds = (
        sorted(
            ((i, h) for i in range(n_gx) for h in range(2) if (i, h) != (0, 0)),
            key=lambda t: -ring(t[0], n_gx) - 0.3 * t[1],
        ),
        sorted(
            ((i, h) for i in range(n_gy // 2) for h in range(n_gz) if (i, h) != (0, 0)),
            key=lambda t: -ring(t[0], n_gy // 2) - ring(t[1], n_gz),
        ),
    )
    rounds = (
        [(lax.rem(gx + i, n_gx), gy if h == 0 else pair, gz) for i, h in rounds[0]],
        [(gx, lax.rem(gy + 2 * i, n_gy), lax.rem(gz + h, n_gz)) for i, h in rounds[1]],
    )
    slots = (gx * 2 + lax.rem(gy, 2), (gy // 2) * n_gz + gz)
    for n, targets in enumerate(rounds):
        here = part_in.at[n, slots[n], pl.ds(0, 1)]
        part[n, 0:1] = mine
        for target in targets:
            pltpu.make_async_remote_copy(
                src_ref=part.at[n, pl.ds(0, 1)], dst_ref=here,
                send_sem=ar_send.at[n], recv_sem=ar_recv.at[n],
                device_id=target, device_id_type=MESH,
            ).start()
        here[...] = mine
        wait_rows(ar_recv.at[n], len(targets))
        sent.append((ar_send.at[n], len(targets)))
        terms = [part_in[n, i, 0:1] for i in range(len(targets) + 1)]
        while len(terms) > 1:
            terms = [sum(terms[i + 1 : i + 2], terms[i]) for i in range(0, len(terms), 2)]
        mine = terms[0]
    squares = [
        jnp.sum(jnp.where(at == i, mine, 0.0), axis=1, keepdims=True) for i in range(ITERS + 1)
    ]
    for i in range(ITERS):
        hist_ref[i] = jnp.sum(jnp.sqrt(squares[i + 1] / squares[0]))
    for sem, rows in sent:
        wait_rows(sem, rows)


def solution(mesh):
    sizes = (mesh.shape["gx"], mesh.shape["gy"], mesh.shape["gz"])
    f32 = jnp.float32

    def vmem(*shape):
        return pltpu.VMEM(shape, f32)

    scratch = [
        vmem(8, 32, LANES), vmem(8, 32, LANES), vmem(8, 32, LANES),
        pltpu.VMEM((32, LANES), jnp.int32),
        vmem(2, 8, 8, LANES), vmem(2, ROWS, LANES), vmem(2, 2, 16, LANES),
        vmem(2, 3, 32, LANES), vmem(2, 2, 32, LANES), vmem(2, 2, 32, LANES),
        vmem(2, 8, 8, LANES), vmem(2, 2, 3, 8, LANES),
        vmem(2, ROWS, LANES), vmem(2, 2, 16, LANES), vmem(3, 2, 2, 8, LANES),
        vmem(ITERS, 16, ROWS, LANES), vmem(ITERS, 2, 2, 32, LANES), vmem(ITERS, 2, 2, 16, LANES),
        vmem(ITERS, 2, 6, ROWS, LANES), vmem(ITERS, 2, 15, 8, LANES),
        vmem(ITERS, 2, 2, 40, LANES),
        vmem(ITERS, 2, ROWS, LANES), vmem(ITERS, 2, 2, 16, LANES), vmem(ITERS, 3, 2, 2, 8, LANES),
        vmem(FLAT, LANES), vmem(SIDE, LANES), vmem(SIDE, LANES), vmem(FLAT, LANES), vmem(FLAT, LANES),
        vmem(6, FLAT, LANES), vmem(7, ROWS, LANES), vmem(7, ROWS, LANES),
        vmem(FLAT, LANES), vmem(ROWS, LANES), vmem(ROWS, LANES), vmem(8, ROWS, LANES),
    ]
    for _ in range(5):
        scratch += [vmem(FLAT, LANES), vmem(SIDE, LANES), vmem(SIDE, LANES)]
    scratch += [
        pltpu.VMEM((2 * LANES, 2 * LANES), jnp.bfloat16),
        vmem(2, 8, LANES), vmem(2, 16, 8, LANES),
        vmem(2048, LANES),
        pltpu.SemaphoreType.DMA, pltpu.SemaphoreType.DMA, pltpu.SemaphoreType.DMA,
        pltpu.SemaphoreType.DMA((ITERS,)), pltpu.SemaphoreType.DMA((ITERS,)),
        pltpu.SemaphoreType.DMA((2,)), pltpu.SemaphoreType.DMA((2,)),
    ]

    def per_device(source, permeability, storage, column_depth):
        return pl.pallas_call(
            functools.partial(kernel, sizes),
            out_shape=(
                jax.ShapeDtypeStruct(source.shape, f32),
                jax.ShapeDtypeStruct((ITERS,), f32),
            ),
            in_specs=[pl.BlockSpec(memory_space=pl.ANY)] * 4,
            out_specs=(
                pl.BlockSpec(memory_space=pltpu.VMEM),
                pl.BlockSpec(memory_space=pltpu.SMEM),
            ),
            scratch_shapes=scratch,
            compiler_params=pltpu.CompilerParams(
                collective_id=0, has_side_effects=True, vmem_limit_bytes=55056 * 2**10
            ),
            name="schwarz",
        )(source, permeability, storage, column_depth)

    placed = (P("gz", "gx", "gy"), P("gz", "gx", "gy"), P("gz", "gx", "gy"), P("gx", "gy"))
    return jax.shard_map(
        per_device,
        mesh=mesh,
        in_specs=placed,
        out_specs=(P("gz", "gx", "gy"), P()),
        check_vma=False,
    )
```

```python
import functools
import math

import jax
import jax.numpy as jnp
from jax import lax
from jax.experimental import pallas as pl
from jax.experimental.pallas import tpu as pltpu
from jax.sharding import PartitionSpec as P

MESH = pl.DeviceIdType.MESH
ITERS = 3
RELAX = 0.9

PLANES, ROWS, LANES, PAD, STEP = 14, 40, 128, 8, 9
FLAT = PLANES * ROWS + 2 * PAD
SIDE = ROWS + 2 * PAD
DIRS = tuple(
    (sz, sx, sy)
    for sz in (-1, 0, 1)
    for sx in (-1, 0, 1)
    for sy in (-1, 0, 1)
    if (sz, sx, sy) != (0, 0, 0)
)
DIRS = tuple(sorted(DIRS, key=lambda s: -(abs(s[0]) + abs(s[1]) + abs(s[2]))))


def plane(z, count=1):
    return pl.ds(PAD + ROWS * z, ROWS * count)


MIDDLE = pl.ds(PAD, ROWS)


def iota(axis, shape=(ROWS, LANES)):
    return lax.broadcasted_iota(jnp.int32, shape, axis)


def roll(x, shift):
    return pltpu.roll(x, shift % LANES, axis=x.ndim - 1)


def both(*flags):
    return functools.reduce(jnp.logical_and, flags)


def either(*flags):
    return functools.reduce(jnp.logical_or, flags)


def between(x, low, high):
    return both(x >= low, x <= high)


def lanes_between(lane, low, high):
    if low < 0:
        return either(lane >= low + LANES, lane <= high)
    return between(lane, low, high)


def classes(shape, offset):
    u = lax.rem(iota(1, shape) + offset, LANES)
    z = (u * 57) >> 9
    return z, u - STEP * z


def strip(sx):
    return pl.ds(1 if sx > 0 else 2, 5)


def add_tiles(acc, first, last):
    return jnp.concatenate([acc[:8] + first, acc[8 : ROWS - 8], acc[ROWS - 8 :] + last], axis=0)


WIDTH = 43


def fold(side, first):
    t = [side[8 * i : 8 * i + 8] for i in range(5)]
    at = lax.rem(iota(1, (8, LANES)) + (LANES - first), LANES)
    one = jnp.where(
        at < WIDTH, t[0], jnp.where(at < 2 * WIDTH, roll(t[1], WIDTH), roll(t[2], 2 * WIDTH))
    )
    two = jnp.where(at < WIDTH, t[3], roll(t[4], WIDTH))
    return jnp.concatenate([one, two], axis=0)


def unfold(both_tiles, shift):
    return jnp.concatenate(
        [roll(both_tiles[8 * (i // 3) : 8 * (i // 3) + 8], shift - WIDTH * (i % 3)) for i in range(5)],
        axis=0,
    )


def part_of(v):
    return (v + 1) // 2


def kernel(
    sizes, src_hbm, perm_hbm, stor_hbm, depth_hbm, out_ref, hist_ref,
    in_src, in_perm, in_stor, in_depth,
    own_rows, own_side, own_fold, rz_k, rz_s, rz_q, rx0, rzx0, ry0, rzy0, rxy0,
    send, zx_out, fold_out, rz, rx, rzx, ry, rzy, rxy,
    k_main, k_a, k_b, s_main, q_main,
    w_main, w_a, w_b, alpha, alpha_a, alpha_b, scale,
    r0_main, r0_a, r0_b, r_main, r_a, r_b, u_main, u_a, u_b, v_main, v_a, v_b, p_main, p_a, p_b,
    shifter, part, part_in, tally,
    load_sem, send0, recv0, sends, recvs, ar_send, ar_recv,
):
    n_gx, n_gy, n_gz = sizes
    gx, gy, gz = lax.axis_index("gx"), lax.axis_index("gy"), lax.axis_index("gz")

    def device(s):
        return (
            lax.rem(gx + s[1] + n_gx, n_gx),
            lax.rem(gy + s[2] + n_gy, n_gy),
            lax.rem(gz + s[0] + n_gz, n_gz),
        )

    def wait_rows(sem, rows):
        span = tally.at[pl.ds(0, rows)]
        pltpu.make_async_copy(span, span, sem).wait()

    def rows_of(ref):
        return math.prod(ref.shape[:-1])

    rxy0[...] = jnp.zeros(rxy0.shape, jnp.float32)
    barrier = pltpu.get_barrier_semaphore()
    for s in DIRS:
        pl.semaphore_signal(barrier, inc=1, device_id=device(s), device_id_type=MESH)

    loads = [
        pltpu.make_async_copy(a, b, load_sem)
        for a, b in (
            (depth_hbm, in_depth), (perm_hbm, in_perm), (stor_hbm, in_stor), (src_hbm, in_src)
        )
    ]
    for copy in loads:
        copy.start()

    zero_plane = jnp.zeros((ROWS, LANES), jnp.float32)
    for ref in (rz, rxy, rx):
        ref[...] = jnp.zeros(ref.shape, jnp.float32)
    own_rows[...] = jnp.zeros(own_rows.shape, jnp.float32)
    own_side[...] = jnp.zeros(own_side.shape, jnp.float32)
    for ref in (k_main, s_main, q_main):
        ref[...] = jnp.zeros((FLAT, LANES), jnp.float32)
    for ref in (r0_main, r_main, u_main, v_main, p_main):
        ref[0 : PAD + ROWS] = jnp.zeros((PAD + ROWS, LANES), jnp.float32)
        ref[FLAT - PAD - ROWS :] = jnp.zeros((PAD + ROWS, LANES), jnp.float32)
    for ref in (k_a, k_b, r0_a, r0_b, r_a, r_b, u_a, u_b, v_a, v_b, p_a, p_b):
        ref[...] = jnp.zeros((SIDE, LANES), jnp.float32)

    at_in, at_out = iota(0, (2 * LANES, 2 * LANES)), iota(1, (2 * LANES, 2 * LANES))
    from_lane = lax.rem(at_out + jnp.where(at_out < LANES, LANES - 1, 1), LANES)
    shifter[...] = jnp.where(lax.rem(at_in, LANES) == from_lane, 1.0, 0.0).astype(jnp.bfloat16)

    lane, row = iota(1), iota(0)
    x = row - 4
    z_fa, y_fa = classes((ROWS, LANES), 0)
    z_fb, y_fb = classes((ROWS, LANES), 5)
    z_pa, y_pa = classes((ROWS, LANES), 1)
    z_pb, y_pb = classes((ROWS, LANES), 4)
    y_fa, y_fb, y_pa, y_pb = y_fa - 2, y_fb - 7, y_pa - 3, y_pb - 6

    def gather(accs, z, value):
        at = iota(1, value.shape)
        moved = roll(value, STEP * z + 2)
        return (
            jnp.where(lanes_between(at, STEP * z + 2, STEP * z + 8), moved, accs[0]),
            jnp.where(lanes_between(at, STEP * z - 5, STEP * z + 1), moved, accs[1]),
        )

    wait_rows(load_sem, 3 * 8 * 32 + 32)

    depth = in_depth[...]
    for z in range(8):
        in_perm[z] = jnp.where((gz * 8 + z) < depth, in_perm[z], 0.0)

    pl.semaphore_wait(barrier, len(DIRS))

    rows0 = []

    def post0(src, dst, s):
        pltpu.make_async_remote_copy(
            src_ref=src, dst_ref=dst, send_sem=send0, recv_sem=recv0,
            device_id=device(s), device_id_type=MESH,
        ).start()
        rows0.append(rows_of(src))

    for sz in (-1, 1):
        u = part_of(sz)
        post0(in_perm.at[pl.ds(5 * u, 3)], rz_k.at[u], (sz, 0, 0))
        post0(in_stor.at[pl.ds(6 * u, 2)], rz_s.at[u], (sz, 0, 0))
        post0(in_src.at[pl.ds(6 * u, 2)], rz_q.at[u], (sz, 0, 0))
    zero_block = jnp.zeros((32, LANES), jnp.float32)
    edges = [(zero_block, zero_block)] * 3
    for z in range(8):
        for f, ref in enumerate((in_perm, in_stor, in_src)):
            edges[f] = gather(edges[f], z + 3, ref[z])
        for v, low in ((0, 0), (1, 29)):
            own_rows[v, z, 0:3] = in_perm[z, low : low + 3]
            for i, ref in ((3, in_stor), (5, in_src)):
                own_rows[v, z, i : i + 2] = ref[z, low + v : low + v + 2]
    _, c = classes((32, LANES), 4)
    own_side[0, 4:36] = jnp.where(
        c >= 6, edges[0][0], jnp.where(c >= 3, roll(edges[1][0], -3), roll(edges[2][0], -6))
    )
    _, c = classes((32, LANES), 1)
    own_side[1, 4:36] = jnp.where(
        c < 3, edges[0][1], jnp.where(c < 6, roll(edges[1][1], 3), roll(edges[2][1], 6))
    )
    for d in range(2):
        for u in range(2):
            own_fold[u, d] = fold(own_side[d], STEP * (8 if u else 3) - (1 if d else 4))
    for s in DIRS:
        sz, sx, sy = s
        u, v, d = part_of(sz), part_of(sx), part_of(sy)
        if sy == 0:
            if sz == 0:
                post0(own_rows.at[v, :, pl.ds(0, 7)], rx0.at[v, :, pl.ds(0, 7)], s)
            elif sx != 0:
                post0(
                    own_rows.at[v, pl.ds(5 * u, 3), pl.ds(0, 7)],
                    rzx0.at[u, v, :, pl.ds(0, 7)], s,
                )
        elif sx != 0:
            post0(
                own_side.at[d, pl.ds(33 if v else 4, 3)],
                rxy0.at[sz + 1, v, d, pl.ds(1 if v else 4, 3)], s,
            )
        elif sz != 0:
            post0(own_fold.at[u, d], rzy0.at[u, d], s)
        else:
            post0(own_side.at[d], ry0.at[d], s)
    wait_rows(recv0, sum(rows0))

    def inside(flag):
        return flag.astype(jnp.float32)

    below, above = inside(gz > 0), inside(gz < n_gz - 1)
    before, after = inside(gx > 0), inside(gx < n_gx - 1)
    in_z = {z: below if z < 3 else above for z in (0, 1, 2, 11, 12, 13)}
    for z in range(PLANES):
        base = PAD + ROWS * z
        if 3 <= z <= 10:
            middle = in_perm[z - 3]
            low, high = rx0[1, z - 3], rx0[0, z - 3]
            gain = 1.0
            s_main[base + 4 : base + 36] = in_stor[z - 3]
            q_main[base + 4 : base + 36] = in_src[z - 3]
        else:
            u, i = (1, z) if z < 3 else (0, z - 11)
            middle = rz_k[u, i] * in_z[z]
            low, high = rzx0[u, 1, i], rzx0[u, 0, i]
            gain = in_z[z]
            if 1 <= z <= 12:
                i = z - 1 if z < 3 else z - 11
                s_main[base + 4 : base + 36] = rz_s[u, i]
                q_main[base + 4 : base + 36] = rz_q[u, i]
        k_main[base + 4 : base + 36] = middle
        k_main[base + 1 : base + 4] = low[0:3] * (before * gain)
        k_main[base + 36 : base + 39] = high[0:3] * (after * gain)
        s_main[base + 2 : base + 4] = low[3:5]
        s_main[base + 36 : base + 38] = high[3:5]
        q_main[base + 2 : base + 4] = low[5:7]
        q_main[base + 36 : base + 38] = high[5:7]

    def z_sum(here, lower, upper, offset, shift=0, move=roll, reach=5):
        z, _ = classes(here.shape, offset)
        moved = jnp.where(
            z < reach, move(lower, -8 * STEP - shift),
            jnp.where(between(z, 14 - reach, 13), move(upper, 8 * STEP + shift), 0.0),
        )
        return here + moved

    def beside(y, zy, xy, d, reach=5):
        offset = 1 if d else 4
        return add_tiles(
            z_sum(y[d], zy[1, d], zy[0, d], offset, move=unfold, reach=reach),
            z_sum(xy[1, 1, d], xy[2, 1, d], xy[0, 1, d], offset, reach=reach),
            z_sum(xy[1, 0, d], xy[2, 0, d], xy[0, 0, d], offset, reach=reach),
        )

    from_left, from_right = (beside(ry0, rzy0, rxy0, d, 3) for d in (1, 0))

    def grid_z(z):
        return both(either(z >= 3, gz > 0), either(z <= 10, gz < n_gz - 1))

    row_in = both(either(x >= 0, gx > 0), either(x < 32, gx < n_gx - 1))
    gain_a = jnp.where(both(row_in, grid_z(z_pa), gy > 0), 1.0, 0.0)
    gain_b = jnp.where(both(row_in, grid_z(z_pb), gy < n_gy - 1), 1.0, 0.0)
    k_edges, s_edges, q_edges = ((zero_plane, zero_plane) for _ in range(3))
    for z in range(PLANES):
        k_edges = gather(k_edges, z, k_main[plane(z)])
        if 1 <= z <= 12:
            s_edges = gather(s_edges, z, s_main[plane(z)])
            q_edges = gather(q_edges, z, q_main[plane(z)])
    k_left, k_right = from_left * gain_a, from_right * gain_b
    k_fa = jnp.where(both(y_pa >= -2, y_pa <= -1), k_left, k_edges[0])
    k_fb = jnp.where(both(y_pb >= 0, y_pb <= 1), k_right, k_edges[1])
    k_pa = jnp.where(y_pa == -3, k_left, k_fa)
    k_pb = jnp.where(y_pb == 2, k_right, k_fb)
    k_a[MIDDLE] = k_fa
    k_b[MIDDLE] = k_fb
    s_a = jnp.where(both(y_pa >= -2, y_pa <= -1), roll(from_left, -3), s_edges[0])
    q_a = jnp.where(both(y_pa >= -2, y_pa <= -1), roll(from_left, -6), q_edges[0])
    s_b = jnp.where(both(y_pb >= 0, y_pb <= 1), roll(from_right, 3), s_edges[1])
    q_b = jnp.where(both(y_pb >= 0, y_pb <= 1), roll(from_right, 6), q_edges[1])

    def weights(centre, others, storage, source, keep):
        idle = jnp.where(centre > 0.0, 0.0, 1.0)
        diagonal = storage + idle
        couplings = []
        for other in others:
            other_idle = jnp.where(other > 0.0, 0.0, 1.0)
            c = (2.0 * centre) * other / ((centre + idle) + (other + other_idle))
            couplings.append(c)
            diagonal = diagonal + c
        gain = jnp.where(keep, RELAX / diagonal, 0.0)
        live = jnp.where(keep, 1.0 - idle, 0.0)
        return [c * gain for c in couplings], live * gain * source, live * RELAX, diagonal

    def around(ref, z, count=1):
        base, rows = PAD + ROWS * z, ROWS * count
        return (
            ref[pl.ds(base - ROWS, rows)],
            ref[pl.ds(base + ROWS, rows)],
            ref[pl.ds(base - 1, rows)],
            ref[pl.ds(base + 1, rows)],
        )

    def side_around(ref, centre):
        return (
            roll(centre, STEP), roll(centre, -STEP), ref[pl.ds(PAD - 1, ROWS)], ref[pl.ds(PAD + 1, ROWS)],
        )

    rows_kept, rows_own = between(row, 2, 37), between(row, 4, 35)
    inner = both(lane > 0, lane < LANES - 1)
    total = zero_plane
    r_edges = (zero_plane, zero_plane)
    for z in range(1, 13):
        centre = k_main[plane(z)]
        ws, r, al, diagonal = weights(
            centre, around(k_main, z) + (roll(centre, 1), roll(centre, -1)),
            s_main[plane(z)], q_main[plane(z)], rows_kept,
        )
        for i in range(6):
            w_main[i, plane(z)] = ws[i]
        alpha[plane(z)] = al
        r0_main[plane(z)] = r
        r_edges = gather(r_edges, z, r)
        if 3 <= z <= 10:
            sc = jnp.where(both(rows_own, inner), diagonal * (1.0 / RELAX), 0.0)
            scale[z - 3] = sc
            total = total + (r * sc) * (r * sc)
    scale_side = []
    for ref, k_f, left, right, st, q, z, y, low, high, w_ref, al_ref, r_ref, edge, own in (
        (k_a, k_fa, k_pa, k_fa, s_a, q_a, z_fa, y_fa, -2, 5, w_a, alpha_a, r0_a, r_edges[0], 0),
        (k_b, k_fb, k_fb, k_pb, s_b, q_b, z_fb, y_fb, -6, 1, w_b, alpha_b, r0_b, r_edges[1], -1),
    ):
        keep = both(rows_kept, between(z, 1, 12), between(y, low, high))
        ws, r, al, diagonal = weights(
            k_f, side_around(ref, k_f) + (roll(left, 1), roll(right, -1)), st, q, keep
        )
        for i in range(6):
            w_ref[i] = ws[i]
        if low == -2:
            w_ref[6] = jnp.where(y == -2, 0.0, ws[4])
        else:
            w_ref[6] = jnp.where(y == 1, 0.0, ws[5])
        al_ref[...] = al
        r_ref[MIDDLE] = jnp.where(y <= 0 if low == -2 else y >= -1, r, edge)
        sc = jnp.where(
            both(rows_own, between(z, 3, 10), y == own), diagonal * (1.0 / RELAX), 0.0
        )
        scale_side.append(sc)
        total = total + (r * sc) * (r * sc)

    def half(flag):
        return jnp.where(flag, 0.5, 1.0)

    def axis_gain(position, extent, owner, owners):
        inner_low = both(position >= 0, position < 2, owner > 0)
        inner_high = both(position >= extent - 2, position < extent, owner < owners - 1)
        outer = either(
            both(position >= -2, position < 0), both(position >= extent, position < extent + 2)
        )
        return half(either(outer, inner_low, inner_high))

    x_gain = axis_gain(x, 32, gx, n_gx)
    main_gain = x_gain * axis_gain(lane, 128, gy, n_gy)
    side_gain = (
        x_gain * axis_gain(z_pa - 3, 8, gz, n_gz) * axis_gain(y_pa, 128, gy, n_gy),
        x_gain * axis_gain(z_pb - 3, 8, gz, n_gz) * axis_gain(y_pb + 128, 128, gy, n_gy),
    )

    def z_gain(z):
        if z in (0, 13):
            return 1.0
        if z in (1, 2, 11, 12):
            return 0.5
        if z in (3, 4):
            return jnp.where(gz > 0, 0.5, 1.0)
        if z in (9, 10):
            return jnp.where(gz < n_gz - 1, 0.5, 1.0)
        return 1.0

    def side_sweep(ref, rhs, w_ref, last):
        value = ref[MIDDLE]
        others = side_around(ref, value) + (roll(value, 1), roll(value, -1))
        value = (1.0 - RELAX) * value + rhs[MIDDLE]
        for i, other in enumerate(others):
            value = value + w_ref[6 if i == last else i] * other
        return value

    def main_sweep(ref, rhs, z):
        value = ref[plane(z, 2)]
        hi = value.astype(jnp.bfloat16)
        lo = (value - hi.astype(jnp.float32)).astype(jnp.bfloat16)
        beside_y = jnp.dot(
            jnp.concatenate([hi, lo], axis=1), shifter[...], preferred_element_type=jnp.float32
        )
        others = around(ref, z, 2) + (beside_y[:, :LANES], beside_y[:, LANES:])
        value = (1.0 - RELAX) * value + rhs[plane(z, 2)]
        for i, other in enumerate(others):
            value = value + w_main[i, plane(z, 2)] * other
        return value

    partials = [total]
    sent = [(send0, sum(rows0))]
    for k in range(ITERS):
        rhs, rhs_a, rhs_b = (r0_main, r0_a, r0_b) if k == 0 else (r_main, r_a, r_b)
        rows = []
        last_one = k == ITERS - 1

        def post(source, target, s):
            pltpu.make_async_remote_copy(
                src_ref=source, dst_ref=target, send_sem=sends.at[k], recv_sem=recvs.at[k],
                device_id=device(s), device_id_type=MESH,
            ).start()
            rows.append(rows_of(source))

        for before_ref, after_ref in (((rhs_a, rhs_b), (u_a, u_b)), ((u_a, u_b), (v_a, v_b))):
            after_ref[0][MIDDLE] = side_sweep(before_ref[0], rhs_a, w_a, 4)
            after_ref[1][MIDDLE] = side_sweep(before_ref[1], rhs_b, w_b, 5)
        side_a = side_sweep(v_a, rhs_a, w_a, 4)
        side_b = side_sweep(v_b, rhs_b, w_b, 5)
        far_b = roll(side_b, 64)
        send[k, 0] = jnp.where(lane < 60, side_a, far_b)
        send[k, 13] = jnp.where(lane < 60, far_b, side_a)
        send[k, 14] = side_a
        send[k, 15] = side_b
        for d, value in ((0, side_a), (1, side_b)):
            for u in range(2):
                fold_out[k, u, d] = fold(value, STEP * (8 if u else 1) - d)
        for s in DIRS:
            sz, sx, sy = s
            u, v, d = part_of(sz), part_of(sx), part_of(sy)
            if sy != 0:
                if sx != 0:
                    post(
                        send.at[k, 14 + d, pl.ds(33 if v else 2, 5)],
                        rxy.at[k, sz + 1, v, d, strip(sx)], s,
                    )
                elif sz != 0:
                    post(fold_out.at[k, u, d], rzy.at[k, u, d], s)
                else:
                    post(send.at[k, 14 + d], ry.at[k, d], s)

        for z in range(1, 13, 2):
            u_main[plane(z, 2)] = main_sweep(rhs, rhs, z)
        for z in range(1, 13, 2):
            v_main[plane(z, 2)] = main_sweep(u_main, rhs, z)
        for z in (1, 3, 5, 11, 9, 7):
            value = main_sweep(v_main, rhs, z)
            send[k, z] = value[:ROWS]
            send[k, z + 1] = value[ROWS:]
            if z in (5, 7):
                sz = -1 if z == 5 else 1
                count = 4 if last_one else 6
                skip = 6 - count if sz > 0 else 0
                planes, places = pl.ds((8 if sz > 0 else 0) + skip, count), pl.ds(skip, count)
                u = part_of(sz)
                pieces = pl.ds(2 + 5 * skip, 5 * count)
                for v, low in ((0, 2), (1, 33)):
                    for i in range(skip, skip + count):
                        zx_out[k, u, v, 2 + 5 * i : 7 + 5 * i] = send[
                            k, (8 + i) if u else i, low : low + 5
                        ]
                    post(
                        zx_out.at[k, u, v, pieces], rzx.at[k, u, v, pieces],
                        (sz, 2 * v - 1, 0),
                    )
                kept = pl.ds(2, 36)
                post(send.at[k, planes, kept], rz.at[k, u, places, kept], (sz, 0, 0))
        for sx in (-1, 1):
            v = part_of(sx)
            post(
                send.at[k, pl.ds(1, 15), pl.ds(33 if v else 2, 5)],
                rx.at[k, v, :, strip(sx)], (0, sx, 0),
            )
        wait_rows(recvs.at[k], sum(rows))
        sent.append((sends.at[k], sum(rows)))

        def edge_rows(u, v, i):
            at = iota(0, (8, LANES))
            tile = rzx[k, u, v, 5 * i + v : 5 * i + v + 8]
            return jnp.where(between(at, 2 - v, 6 - v), tile, 0.0)

        new_p = []
        for own, d, offset, shift, y, low, high, outer_low, outer_high, ref in (
            (14, 1, 1, 0, y_pa, -2, 3, -3, 1, p_a),
            (15, 0, 4, 64, y_pb, -4, 1, -2, 2, p_b),
        ):
            here = add_tiles(
                z_sum(send[k, own], rz[k, 1, 5], rz[k, 0, 0], offset, shift),
                z_sum(rx[k, 1, own - 1], edge_rows(1, 1, 5), edge_rows(0, 1, 0), offset, shift),
                z_sum(rx[k, 0, own - 1], edge_rows(1, 0, 5), edge_rows(0, 0, 0), offset, shift),
            )
            other = beside(ry.at[k], rzy.at[k], rxy.at[k], d)
            value = jnp.where(between(y, low, high), here, 0.0) + jnp.where(
                between(y, outer_low, outer_high), other, 0.0
            )
            value = value * side_gain[1 - d]
            if k > 0:
                value = ref[MIDDLE] + value
            ref[MIDDLE] = value
            new_p.append(value)
        edges = jnp.where(between(y_pa, 0, 3), new_p[0], new_p[1])
        edge_lane = either(lane < 4, lane >= LANES - 4)
        for z in range(2, 12) if last_one else range(PLANES):
            solved = 1 <= z <= 12
            value = send[k, z] if solved else zero_plane
            first = rx[k, 1, z - 1] if solved else jnp.zeros((8, LANES), jnp.float32)
            last = rx[k, 0, z - 1] if solved else jnp.zeros((8, LANES), jnp.float32)
            if z <= 4:
                value = value + rz[k, 1, z]
                first = first + edge_rows(1, 1, z)
                last = last + edge_rows(1, 0, z)
            if z >= 9:
                value = value + rz[k, 0, z - 8]
                first = first + edge_rows(0, 1, z - 8)
                last = last + edge_rows(0, 0, z - 8)
            value = add_tiles(value, first, last) * (main_gain * z_gain(z))
            if k > 0:
                value = p_main[plane(z)] + value
            p_main[plane(z)] = jnp.where(edge_lane, roll(edges, -(STEP * z + 2)), value)

        total = zero_plane
        r_edges = (zero_plane, zero_plane)
        for z in range(3, 11) if last_one else range(1, 13):
            centre = p_main[plane(z)]
            value = r0_main[plane(z)] - alpha[plane(z)] * centre
            for i, other in enumerate(
                around(p_main, z) + (roll(centre, 1), roll(centre, -1))
            ):
                value = value + w_main[i, plane(z)] * other
            if not last_one:
                r_main[plane(z)] = value
                r_edges = gather(r_edges, z, value)
            if 3 <= z <= 10:
                value = value * scale[z - 3]
                total = total + value * value
        for i, (ref, r0, al, w_ref, r_ref, p) in enumerate(
            ((p_a, r0_a, alpha_a, w_a, r_a, new_p[0]), (p_b, r0_b, alpha_b, w_b, r_b, new_p[1]))
        ):
            value = r0[MIDDLE] - al[...] * p
            for n, other in enumerate(side_around(ref, p) + (roll(p, 1), roll(p, -1))):
                value = value + w_ref[n] * other
            if not last_one:
                r_ref[MIDDLE] = jnp.where(y_fa <= 0 if i == 0 else y_fb >= -1, value, r_edges[i])
            value = value * scale_side[i]
            total = total + value * value
        partials.append(total)

    for z in range(8):
        out_ref[z] = p_main[pl.ds(PAD + ROWS * (z + 3) + 4, 32)]

    at = iota(1, (1, LANES)) // 32
    mine = jnp.zeros((1, LANES), jnp.float32)
    for i, value in enumerate(partials):
        value = jnp.sum(value, axis=0, keepdims=True)
        value = value + roll(value, 64)
        mine = jnp.where(at == i, value + roll(value, 32), mine)
    pair = gy + 1 - 2 * lax.rem(gy, 2)

    def ring(i, n):
        return min(i, n - i)

    rounds = (
        sorted(
            ((i, h) for i in range(n_gx) for h in range(2) if (i, h) != (0, 0)),
            key=lambda t: -ring(t[0], n_gx) - 0.3 * t[1],
        ),
        sorted(
            ((i, h) for i in range(n_gy // 2) for h in range(n_gz) if (i, h) != (0, 0)),
            key=lambda t: -ring(t[0], n_gy // 2) - ring(t[1], n_gz),
        ),
    )
    rounds = (
        [(lax.rem(gx + i, n_gx), gy if h == 0 else pair, gz) for i, h in rounds[0]],
        [(gx, lax.rem(gy + 2 * i, n_gy), lax.rem(gz + h, n_gz)) for i, h in rounds[1]],
    )
    slots = (gx * 2 + lax.rem(gy, 2), (gy // 2) * n_gz + gz)
    for n, targets in enumerate(rounds):
        here = part_in.at[n, slots[n], pl.ds(0, 1)]
        part[n, 0:1] = mine
        for target in targets:
            pltpu.make_async_remote_copy(
                src_ref=part.at[n, pl.ds(0, 1)], dst_ref=here,
                send_sem=ar_send.at[n], recv_sem=ar_recv.at[n],
                device_id=target, device_id_type=MESH,
            ).start()
        here[...] = mine
        wait_rows(ar_recv.at[n], len(targets))
        sent.append((ar_send.at[n], len(targets)))
        terms = [part_in[n, i, 0:1] for i in range(len(targets) + 1)]
        while len(terms) > 1:
            terms = [sum(terms[i + 1 : i + 2], terms[i]) for i in range(0, len(terms), 2)]
        mine = terms[0]
    squares = [
        jnp.sum(jnp.where(at == i, mine, 0.0), axis=1, keepdims=True) for i in range(ITERS + 1)
    ]
    for i in range(ITERS):
        hist_ref[i] = jnp.sum(jnp.sqrt(squares[i + 1] / squares[0]))
    for sem, rows in sent:
        wait_rows(sem, rows)


def solution(mesh):
    sizes = (mesh.shape["gx"], mesh.shape["gy"], mesh.shape["gz"])
    f32 = jnp.float32

    def vmem(*shape):
        return pltpu.VMEM(shape, f32)

    scratch = [
        vmem(8, 32, LANES), vmem(8, 32, LANES), vmem(8, 32, LANES),
        pltpu.VMEM((32, LANES), jnp.int32),
        vmem(2, 8, 8, LANES), vmem(2, ROWS, LANES), vmem(2, 2, 16, LANES),
        vmem(2, 3, 32, LANES), vmem(2, 2, 32, LANES), vmem(2, 2, 32, LANES),
        vmem(2, 8, 8, LANES), vmem(2, 2, 3, 8, LANES),
        vmem(2, ROWS, LANES), vmem(2, 2, 16, LANES), vmem(3, 2, 2, 8, LANES),
        vmem(ITERS, 16, ROWS, LANES), vmem(ITERS, 2, 2, 32, LANES), vmem(ITERS, 2, 2, 16, LANES),
        vmem(ITERS, 2, 6, ROWS, LANES), vmem(ITERS, 2, 15, 8, LANES),
        vmem(ITERS, 2, 2, 40, LANES),
        vmem(ITERS, 2, ROWS, LANES), vmem(ITERS, 2, 2, 16, LANES), vmem(ITERS, 3, 2, 2, 8, LANES),
        vmem(FLAT, LANES), vmem(SIDE, LANES), vmem(SIDE, LANES), vmem(FLAT, LANES), vmem(FLAT, LANES),
        vmem(6, FLAT, LANES), vmem(7, ROWS, LANES), vmem(7, ROWS, LANES),
        vmem(FLAT, LANES), vmem(ROWS, LANES), vmem(ROWS, LANES), vmem(8, ROWS, LANES),
    ]
    for _ in range(5):
        scratch += [vmem(FLAT, LANES), vmem(SIDE, LANES), vmem(SIDE, LANES)]
    scratch += [
        pltpu.VMEM((2 * LANES, 2 * LANES), jnp.bfloat16),
        vmem(2, 8, LANES), vmem(2, 16, 8, LANES),
        vmem(2048, LANES),
        pltpu.SemaphoreType.DMA, pltpu.SemaphoreType.DMA, pltpu.SemaphoreType.DMA,
        pltpu.SemaphoreType.DMA((ITERS,)), pltpu.SemaphoreType.DMA((ITERS,)),
        pltpu.SemaphoreType.DMA((2,)), pltpu.SemaphoreType.DMA((2,)),
    ]

    def per_device(source, permeability, storage, column_depth):
        return pl.pallas_call(
            functools.partial(kernel, sizes),
            out_shape=(
                jax.ShapeDtypeStruct(source.shape, f32),
                jax.ShapeDtypeStruct((ITERS,), f32),
            ),
            in_specs=[pl.BlockSpec(memory_space=pl.ANY)] * 4,
            out_specs=(
                pl.BlockSpec(memory_space=pltpu.VMEM),
                pl.BlockSpec(memory_space=pltpu.SMEM),
            ),
            scratch_shapes=scratch,
            compiler_params=pltpu.CompilerParams(
                collective_id=0, has_side_effects=True, vmem_limit_bytes=55056 * 2**10
            ),
            name="schwarz",
        )(source, permeability, storage, column_depth)

    placed = (P("gz", "gx", "gy"), P("gz", "gx", "gy"), P("gz", "gx", "gy"), P("gx", "gy"))
    return jax.shard_map(
        per_device,
        mesh=mesh,
        in_specs=placed,
        out_specs=(P("gz", "gx", "gy"), P()),
        check_vma=False,
    )
```

```python
import functools
import math

import jax
import jax.numpy as jnp
from jax import lax
from jax.experimental import pallas as pl
from jax.experimental.pallas import tpu as pltpu
from jax.sharding import PartitionSpec as P

MESH = pl.DeviceIdType.MESH
ITERS = 3
RELAX = 0.9

PLANES, ROWS, LANES, PAD, STEP = 14, 40, 128, 8, 9
FLAT = PLANES * ROWS + 2 * PAD
SIDE = ROWS + 2 * PAD
DIRS = tuple(
    (sz, sx, sy)
    for sz in (-1, 0, 1)
    for sx in (-1, 0, 1)
    for sy in (-1, 0, 1)
    if (sz, sx, sy) != (0, 0, 0)
)
DIRS = tuple(sorted(DIRS, key=lambda s: -(abs(s[0]) + abs(s[1]) + abs(s[2]))))


def plane(z, count=1):
    return pl.ds(PAD + ROWS * z, ROWS * count)


MIDDLE = pl.ds(PAD, ROWS)


def iota(axis, shape=(ROWS, LANES)):
    return lax.broadcasted_iota(jnp.int32, shape, axis)


def roll(x, shift):
    return pltpu.roll(x, shift % LANES, axis=x.ndim - 1)


def both(*flags):
    return functools.reduce(jnp.logical_and, flags)


def either(*flags):
    return functools.reduce(jnp.logical_or, flags)


def between(x, low, high):
    return both(x >= low, x <= high)


def lanes_between(lane, low, high):
    if low < 0:
        return either(lane >= low + LANES, lane <= high)
    return between(lane, low, high)


def classes(shape, offset):
    u = lax.rem(iota(1, shape) + offset, LANES)
    z = (u * 57) >> 9
    return z, u - STEP * z


def strip(sx):
    return pl.ds(1 if sx > 0 else 2, 5)


def add_tiles(acc, first, last):
    return jnp.concatenate([acc[:8] + first, acc[8 : ROWS - 8], acc[ROWS - 8 :] + last], axis=0)


WIDTH = 43


def fold(side, first):
    t = [side[8 * i : 8 * i + 8] for i in range(5)]
    at = lax.rem(iota(1, (8, LANES)) + (LANES - first), LANES)
    one = jnp.where(
        at < WIDTH, t[0], jnp.where(at < 2 * WIDTH, roll(t[1], WIDTH), roll(t[2], 2 * WIDTH))
    )
    two = jnp.where(at < WIDTH, t[3], roll(t[4], WIDTH))
    return jnp.concatenate([one, two], axis=0)


def unfold(both_tiles, shift):
    return jnp.concatenate(
        [roll(both_tiles[8 * (i // 3) : 8 * (i // 3) + 8], shift - WIDTH * (i % 3)) for i in range(5)],
        axis=0,
    )


def part_of(v):
    return (v + 1) // 2


def kernel(
    sizes, src_hbm, perm_hbm, stor_hbm, depth_hbm, out_ref, hist_ref,
    in_src, in_perm, in_stor, in_depth,
    own_rows, own_side, own_fold, rz_k, rz_s, rz_q, rx0, rzx0, ry0, rzy0, rxy0,
    send, zx_out, fold_out, rz, rx, rzx, ry, rzy, rxy,
    k_main, k_a, k_b, s_main, q_main,
    w_main, w_a, w_b, alpha, alpha_a, alpha_b, scale,
    r0_main, r0_a, r0_b, r_main, r_a, r_b, u_main, u_a, u_b, v_main, v_a, v_b, p_main, p_a, p_b,
    shifter, part, part_in, tally,
    load_sem, send0, recv0, sends, recvs, ar_send, ar_recv,
):
    n_gx, n_gy, n_gz = sizes
    gx, gy, gz = lax.axis_index("gx"), lax.axis_index("gy"), lax.axis_index("gz")

    def device(s):
        return (
            lax.rem(gx + s[1] + n_gx, n_gx),
            lax.rem(gy + s[2] + n_gy, n_gy),
            lax.rem(gz + s[0] + n_gz, n_gz),
        )

    def wait_rows(sem, rows):
        span = tally.at[pl.ds(0, rows)]
        pltpu.make_async_copy(span, span, sem).wait()

    def rows_of(ref):
        return math.prod(ref.shape[:-1])

    rxy0[...] = jnp.zeros(rxy0.shape, jnp.float32)
    barrier = pltpu.get_barrier_semaphore()
    for s in DIRS:
        pl.semaphore_signal(barrier, inc=1, device_id=device(s), device_id_type=MESH)

    loads = [
        pltpu.make_async_copy(a, b, load_sem)
        for a, b in (
            (depth_hbm, in_depth), (perm_hbm, in_perm), (stor_hbm, in_stor), (src_hbm, in_src)
        )
    ]
    for copy in loads:
        copy.start()

    zero_plane = jnp.zeros((ROWS, LANES), jnp.float32)
    for ref in (rz, rxy, rx):
        ref[...] = jnp.zeros(ref.shape, jnp.float32)
    own_rows[...] = jnp.zeros(own_rows.shape, jnp.float32)
    own_side[...] = jnp.zeros(own_side.shape, jnp.float32)
    for ref in (k_main, s_main, q_main):
        ref[...] = jnp.zeros((FLAT, LANES), jnp.float32)
    for ref in (r0_main, r_main, u_main, v_main, p_main):
        ref[0 : PAD + ROWS] = jnp.zeros((PAD + ROWS, LANES), jnp.float32)
        ref[FLAT - PAD - ROWS :] = jnp.zeros((PAD + ROWS, LANES), jnp.float32)
    for ref in (k_a, k_b, r0_a, r0_b, r_a, r_b, u_a, u_b, v_a, v_b, p_a, p_b):
        ref[...] = jnp.zeros((SIDE, LANES), jnp.float32)

    at_in, at_out = iota(0, (2 * LANES, 2 * LANES)), iota(1, (2 * LANES, 2 * LANES))
    from_lane = lax.rem(at_out + jnp.where(at_out < LANES, LANES - 1, 1), LANES)
    shifter[...] = jnp.where(lax.rem(at_in, LANES) == from_lane, 1.0, 0.0).astype(jnp.bfloat16)

    lane, row = iota(1), iota(0)
    x = row - 4
    z_fa, y_fa = classes((ROWS, LANES), 0)
    z_fb, y_fb = classes((ROWS, LANES), 5)
    z_pa, y_pa = classes((ROWS, LANES), 1)
    z_pb, y_pb = classes((ROWS, LANES), 4)
    y_fa, y_fb, y_pa, y_pb = y_fa - 2, y_fb - 7, y_pa - 3, y_pb - 6

    def gather(accs, z, value):
        at = iota(1, value.shape)
        moved = roll(value, STEP * z + 2)
        return (
            jnp.where(lanes_between(at, STEP * z + 2, STEP * z + 8), moved, accs[0]),
            jnp.where(lanes_between(at, STEP * z - 5, STEP * z + 1), moved, accs[1]),
        )

    wait_rows(load_sem, 3 * 8 * 32 + 32)

    depth = in_depth[...]
    for z in range(8):
        in_perm[z] = jnp.where((gz * 8 + z) < depth, in_perm[z], 0.0)

    zero_block = jnp.zeros((32, LANES), jnp.float32)
    edges = [(zero_block, zero_block)] * 3
    for z in range(8):
        for f, ref in enumerate((in_perm, in_stor, in_src)):
            edges[f] = gather(edges[f], z + 3, ref[z])
        for v, low in ((0, 0), (1, 29)):
            own_rows[v, z, 0:3] = in_perm[z, low : low + 3]
            for i, ref in ((3, in_stor), (5, in_src)):
                own_rows[v, z, i : i + 2] = ref[z, low + v : low + v + 2]
    _, c = classes((32, LANES), 4)
    own_side[0, 4:36] = jnp.where(
        c >= 6, edges[0][0], jnp.where(c >= 3, roll(edges[1][0], -3), roll(edges[2][0], -6))
    )
    _, c = classes((32, LANES), 1)
    own_side[1, 4:36] = jnp.where(
        c < 3, edges[0][1], jnp.where(c < 6, roll(edges[1][1], 3), roll(edges[2][1], 6))
    )
    for d in range(2):
        for u in range(2):
            own_fold[u, d] = fold(own_side[d], STEP * (8 if u else 3) - (1 if d else 4))
    pl.semaphore_wait(barrier, len(DIRS))

    rows0 = []

    def post0(src, dst, s):
        pltpu.make_async_remote_copy(
            src_ref=src, dst_ref=dst, send_sem=send0, recv_sem=recv0,
            device_id=device(s), device_id_type=MESH,
        ).start()
        rows0.append(rows_of(src))

    for sz in (-1, 1):
        u = part_of(sz)
        post0(in_perm.at[pl.ds(5 * u, 3)], rz_k.at[u], (sz, 0, 0))
        post0(in_stor.at[pl.ds(6 * u, 2)], rz_s.at[u], (sz, 0, 0))
        post0(in_src.at[pl.ds(6 * u, 2)], rz_q.at[u], (sz, 0, 0))
    for s in DIRS:
        sz, sx, sy = s
        u, v, d = part_of(sz), part_of(sx), part_of(sy)
        if sy == 0:
            if sz == 0:
                post0(own_rows.at[v, :, pl.ds(0, 7)], rx0.at[v, :, pl.ds(0, 7)], s)
            elif sx != 0:
                post0(
                    own_rows.at[v, pl.ds(5 * u, 3), pl.ds(0, 7)],
                    rzx0.at[u, v, :, pl.ds(0, 7)], s,
                )
        elif sx != 0:
            post0(
                own_side.at[d, pl.ds(33 if v else 4, 3)],
                rxy0.at[sz + 1, v, d, pl.ds(1 if v else 4, 3)], s,
            )
        elif sz != 0:
            post0(own_fold.at[u, d], rzy0.at[u, d], s)
        else:
            post0(own_side.at[d], ry0.at[d], s)
    wait_rows(recv0, sum(rows0))

    def inside(flag):
        return flag.astype(jnp.float32)

    below, above = inside(gz > 0), inside(gz < n_gz - 1)
    before, after = inside(gx > 0), inside(gx < n_gx - 1)
    in_z = {z: below if z < 3 else above for z in (0, 1, 2, 11, 12, 13)}
    for z in range(PLANES):
        base = PAD + ROWS * z
        if 3 <= z <= 10:
            middle = in_perm[z - 3]
            low, high = rx0[1, z - 3], rx0[0, z - 3]
            gain = 1.0
            s_main[base + 4 : base + 36] = in_stor[z - 3]
            q_main[base + 4 : base + 36] = in_src[z - 3]
        else:
            u, i = (1, z) if z < 3 else (0, z - 11)
            middle = rz_k[u, i] * in_z[z]
            low, high = rzx0[u, 1, i], rzx0[u, 0, i]
            gain = in_z[z]
            if 1 <= z <= 12:
                i = z - 1 if z < 3 else z - 11
                s_main[base + 4 : base + 36] = rz_s[u, i]
                q_main[base + 4 : base + 36] = rz_q[u, i]
        k_main[base + 4 : base + 36] = middle
        k_main[base + 1 : base + 4] = low[0:3] * (before * gain)
        k_main[base + 36 : base + 39] = high[0:3] * (after * gain)
        s_main[base + 2 : base + 4] = low[3:5]
        s_main[base + 36 : base + 38] = high[3:5]
        q_main[base + 2 : base + 4] = low[5:7]
        q_main[base + 36 : base + 38] = high[5:7]

    def z_sum(here, lower, upper, offset, shift=0, move=roll, reach=5):
        z, _ = classes(here.shape, offset)
        moved = jnp.where(
            z < reach, move(lower, -8 * STEP - shift),
            jnp.where(between(z, 14 - reach, 13), move(upper, 8 * STEP + shift), 0.0),
        )
        return here + moved

    def beside(y, zy, xy, d, reach=5):
        offset = 1 if d else 4
        return add_tiles(
            z_sum(y[d], zy[1, d], zy[0, d], offset, move=unfold, reach=reach),
            z_sum(xy[1, 1, d], xy[2, 1, d], xy[0, 1, d], offset, reach=reach),
            z_sum(xy[1, 0, d], xy[2, 0, d], xy[0, 0, d], offset, reach=reach),
        )

    from_left, from_right = (beside(ry0, rzy0, rxy0, d, 3) for d in (1, 0))

    def grid_z(z):
        return both(either(z >= 3, gz > 0), either(z <= 10, gz < n_gz - 1))

    row_in = both(either(x >= 0, gx > 0), either(x < 32, gx < n_gx - 1))
    gain_a = jnp.where(both(row_in, grid_z(z_pa), gy > 0), 1.0, 0.0)
    gain_b = jnp.where(both(row_in, grid_z(z_pb), gy < n_gy - 1), 1.0, 0.0)
    k_edges, s_edges, q_edges = ((zero_plane, zero_plane) for _ in range(3))
    for z in range(PLANES):
        k_edges = gather(k_edges, z, k_main[plane(z)])
        if 1 <= z <= 12:
            s_edges = gather(s_edges, z, s_main[plane(z)])
            q_edges = gather(q_edges, z, q_main[plane(z)])
    k_left, k_right = from_left * gain_a, from_right * gain_b
    k_fa = jnp.where(both(y_pa >= -2, y_pa <= -1), k_left, k_edges[0])
    k_fb = jnp.where(both(y_pb >= 0, y_pb <= 1), k_right, k_edges[1])
    k_pa = jnp.where(y_pa == -3, k_left, k_fa)
    k_pb = jnp.where(y_pb == 2, k_right, k_fb)
    k_a[MIDDLE] = k_fa
    k_b[MIDDLE] = k_fb
    s_a = jnp.where(both(y_pa >= -2, y_pa <= -1), roll(from_left, -3), s_edges[0])
    q_a = jnp.where(both(y_pa >= -2, y_pa <= -1), roll(from_left, -6), q_edges[0])
    s_b = jnp.where(both(y_pb >= 0, y_pb <= 1), roll(from_right, 3), s_edges[1])
    q_b = jnp.where(both(y_pb >= 0, y_pb <= 1), roll(from_right, 6), q_edges[1])

    def weights(centre, others, storage, source, keep):
        idle = jnp.where(centre > 0.0, 0.0, 1.0)
        diagonal = storage + idle
        couplings = []
        for other in others:
            other_idle = jnp.where(other > 0.0, 0.0, 1.0)
            c = (2.0 * centre) * other / ((centre + idle) + (other + other_idle))
            couplings.append(c)
            diagonal = diagonal + c
        gain = jnp.where(keep, RELAX / diagonal, 0.0)
        live = jnp.where(keep, 1.0 - idle, 0.0)
        return [c * gain for c in couplings], live * gain * source, live * RELAX, diagonal

    def around(ref, z, count=1):
        base, rows = PAD + ROWS * z, ROWS * count
        return (
            ref[pl.ds(base - ROWS, rows)],
            ref[pl.ds(base + ROWS, rows)],
            ref[pl.ds(base - 1, rows)],
            ref[pl.ds(base + 1, rows)],
        )

    def side_around(ref, centre):
        return (
            roll(centre, STEP), roll(centre, -STEP), ref[pl.ds(PAD - 1, ROWS)], ref[pl.ds(PAD + 1, ROWS)],
        )

    rows_kept, rows_own = between(row, 2, 37), between(row, 4, 35)
    inner = both(lane > 0, lane < LANES - 1)
    total = zero_plane
    r_edges = (zero_plane, zero_plane)
    for z in range(1, 13):
        centre = k_main[plane(z)]
        ws, r, al, diagonal = weights(
            centre, around(k_main, z) + (roll(centre, 1), roll(centre, -1)),
            s_main[plane(z)], q_main[plane(z)], rows_kept,
        )
        for i in range(6):
            w_main[i, plane(z)] = ws[i]
        alpha[plane(z)] = al
        r0_main[plane(z)] = r
        r_edges = gather(r_edges, z, r)
        if 3 <= z <= 10:
            sc = jnp.where(both(rows_own, inner), diagonal * (1.0 / RELAX), 0.0)
            scale[z - 3] = sc
            total = total + (r * sc) * (r * sc)
    scale_side = []
    for ref, k_f, left, right, st, q, z, y, low, high, w_ref, al_ref, r_ref, edge, own in (
        (k_a, k_fa, k_pa, k_fa, s_a, q_a, z_fa, y_fa, -2, 5, w_a, alpha_a, r0_a, r_edges[0], 0),
        (k_b, k_fb, k_fb, k_pb, s_b, q_b, z_fb, y_fb, -6, 1, w_b, alpha_b, r0_b, r_edges[1], -1),
    ):
        keep = both(rows_kept, between(z, 1, 12), between(y, low, high))
        ws, r, al, diagonal = weights(
            k_f, side_around(ref, k_f) + (roll(left, 1), roll(right, -1)), st, q, keep
        )
        for i in range(6):
            w_ref[i] = ws[i]
        if low == -2:
            w_ref[6] = jnp.where(y == -2, 0.0, ws[4])
        else:
            w_ref[6] = jnp.where(y == 1, 0.0, ws[5])
        al_ref[...] = al
        r_ref[MIDDLE] = jnp.where(y <= 0 if low == -2 else y >= -1, r, edge)
        sc = jnp.where(
            both(rows_own, between(z, 3, 10), y == own), diagonal * (1.0 / RELAX), 0.0
        )
        scale_side.append(sc)
        total = total + (r * sc) * (r * sc)

    def half(flag):
        return jnp.where(flag, 0.5, 1.0)

    def axis_gain(position, extent, owner, owners):
        inner_low = both(position >= 0, position < 2, owner > 0)
        inner_high = both(position >= extent - 2, position < extent, owner < owners - 1)
        outer = either(
            both(position >= -2, position < 0), both(position >= extent, position < extent + 2)
        )
        return half(either(outer, inner_low, inner_high))

    x_gain = axis_gain(x, 32, gx, n_gx)
    main_gain = x_gain * axis_gain(lane, 128, gy, n_gy)
    side_gain = (
        x_gain * axis_gain(z_pa - 3, 8, gz, n_gz) * axis_gain(y_pa, 128, gy, n_gy),
        x_gain * axis_gain(z_pb - 3, 8, gz, n_gz) * axis_gain(y_pb + 128, 128, gy, n_gy),
    )

    def z_gain(z):
        if z in (0, 13):
            return 1.0
        if z in (1, 2, 11, 12):
            return 0.5
        if z in (3, 4):
            return jnp.where(gz > 0, 0.5, 1.0)
        if z in (9, 10):
            return jnp.where(gz < n_gz - 1, 0.5, 1.0)
        return 1.0

    def side_sweep(ref, rhs, w_ref, last):
        value = ref[MIDDLE]
        others = side_around(ref, value) + (roll(value, 1), roll(value, -1))
        value = (1.0 - RELAX) * value + rhs[MIDDLE]
        for i, other in enumerate(others):
            value = value + w_ref[6 if i == last else i] * other
        return value

    def main_sweep(ref, rhs, z):
        value = ref[plane(z, 2)]
        hi = value.astype(jnp.bfloat16)
        lo = (value - hi.astype(jnp.float32)).astype(jnp.bfloat16)
        beside_y = jnp.dot(
            jnp.concatenate([hi, lo], axis=1), shifter[...], preferred_element_type=jnp.float32
        )
        others = around(ref, z, 2) + (beside_y[:, :LANES], beside_y[:, LANES:])
        value = (1.0 - RELAX) * value + rhs[plane(z, 2)]
        for i, other in enumerate(others):
            value = value + w_main[i, plane(z, 2)] * other
        return value

    partials = [total]
    sent = [(send0, sum(rows0))]
    for k in range(ITERS):
        rhs, rhs_a, rhs_b = (r0_main, r0_a, r0_b) if k == 0 else (r_main, r_a, r_b)
        rows = []
        last_one = k == ITERS - 1

        def post(source, target, s):
            pltpu.make_async_remote_copy(
                src_ref=source, dst_ref=target, send_sem=sends.at[k], recv_sem=recvs.at[k],
                device_id=device(s), device_id_type=MESH,
            ).start()
            rows.append(rows_of(source))

        for before_ref, after_ref in (((rhs_a, rhs_b), (u_a, u_b)), ((u_a, u_b), (v_a, v_b))):
            after_ref[0][MIDDLE] = side_sweep(before_ref[0], rhs_a, w_a, 4)
            after_ref[1][MIDDLE] = side_sweep(before_ref[1], rhs_b, w_b, 5)
        side_a = side_sweep(v_a, rhs_a, w_a, 4)
        side_b = side_sweep(v_b, rhs_b, w_b, 5)
        far_b = roll(side_b, 64)
        send[k, 0] = jnp.where(lane < 60, side_a, far_b)
        send[k, 13] = jnp.where(lane < 60, far_b, side_a)
        send[k, 14] = side_a
        send[k, 15] = side_b
        for d, value in ((0, side_a), (1, side_b)):
            for u in range(2):
                fold_out[k, u, d] = fold(value, STEP * (8 if u else 1) - d)
        for s in DIRS:
            sz, sx, sy = s
            u, v, d = part_of(sz), part_of(sx), part_of(sy)
            if sy != 0:
                if sx != 0:
                    post(
                        send.at[k, 14 + d, pl.ds(33 if v else 2, 5)],
                        rxy.at[k, sz + 1, v, d, strip(sx)], s,
                    )
                elif sz != 0:
                    post(fold_out.at[k, u, d], rzy.at[k, u, d], s)
                else:
                    post(send.at[k, 14 + d], ry.at[k, d], s)

        for z in range(1, 13, 2):
            u_main[plane(z, 2)] = main_sweep(rhs, rhs, z)
        for z in range(1, 13, 2):
            v_main[plane(z, 2)] = main_sweep(u_main, rhs, z)
        for z in (1, 3, 5, 11, 9, 7):
            value = main_sweep(v_main, rhs, z)
            send[k, z] = value[:ROWS]
            send[k, z + 1] = value[ROWS:]
            if z in (5, 7):
                sz = -1 if z == 5 else 1
                count = 4 if last_one else 6
                skip = 6 - count if sz > 0 else 0
                planes, places = pl.ds((8 if sz > 0 else 0) + skip, count), pl.ds(skip, count)
                u = part_of(sz)
                pieces = pl.ds(2 + 5 * skip, 5 * count)
                for v, low in ((0, 2), (1, 33)):
                    for i in range(skip, skip + count):
                        zx_out[k, u, v, 2 + 5 * i : 7 + 5 * i] = send[
                            k, (8 + i) if u else i, low : low + 5
                        ]
                    post(
                        zx_out.at[k, u, v, pieces], rzx.at[k, u, v, pieces],
                        (sz, 2 * v - 1, 0),
                    )
                kept = pl.ds(2, 36)
                post(send.at[k, planes, kept], rz.at[k, u, places, kept], (sz, 0, 0))
        for sx in (-1, 1):
            v = part_of(sx)
            post(
                send.at[k, pl.ds(1, 15), pl.ds(33 if v else 2, 5)],
                rx.at[k, v, :, strip(sx)], (0, sx, 0),
            )
        wait_rows(recvs.at[k], sum(rows))
        sent.append((sends.at[k], sum(rows)))

        def edge_rows(u, v, i):
            at = iota(0, (8, LANES))
            tile = rzx[k, u, v, 5 * i + v : 5 * i + v + 8]
            return jnp.where(between(at, 2 - v, 6 - v), tile, 0.0)

        new_p = []
        for own, d, offset, shift, y, low, high, outer_low, outer_high, ref in (
            (14, 1, 1, 0, y_pa, -2, 3, -3, 1, p_a),
            (15, 0, 4, 64, y_pb, -4, 1, -2, 2, p_b),
        ):
            here = add_tiles(
                z_sum(send[k, own], rz[k, 1, 5], rz[k, 0, 0], offset, shift),
                z_sum(rx[k, 1, own - 1], edge_rows(1, 1, 5), edge_rows(0, 1, 0), offset, shift),
                z_sum(rx[k, 0, own - 1], edge_rows(1, 0, 5), edge_rows(0, 0, 0), offset, shift),
            )
            other = beside(ry.at[k], rzy.at[k], rxy.at[k], d)
            value = jnp.where(between(y, low, high), here, 0.0) + jnp.where(
                between(y, outer_low, outer_high), other, 0.0
            )
            value = value * side_gain[1 - d]
            if k > 0:
                value = ref[MIDDLE] + value
            ref[MIDDLE] = value
            new_p.append(value)
        edges = jnp.where(between(y_pa, 0, 3), new_p[0], new_p[1])
        edge_lane = either(lane < 4, lane >= LANES - 4)
        for z in range(2, 12) if last_one else range(PLANES):
            solved = 1 <= z <= 12
            value = send[k, z] if solved else zero_plane
            first = rx[k, 1, z - 1] if solved else jnp.zeros((8, LANES), jnp.float32)
            last = rx[k, 0, z - 1] if solved else jnp.zeros((8, LANES), jnp.float32)
            if z <= 4:
                value = value + rz[k, 1, z]
                first = first + edge_rows(1, 1, z)
                last = last + edge_rows(1, 0, z)
            if z >= 9:
                value = value + rz[k, 0, z - 8]
                first = first + edge_rows(0, 1, z - 8)
                last = last + edge_rows(0, 0, z - 8)
            value = add_tiles(value, first, last) * (main_gain * z_gain(z))
            if k > 0:
                value = p_main[plane(z)] + value
            p_main[plane(z)] = jnp.where(edge_lane, roll(edges, -(STEP * z + 2)), value)

        total = zero_plane
        r_edges = (zero_plane, zero_plane)
        for z in range(3, 11) if last_one else range(1, 13):
            centre = p_main[plane(z)]
            value = r0_main[plane(z)] - alpha[plane(z)] * centre
            for i, other in enumerate(
                around(p_main, z) + (roll(centre, 1), roll(centre, -1))
            ):
                value = value + w_main[i, plane(z)] * other
            if not last_one:
                r_main[plane(z)] = value
                r_edges = gather(r_edges, z, value)
            if 3 <= z <= 10:
                value = value * scale[z - 3]
                total = total + value * value
        for i, (ref, r0, al, w_ref, r_ref, p) in enumerate(
            ((p_a, r0_a, alpha_a, w_a, r_a, new_p[0]), (p_b, r0_b, alpha_b, w_b, r_b, new_p[1]))
        ):
            value = r0[MIDDLE] - al[...] * p
            for n, other in enumerate(side_around(ref, p) + (roll(p, 1), roll(p, -1))):
                value = value + w_ref[n] * other
            if not last_one:
                r_ref[MIDDLE] = jnp.where(y_fa <= 0 if i == 0 else y_fb >= -1, value, r_edges[i])
            value = value * scale_side[i]
            total = total + value * value
        partials.append(total)

    for z in range(8):
        out_ref[z] = p_main[pl.ds(PAD + ROWS * (z + 3) + 4, 32)]

    at = iota(1, (1, LANES)) // 32
    mine = jnp.zeros((1, LANES), jnp.float32)
    for i, value in enumerate(partials):
        value = jnp.sum(value, axis=0, keepdims=True)
        value = value + roll(value, 64)
        mine = jnp.where(at == i, value + roll(value, 32), mine)
    pair = gy + 1 - 2 * lax.rem(gy, 2)

    def ring(i, n):
        return min(i, n - i)

    chips = sorted(
        (
            (i, j, h)
            for i in range(n_gx)
            for j in range(n_gy // 2)
            for h in range(n_gz)
            if (i, j, h) != (0, 0, 0)
        ),
        key=lambda t: -ring(t[0], n_gx) - ring(t[1], n_gy // 2) - ring(t[2], n_gz),
    )
    rounds = (
        [(gx, pair, gz)],
        [
            (lax.rem(gx + i, n_gx), lax.rem(gy + 2 * j, n_gy), lax.rem(gz + h, n_gz))
            for i, j, h in chips
        ],
    )
    slots = (lax.rem(gy, 2), (gx * (n_gy // 2) + gy // 2) * n_gz + gz)
    for n, targets in enumerate(rounds):
        here = part_in.at[n, slots[n], pl.ds(0, 1)]
        part[n, 0:1] = mine
        for target in targets:
            pltpu.make_async_remote_copy(
                src_ref=part.at[n, pl.ds(0, 1)], dst_ref=here,
                send_sem=ar_send.at[n], recv_sem=ar_recv.at[n],
                device_id=target, device_id_type=MESH,
            ).start()
        here[...] = mine
        wait_rows(ar_recv.at[n], len(targets))
        sent.append((ar_send.at[n], len(targets)))
        terms = [part_in[n, i, 0:1] for i in range(len(targets) + 1)]
        while len(terms) > 1:
            terms = [sum(terms[i + 1 : i + 2], terms[i]) for i in range(0, len(terms), 2)]
        mine = terms[0]
    squares = [
        jnp.sum(jnp.where(at == i, mine, 0.0), axis=1, keepdims=True) for i in range(ITERS + 1)
    ]
    for i in range(ITERS):
        hist_ref[i] = jnp.sum(jnp.sqrt(squares[i + 1] / squares[0]))
    for sem, rows in sent:
        wait_rows(sem, rows)


def solution(mesh):
    sizes = (mesh.shape["gx"], mesh.shape["gy"], mesh.shape["gz"])
    f32 = jnp.float32

    def vmem(*shape):
        return pltpu.VMEM(shape, f32)

    scratch = [
        vmem(8, 32, LANES), vmem(8, 32, LANES), vmem(8, 32, LANES),
        pltpu.VMEM((32, LANES), jnp.int32),
        vmem(2, 8, 8, LANES), vmem(2, ROWS, LANES), vmem(2, 2, 16, LANES),
        vmem(2, 3, 32, LANES), vmem(2, 2, 32, LANES), vmem(2, 2, 32, LANES),
        vmem(2, 8, 8, LANES), vmem(2, 2, 3, 8, LANES),
        vmem(2, ROWS, LANES), vmem(2, 2, 16, LANES), vmem(3, 2, 2, 8, LANES),
        vmem(ITERS, 16, ROWS, LANES), vmem(ITERS, 2, 2, 32, LANES), vmem(ITERS, 2, 2, 16, LANES),
        vmem(ITERS, 2, 6, ROWS, LANES), vmem(ITERS, 2, 15, 8, LANES),
        vmem(ITERS, 2, 2, 40, LANES),
        vmem(ITERS, 2, ROWS, LANES), vmem(ITERS, 2, 2, 16, LANES), vmem(ITERS, 3, 2, 2, 8, LANES),
        vmem(FLAT, LANES), vmem(SIDE, LANES), vmem(SIDE, LANES), vmem(FLAT, LANES), vmem(FLAT, LANES),
        vmem(6, FLAT, LANES), vmem(7, ROWS, LANES), vmem(7, ROWS, LANES),
        vmem(FLAT, LANES), vmem(ROWS, LANES), vmem(ROWS, LANES), vmem(8, ROWS, LANES),
    ]
    for _ in range(5):
        scratch += [vmem(FLAT, LANES), vmem(SIDE, LANES), vmem(SIDE, LANES)]
    scratch += [
        pltpu.VMEM((2 * LANES, 2 * LANES), jnp.bfloat16),
        vmem(2, 8, LANES), vmem(2, 128, 8, LANES),
        vmem(2048, LANES),
        pltpu.SemaphoreType.DMA, pltpu.SemaphoreType.DMA, pltpu.SemaphoreType.DMA,
        pltpu.SemaphoreType.DMA((ITERS,)), pltpu.SemaphoreType.DMA((ITERS,)),
        pltpu.SemaphoreType.DMA((2,)), pltpu.SemaphoreType.DMA((2,)),
    ]

    def per_device(source, permeability, storage, column_depth):
        return pl.pallas_call(
            functools.partial(kernel, sizes),
            out_shape=(
                jax.ShapeDtypeStruct(source.shape, f32),
                jax.ShapeDtypeStruct((ITERS,), f32),
            ),
            in_specs=[pl.BlockSpec(memory_space=pl.ANY)] * 4,
            out_specs=(
                pl.BlockSpec(memory_space=pltpu.VMEM),
                pl.BlockSpec(memory_space=pltpu.SMEM),
            ),
            scratch_shapes=scratch,
            compiler_params=pltpu.CompilerParams(
                collective_id=0, has_side_effects=True, vmem_limit_bytes=55056 * 2**10
            ),
            name="schwarz",
        )(source, permeability, storage, column_depth)

    placed = (P("gz", "gx", "gy"), P("gz", "gx", "gy"), P("gz", "gx", "gy"), P("gx", "gy"))
    return jax.shard_map(
        per_device,
        mesh=mesh,
        in_specs=placed,
        out_specs=(P("gz", "gx", "gy"), P()),
        check_vma=False,
    )
```

```python
import functools
import math

import jax
import jax.numpy as jnp
from jax import lax
from jax.experimental import pallas as pl
from jax.experimental.pallas import tpu as pltpu
from jax.sharding import PartitionSpec as P

MESH = pl.DeviceIdType.MESH
ITERS = 3
RELAX = 0.9

PLANES, ROWS, LANES, PAD, STEP = 14, 40, 128, 8, 9
FLAT = PLANES * ROWS + 2 * PAD
SIDE = ROWS + 2 * PAD
DIRS = tuple(
    (sz, sx, sy)
    for sz in (-1, 0, 1)
    for sx in (-1, 0, 1)
    for sy in (-1, 0, 1)
    if (sz, sx, sy) != (0, 0, 0)
)
DIRS = tuple(sorted(DIRS, key=lambda s: -(abs(s[0]) + abs(s[1]) + abs(s[2]))))


def plane(z, count=1):
    return pl.ds(PAD + ROWS * z, ROWS * count)


MIDDLE = pl.ds(PAD, ROWS)


def iota(axis, shape=(ROWS, LANES)):
    return lax.broadcasted_iota(jnp.int32, shape, axis)


def roll(x, shift):
    return pltpu.roll(x, shift % LANES, axis=x.ndim - 1)


def both(*flags):
    return functools.reduce(jnp.logical_and, flags)


def either(*flags):
    return functools.reduce(jnp.logical_or, flags)


def between(x, low, high):
    return both(x >= low, x <= high)


def lanes_between(lane, low, high):
    if low < 0:
        return either(lane >= low + LANES, lane <= high)
    return between(lane, low, high)


def classes(shape, offset):
    u = lax.rem(iota(1, shape) + offset, LANES)
    z = (u * 57) >> 9
    return z, u - STEP * z


def strip(sx, count, first=0):
    return pl.ds(first + (6 - count if sx > 0 else 2), count)


def add_tiles(acc, first, last):
    return jnp.concatenate([acc[:8] + first, acc[8 : ROWS - 8], acc[ROWS - 8 :] + last], axis=0)


WIDTH = 43


def fold(side, first):
    t = [side[8 * i : 8 * i + 8] for i in range(5)]
    at = lax.rem(iota(1, (8, LANES)) + (LANES - first), LANES)
    one = jnp.where(
        at < WIDTH, t[0], jnp.where(at < 2 * WIDTH, roll(t[1], WIDTH), roll(t[2], 2 * WIDTH))
    )
    two = jnp.where(at < WIDTH, t[3], roll(t[4], WIDTH))
    return jnp.concatenate([one, two], axis=0)


def unfold(both_tiles, shift):
    return jnp.concatenate(
        [roll(both_tiles[8 * (i // 3) : 8 * (i // 3) + 8], shift - WIDTH * (i % 3)) for i in range(5)],
        axis=0,
    )


def part_of(v):
    return (v + 1) // 2


def kernel(
    sizes, src_hbm, perm_hbm, stor_hbm, depth_hbm, out_ref, hist_ref,
    in_src, in_perm, in_stor, in_depth,
    own_rows, own_side, own_fold, rz_k, rz_s, rz_q, rx0, rzx0, ry0, rzy0, rxy0,
    send, zx_out, fold_out, rz, rx, rzx, ry, rzy, rxy,
    k_main, k_a, k_b, s_main, q_main,
    w_main, w_a, w_b, alpha, alpha_a, alpha_b, scale,
    r0_main, r0_a, r0_b, r_main, r_a, r_b, u_main, u_a, u_b, v_main, v_a, v_b, p_main, p_a, p_b,
    shifter, part, part_in, tally,
    load_sem, send0, recv0, sends, recvs, ar_send, ar_recv,
):
    n_gx, n_gy, n_gz = sizes
    gx, gy, gz = lax.axis_index("gx"), lax.axis_index("gy"), lax.axis_index("gz")

    def device(s):
        return (
            lax.rem(gx + s[1] + n_gx, n_gx),
            lax.rem(gy + s[2] + n_gy, n_gy),
            lax.rem(gz + s[0] + n_gz, n_gz),
        )

    def wait_rows(sem, rows):
        span = tally.at[pl.ds(0, rows)]
        pltpu.make_async_copy(span, span, sem).wait()

    def rows_of(ref):
        return math.prod(ref.shape[:-1])

    rxy0[...] = jnp.zeros(rxy0.shape, jnp.float32)
    barrier = pltpu.get_barrier_semaphore()
    for s in DIRS:
        pl.semaphore_signal(barrier, inc=1, device_id=device(s), device_id_type=MESH)

    loads = [
        pltpu.make_async_copy(a, b, load_sem)
        for a, b in (
            (depth_hbm, in_depth), (perm_hbm, in_perm), (stor_hbm, in_stor), (src_hbm, in_src)
        )
    ]
    for copy in loads:
        copy.start()

    zero_plane = jnp.zeros((ROWS, LANES), jnp.float32)
    for ref in (rz, rxy, rx):
        ref[...] = jnp.zeros(ref.shape, jnp.float32)
    own_rows[...] = jnp.zeros(own_rows.shape, jnp.float32)
    own_side[...] = jnp.zeros(own_side.shape, jnp.float32)
    for ref in (k_main, s_main, q_main):
        ref[...] = jnp.zeros((FLAT, LANES), jnp.float32)
    for ref in (r0_main, r_main, u_main, v_main, p_main):
        ref[0 : PAD + ROWS] = jnp.zeros((PAD + ROWS, LANES), jnp.float32)
        ref[FLAT - PAD - ROWS :] = jnp.zeros((PAD + ROWS, LANES), jnp.float32)
    for ref in (k_a, k_b, r0_a, r0_b, r_a, r_b, u_a, u_b, v_a, v_b, p_a, p_b):
        ref[...] = jnp.zeros((SIDE, LANES), jnp.float32)

    at_in, at_out = iota(0, (2 * LANES, 2 * LANES)), iota(1, (2 * LANES, 2 * LANES))
    from_lane = lax.rem(at_out + jnp.where(at_out < LANES, LANES - 1, 1), LANES)
    shifter[...] = jnp.where(lax.rem(at_in, LANES) == from_lane, 1.0, 0.0).astype(jnp.bfloat16)

    lane, row = iota(1), iota(0)
    x = row - 4
    z_fa, y_fa = classes((ROWS, LANES), 0)
    z_fb, y_fb = classes((ROWS, LANES), 5)
    z_pa, y_pa = classes((ROWS, LANES), 1)
    z_pb, y_pb = classes((ROWS, LANES), 4)
    y_fa, y_fb, y_pa, y_pb = y_fa - 2, y_fb - 7, y_pa - 3, y_pb - 6

    def gather(accs, z, value):
        at = iota(1, value.shape)
        moved = roll(value, STEP * z + 2)
        return (
            jnp.where(lanes_between(at, STEP * z + 2, STEP * z + 8), moved, accs[0]),
            jnp.where(lanes_between(at, STEP * z - 5, STEP * z + 1), moved, accs[1]),
        )

    wait_rows(load_sem, 3 * 8 * 32 + 32)

    depth = in_depth[...]
    for z in range(8):
        in_perm[z] = jnp.where((gz * 8 + z) < depth, in_perm[z], 0.0)

    zero_block = jnp.zeros((32, LANES), jnp.float32)
    edges = [(zero_block, zero_block)] * 3
    for z in range(8):
        for f, ref in enumerate((in_perm, in_stor, in_src)):
            edges[f] = gather(edges[f], z + 3, ref[z])
        for v, low in ((0, 0), (1, 29)):
            own_rows[v, z, 0:3] = in_perm[z, low : low + 3]
            for i, ref in ((3, in_stor), (5, in_src)):
                own_rows[v, z, i : i + 2] = ref[z, low + v : low + v + 2]
    _, c = classes((32, LANES), 4)
    own_side[0, 4:36] = jnp.where(
        c >= 6, edges[0][0], jnp.where(c >= 3, roll(edges[1][0], -3), roll(edges[2][0], -6))
    )
    _, c = classes((32, LANES), 1)
    own_side[1, 4:36] = jnp.where(
        c < 3, edges[0][1], jnp.where(c < 6, roll(edges[1][1], 3), roll(edges[2][1], 6))
    )
    for d in range(2):
        for u in range(2):
            own_fold[u, d] = fold(own_side[d], STEP * (8 if u else 3) - (1 if d else 4))
    pl.semaphore_wait(barrier, len(DIRS))

    rows0 = []

    def post0(src, dst, s):
        pltpu.make_async_remote_copy(
            src_ref=src, dst_ref=dst, send_sem=send0, recv_sem=recv0,
            device_id=device(s), device_id_type=MESH,
        ).start()
        rows0.append(rows_of(src))

    for sz in (-1, 1):
        u = part_of(sz)
        post0(in_perm.at[pl.ds(5 * u, 3)], rz_k.at[u], (sz, 0, 0))
        post0(in_stor.at[pl.ds(6 * u, 2)], rz_s.at[u], (sz, 0, 0))
        post0(in_src.at[pl.ds(6 * u, 2)], rz_q.at[u], (sz, 0, 0))
    for s in DIRS:
        sz, sx, sy = s
        u, v, d = part_of(sz), part_of(sx), part_of(sy)
        if sy == 0:
            if sz == 0:
                post0(own_rows.at[v, :, pl.ds(0, 7)], rx0.at[v, :, pl.ds(0, 7)], s)
            elif sx != 0:
                post0(
                    own_rows.at[v, pl.ds(5 * u, 3), pl.ds(0, 7)],
                    rzx0.at[u, v, :, pl.ds(0, 7)], s,
                )
        elif sx != 0:
            post0(
                own_side.at[d, pl.ds(33 if v else 4, 3)],
                rxy0.at[sz + 1, v, d, pl.ds(1 if v else 4, 3)], s,
            )
        elif sz != 0:
            post0(own_fold.at[u, d], rzy0.at[u, d], s)
        else:
            post0(own_side.at[d], ry0.at[d], s)
    wait_rows(recv0, sum(rows0))

    def inside(flag):
        return flag.astype(jnp.float32)

    below, above = inside(gz > 0), inside(gz < n_gz - 1)
    before, after = inside(gx > 0), inside(gx < n_gx - 1)
    in_z = {z: below if z < 3 else above for z in (0, 1, 2, 11, 12, 13)}
    for z in range(PLANES):
        base = PAD + ROWS * z
        if 3 <= z <= 10:
            middle = in_perm[z - 3]
            low, high = rx0[1, z - 3], rx0[0, z - 3]
            gain = 1.0
            s_main[base + 4 : base + 36] = in_stor[z - 3]
            q_main[base + 4 : base + 36] = in_src[z - 3]
        else:
            u, i = (1, z) if z < 3 else (0, z - 11)
            middle = rz_k[u, i] * in_z[z]
            low, high = rzx0[u, 1, i], rzx0[u, 0, i]
            gain = in_z[z]
            if 1 <= z <= 12:
                i = z - 1 if z < 3 else z - 11
                s_main[base + 4 : base + 36] = rz_s[u, i]
                q_main[base + 4 : base + 36] = rz_q[u, i]
        k_main[base + 4 : base + 36] = middle
        k_main[base + 1 : base + 4] = low[0:3] * (before * gain)
        k_main[base + 36 : base + 39] = high[0:3] * (after * gain)
        s_main[base + 2 : base + 4] = low[3:5]
        s_main[base + 36 : base + 38] = high[3:5]
        q_main[base + 2 : base + 4] = low[5:7]
        q_main[base + 36 : base + 38] = high[5:7]

    def z_sum(here, lower, upper, offset, shift=0, move=roll, reach=5):
        z, _ = classes(here.shape, offset)
        moved = jnp.where(
            z < reach, move(lower, -8 * STEP - shift),
            jnp.where(between(z, 14 - reach, 13), move(upper, 8 * STEP + shift), 0.0),
        )
        return here + moved

    def beside(y, zy, xy, d, reach=5):
        offset = 1 if d else 4
        return add_tiles(
            z_sum(y[d], zy[1, d], zy[0, d], offset, move=unfold, reach=reach),
            z_sum(xy[1, 1, d], xy[2, 1, d], xy[0, 1, d], offset, reach=reach),
            z_sum(xy[1, 0, d], xy[2, 0, d], xy[0, 0, d], offset, reach=reach),
        )

    from_left, from_right = (beside(ry0, rzy0, rxy0, d, 3) for d in (1, 0))

    def grid_z(z):
        return both(either(z >= 3, gz > 0), either(z <= 10, gz < n_gz - 1))

    row_in = both(either(x >= 0, gx > 0), either(x < 32, gx < n_gx - 1))
    gain_a = jnp.where(both(row_in, grid_z(z_pa), gy > 0), 1.0, 0.0)
    gain_b = jnp.where(both(row_in, grid_z(z_pb), gy < n_gy - 1), 1.0, 0.0)
    k_edges, s_edges, q_edges = ((zero_plane, zero_plane) for _ in range(3))
    for z in range(PLANES):
        k_edges = gather(k_edges, z, k_main[plane(z)])
        if 1 <= z <= 12:
            s_edges = gather(s_edges, z, s_main[plane(z)])
            q_edges = gather(q_edges, z, q_main[plane(z)])
    k_left, k_right = from_left * gain_a, from_right * gain_b
    k_fa = jnp.where(both(y_pa >= -2, y_pa <= -1), k_left, k_edges[0])
    k_fb = jnp.where(both(y_pb >= 0, y_pb <= 1), k_right, k_edges[1])
    k_pa = jnp.where(y_pa == -3, k_left, k_fa)
    k_pb = jnp.where(y_pb == 2, k_right, k_fb)
    k_a[MIDDLE] = k_fa
    k_b[MIDDLE] = k_fb
    s_a = jnp.where(both(y_pa >= -2, y_pa <= -1), roll(from_left, -3), s_edges[0])
    q_a = jnp.where(both(y_pa >= -2, y_pa <= -1), roll(from_left, -6), q_edges[0])
    s_b = jnp.where(both(y_pb >= 0, y_pb <= 1), roll(from_right, 3), s_edges[1])
    q_b = jnp.where(both(y_pb >= 0, y_pb <= 1), roll(from_right, 6), q_edges[1])

    def weights(centre, others, storage, source, keep):
        idle = jnp.where(centre > 0.0, 0.0, 1.0)
        diagonal = storage + idle
        couplings = []
        for other in others:
            other_idle = jnp.where(other > 0.0, 0.0, 1.0)
            c = (2.0 * centre) * other / ((centre + idle) + (other + other_idle))
            couplings.append(c)
            diagonal = diagonal + c
        gain = jnp.where(keep, RELAX / diagonal, 0.0)
        live = jnp.where(keep, 1.0 - idle, 0.0)
        return [c * gain for c in couplings], live * gain * source, live * RELAX, diagonal

    def around(ref, z, count=1):
        base, rows = PAD + ROWS * z, ROWS * count
        return (
            ref[pl.ds(base - ROWS, rows)],
            ref[pl.ds(base + ROWS, rows)],
            ref[pl.ds(base - 1, rows)],
            ref[pl.ds(base + 1, rows)],
        )

    def side_around(ref, centre):
        return (
            roll(centre, STEP), roll(centre, -STEP), ref[pl.ds(PAD - 1, ROWS)], ref[pl.ds(PAD + 1, ROWS)],
        )

    rows_kept, rows_own = between(row, 2, 37), between(row, 4, 35)
    inner = both(lane > 0, lane < LANES - 1)
    total = zero_plane
    r_edges = (zero_plane, zero_plane)
    for z in range(1, 13):
        centre = k_main[plane(z)]
        ws, r, al, diagonal = weights(
            centre, around(k_main, z) + (roll(centre, 1), roll(centre, -1)),
            s_main[plane(z)], q_main[plane(z)], rows_kept,
        )
        for i in range(6):
            w_main[i, plane(z)] = ws[i]
        alpha[plane(z)] = al
        r0_main[plane(z)] = r
        r_edges = gather(r_edges, z, r)
        if 3 <= z <= 10:
            sc = jnp.where(both(rows_own, inner), diagonal * (1.0 / RELAX), 0.0)
            scale[z - 3] = sc
            total = total + (r * sc) * (r * sc)
    scale_side = []
    for ref, k_f, left, right, st, q, z, y, low, high, w_ref, al_ref, r_ref, edge, own in (
        (k_a, k_fa, k_pa, k_fa, s_a, q_a, z_fa, y_fa, -2, 5, w_a, alpha_a, r0_a, r_edges[0], 0),
        (k_b, k_fb, k_fb, k_pb, s_b, q_b, z_fb, y_fb, -6, 1, w_b, alpha_b, r0_b, r_edges[1], -1),
    ):
        keep = both(rows_kept, between(z, 1, 12), between(y, low, high))
        ws, r, al, diagonal = weights(
            k_f, side_around(ref, k_f) + (roll(left, 1), roll(right, -1)), st, q, keep
        )
        for i in range(6):
            w_ref[i] = ws[i]
        if low == -2:
            w_ref[6] = jnp.where(y == -2, 0.0, ws[4])
        else:
            w_ref[6] = jnp.where(y == 1, 0.0, ws[5])
        al_ref[...] = al
        r_ref[MIDDLE] = jnp.where(y <= 0 if low == -2 else y >= -1, r, edge)
        sc = jnp.where(
            both(rows_own, between(z, 3, 10), y == own), diagonal * (1.0 / RELAX), 0.0
        )
        scale_side.append(sc)
        total = total + (r * sc) * (r * sc)

    def half(flag):
        return jnp.where(flag, 0.5, 1.0)

    def axis_gain(position, extent, owner, owners):
        inner_low = both(position >= 0, position < 2, owner > 0)
        inner_high = both(position >= extent - 2, position < extent, owner < owners - 1)
        outer = either(
            both(position >= -2, position < 0), both(position >= extent, position < extent + 2)
        )
        return half(either(outer, inner_low, inner_high))

    x_gain = axis_gain(x, 32, gx, n_gx)
    main_gain = x_gain * axis_gain(lane, 128, gy, n_gy)
    side_gain = (
        x_gain * axis_gain(z_pa - 3, 8, gz, n_gz) * axis_gain(y_pa, 128, gy, n_gy),
        x_gain * axis_gain(z_pb - 3, 8, gz, n_gz) * axis_gain(y_pb + 128, 128, gy, n_gy),
    )

    def z_gain(z):
        if z in (0, 13):
            return 1.0
        if z in (1, 2, 11, 12):
            return 0.5
        if z in (3, 4):
            return jnp.where(gz > 0, 0.5, 1.0)
        if z in (9, 10):
            return jnp.where(gz < n_gz - 1, 0.5, 1.0)
        return 1.0

    def side_sweep(ref, rhs, w_ref, last):
        value = ref[MIDDLE]
        others = side_around(ref, value) + (roll(value, 1), roll(value, -1))
        value = (1.0 - RELAX) * value + rhs[MIDDLE]
        for i, other in enumerate(others):
            value = value + w_ref[6 if i == last else i] * other
        return value

    def main_sweep(ref, rhs, z):
        value = ref[plane(z, 2)]
        hi = value.astype(jnp.bfloat16)
        lo = (value - hi.astype(jnp.float32)).astype(jnp.bfloat16)
        beside_y = jnp.dot(
            jnp.concatenate([hi, lo], axis=1), shifter[...], preferred_element_type=jnp.float32
        )
        others = around(ref, z, 2) + (beside_y[:, :LANES], beside_y[:, LANES:])
        value = (1.0 - RELAX) * value + rhs[plane(z, 2)]
        for i, other in enumerate(others):
            value = value + w_main[i, plane(z, 2)] * other
        return value

    partials = [total]
    sent = [(send0, sum(rows0))]
    for k in range(ITERS):
        rhs, rhs_a, rhs_b = (r0_main, r0_a, r0_b) if k == 0 else (r_main, r_a, r_b)
        rows = []
        last_one = k == ITERS - 1
        width, head = (3, 4) if last_one else (5, 2)

        def post(source, target, s):
            pltpu.make_async_remote_copy(
                src_ref=source, dst_ref=target, send_sem=sends.at[k], recv_sem=recvs.at[k],
                device_id=device(s), device_id_type=MESH,
            ).start()
            rows.append(rows_of(source))

        for before_ref, after_ref in (((rhs_a, rhs_b), (u_a, u_b)), ((u_a, u_b), (v_a, v_b))):
            after_ref[0][MIDDLE] = side_sweep(before_ref[0], rhs_a, w_a, 4)
            after_ref[1][MIDDLE] = side_sweep(before_ref[1], rhs_b, w_b, 5)
        side_a = side_sweep(v_a, rhs_a, w_a, 4)
        side_b = side_sweep(v_b, rhs_b, w_b, 5)
        far_b = roll(side_b, 64)
        send[k, 0] = jnp.where(lane < 60, side_a, far_b)
        send[k, 13] = jnp.where(lane < 60, far_b, side_a)
        send[k, 14] = side_a
        send[k, 15] = side_b
        for d, value in ((0, side_a), (1, side_b)):
            for u in range(2):
                fold_out[k, u, d] = fold(value, STEP * (8 if u else 1) - d)
        for s in DIRS:
            sz, sx, sy = s
            u, v, d = part_of(sz), part_of(sx), part_of(sy)
            if sy != 0:
                if sx != 0:
                    post(
                        send.at[k, 14 + d, strip(sx, width, 32 * v)],
                        rxy.at[k, sz + 1, v, d, strip(sx, width)], s,
                    )
                elif sz != 0:
                    post(fold_out.at[k, u, d], rzy.at[k, u, d], s)
                else:
                    post(send.at[k, 14 + d], ry.at[k, d], s)

        for z in range(1, 13, 2):
            u_main[plane(z, 2)] = main_sweep(rhs, rhs, z)
        for z in range(1, 13, 2):
            v_main[plane(z, 2)] = main_sweep(u_main, rhs, z)
        for z in (1, 3, 5, 11, 9, 7):
            value = main_sweep(v_main, rhs, z)
            send[k, z] = value[:ROWS]
            send[k, z + 1] = value[ROWS:]
            if z in (5, 7):
                sz = -1 if z == 5 else 1
                count = 4 if last_one else 6
                skip = 6 - count if sz > 0 else 0
                planes, places = pl.ds((8 if sz > 0 else 0) + skip, count), pl.ds(skip, count)
                u = part_of(sz)
                pieces = pl.ds(head + width * skip, width * count)
                for v, low in ((0, 2), (1, 38 - width)):
                    for i in range(skip, skip + count):
                        place = head + width * i
                        zx_out[k, u, v, place : place + width] = send[
                            k, (8 + i) if u else i, low : low + width
                        ]
                    post(
                        zx_out.at[k, u, v, pieces], rzx.at[k, u, v, pieces],
                        (sz, 2 * v - 1, 0),
                    )
                kept = pl.ds(3, 34) if last_one else pl.ds(2, 36)
                post(send.at[k, planes, kept], rz.at[k, u, places, kept], (sz, 0, 0))
        for sx in (-1, 1):
            v = part_of(sx)
            post(
                send.at[k, pl.ds(1, 15), strip(sx, width, 32 * v)],
                rx.at[k, v, :, strip(sx, width)], (0, sx, 0),
            )
        wait_rows(recvs.at[k], sum(rows))
        sent.append((sends.at[k], sum(rows)))

        def edge_rows(u, v, i):
            at = iota(0, (8, LANES))
            first = 6 - width if v else 2
            start = head + width * i - first
            tile = rzx[k, u, v, start : start + 8]
            return jnp.where(between(at, first, first + width - 1), tile, 0.0)

        new_p = []
        for own, d, offset, shift, y, low, high, outer_low, outer_high, ref in (
            (14, 1, 1, 0, y_pa, -2, 3, -3, 1, p_a),
            (15, 0, 4, 64, y_pb, -4, 1, -2, 2, p_b),
        ):
            here = add_tiles(
                z_sum(send[k, own], rz[k, 1, 5], rz[k, 0, 0], offset, shift),
                z_sum(rx[k, 1, own - 1], edge_rows(1, 1, 5), edge_rows(0, 1, 0), offset, shift),
                z_sum(rx[k, 0, own - 1], edge_rows(1, 0, 5), edge_rows(0, 0, 0), offset, shift),
            )
            other = beside(ry.at[k], rzy.at[k], rxy.at[k], d)
            value = jnp.where(between(y, low, high), here, 0.0) + jnp.where(
                between(y, outer_low, outer_high), other, 0.0
            )
            value = value * side_gain[1 - d]
            if k > 0:
                value = ref[MIDDLE] + value
            ref[MIDDLE] = value
            new_p.append(value)
        edges = jnp.where(between(y_pa, 0, 3), new_p[0], new_p[1])
        edge_lane = either(lane < 4, lane >= LANES - 4)
        for z in range(2, 12) if last_one else range(PLANES):
            solved = 1 <= z <= 12
            value = send[k, z] if solved else zero_plane
            first = rx[k, 1, z - 1] if solved else jnp.zeros((8, LANES), jnp.float32)
            last = rx[k, 0, z - 1] if solved else jnp.zeros((8, LANES), jnp.float32)
            if z <= 4:
                value = value + rz[k, 1, z]
                first = first + edge_rows(1, 1, z)
                last = last + edge_rows(1, 0, z)
            if z >= 9:
                value = value + rz[k, 0, z - 8]
                first = first + edge_rows(0, 1, z - 8)
                last = last + edge_rows(0, 0, z - 8)
            value = add_tiles(value, first, last) * (main_gain * z_gain(z))
            if k > 0:
                value = p_main[plane(z)] + value
            p_main[plane(z)] = jnp.where(edge_lane, roll(edges, -(STEP * z + 2)), value)

        total = zero_plane
        r_edges = (zero_plane, zero_plane)
        for z in range(3, 11) if last_one else range(1, 13):
            centre = p_main[plane(z)]
            value = r0_main[plane(z)] - alpha[plane(z)] * centre
            for i, other in enumerate(
                around(p_main, z) + (roll(centre, 1), roll(centre, -1))
            ):
                value = value + w_main[i, plane(z)] * other
            if not last_one:
                r_main[plane(z)] = value
                r_edges = gather(r_edges, z, value)
            if 3 <= z <= 10:
                value = value * scale[z - 3]
                total = total + value * value
        for i, (ref, r0, al, w_ref, r_ref, p) in enumerate(
            ((p_a, r0_a, alpha_a, w_a, r_a, new_p[0]), (p_b, r0_b, alpha_b, w_b, r_b, new_p[1]))
        ):
            value = r0[MIDDLE] - al[...] * p
            for n, other in enumerate(side_around(ref, p) + (roll(p, 1), roll(p, -1))):
                value = value + w_ref[n] * other
            if not last_one:
                r_ref[MIDDLE] = jnp.where(y_fa <= 0 if i == 0 else y_fb >= -1, value, r_edges[i])
            value = value * scale_side[i]
            total = total + value * value
        partials.append(total)

    at = iota(1, (1, LANES)) // 32
    mine = jnp.zeros((1, LANES), jnp.float32)
    for i, value in enumerate(partials):
        value = jnp.sum(value, axis=0, keepdims=True)
        value = value + roll(value, 64)
        mine = jnp.where(at == i, value + roll(value, 32), mine)
    pair = gy + 1 - 2 * lax.rem(gy, 2)

    def ring(i, n):
        return min(i, n - i)

    chips = sorted(
        (
            (i, j, h)
            for i in range(n_gx)
            for j in range(n_gy // 2)
            for h in range(n_gz)
            if (i, j, h) != (0, 0, 0)
        ),
        key=lambda t: -ring(t[0], n_gx) - ring(t[1], n_gy // 2) - ring(t[2], n_gz),
    )
    at_x = [lax.rem(gx + i, n_gx) for i in range(n_gx)]
    at_y = [lax.rem(gy + 2 * i, n_gy) for i in range(n_gy // 2)]
    at_z = [lax.rem(gz + i, n_gz) for i in range(n_gz)]
    rounds = (
        [(gx, pair, gz)],
        [
            (at_x[i], at_y[j], at_z[h])
            for i, j, h in chips
        ],
    )
    slots = (lax.rem(gy, 2), (gx * (n_gy // 2) + gy // 2) * n_gz + gz)
    for n, targets in enumerate(rounds):
        here = part_in.at[n, slots[n], pl.ds(0, 1)]
        part[n, 0:1] = mine
        for target in targets:
            pltpu.make_async_remote_copy(
                src_ref=part.at[n, pl.ds(0, 1)], dst_ref=here,
                send_sem=ar_send.at[n], recv_sem=ar_recv.at[n],
                device_id=target, device_id_type=MESH,
            ).start()
        here[...] = mine
        if n == 1:
            for z in range(8):
                out_ref[z] = p_main[pl.ds(PAD + ROWS * (z + 3) + 4, 32)]
        wait_rows(ar_recv.at[n], len(targets))
        sent.append((ar_send.at[n], len(targets)))
        terms = [part_in[n, i, 0:1] for i in range(len(targets) + 1)]
        while len(terms) > 1:
            terms = [sum(terms[i + 1 : i + 2], terms[i]) for i in range(0, len(terms), 2)]
        mine = terms[0]
    squares = [
        jnp.sum(jnp.where(at == i, mine, 0.0), axis=1, keepdims=True) for i in range(ITERS + 1)
    ]
    for i in range(ITERS):
        hist_ref[i] = jnp.sum(jnp.sqrt(squares[i + 1] / squares[0]))
    for sem, rows in sent:
        wait_rows(sem, rows)


def solution(mesh):
    sizes = (mesh.shape["gx"], mesh.shape["gy"], mesh.shape["gz"])
    f32 = jnp.float32

    def vmem(*shape):
        return pltpu.VMEM(shape, f32)

    scratch = [
        vmem(8, 32, LANES), vmem(8, 32, LANES), vmem(8, 32, LANES),
        pltpu.VMEM((32, LANES), jnp.int32),
        vmem(2, 8, 8, LANES), vmem(2, ROWS, LANES), vmem(2, 2, 16, LANES),
        vmem(2, 3, 32, LANES), vmem(2, 2, 32, LANES), vmem(2, 2, 32, LANES),
        vmem(2, 8, 8, LANES), vmem(2, 2, 3, 8, LANES),
        vmem(2, ROWS, LANES), vmem(2, 2, 16, LANES), vmem(3, 2, 2, 8, LANES),
        vmem(ITERS, 16, ROWS, LANES), vmem(ITERS, 2, 2, 32, LANES), vmem(ITERS, 2, 2, 16, LANES),
        vmem(ITERS, 2, 6, ROWS, LANES), vmem(ITERS, 2, 15, 8, LANES),
        vmem(ITERS, 2, 2, 40, LANES),
        vmem(ITERS, 2, ROWS, LANES), vmem(ITERS, 2, 2, 16, LANES), vmem(ITERS, 3, 2, 2, 8, LANES),
        vmem(FLAT, LANES), vmem(SIDE, LANES), vmem(SIDE, LANES), vmem(FLAT, LANES), vmem(FLAT, LANES),
        vmem(6, FLAT, LANES), vmem(7, ROWS, LANES), vmem(7, ROWS, LANES),
        vmem(FLAT, LANES), vmem(ROWS, LANES), vmem(ROWS, LANES), vmem(8, ROWS, LANES),
    ]
    for _ in range(5):
        scratch += [vmem(FLAT, LANES), vmem(SIDE, LANES), vmem(SIDE, LANES)]
    scratch += [
        pltpu.VMEM((2 * LANES, 2 * LANES), jnp.bfloat16),
        vmem(2, 8, LANES), vmem(2, 128, 8, LANES),
        vmem(2048, LANES),
        pltpu.SemaphoreType.DMA, pltpu.SemaphoreType.DMA, pltpu.SemaphoreType.DMA,
        pltpu.SemaphoreType.DMA((ITERS,)), pltpu.SemaphoreType.DMA((ITERS,)),
        pltpu.SemaphoreType.DMA((2,)), pltpu.SemaphoreType.DMA((2,)),
    ]

    def per_device(source, permeability, storage, column_depth):
        return pl.pallas_call(
            functools.partial(kernel, sizes),
            out_shape=(
                jax.ShapeDtypeStruct(source.shape, f32),
                jax.ShapeDtypeStruct((ITERS,), f32),
            ),
            in_specs=[pl.BlockSpec(memory_space=pl.ANY)] * 4,
            out_specs=(
                pl.BlockSpec(memory_space=pltpu.VMEM),
                pl.BlockSpec(memory_space=pltpu.SMEM),
            ),
            scratch_shapes=scratch,
            compiler_params=pltpu.CompilerParams(
                collective_id=0, has_side_effects=True, vmem_limit_bytes=55056 * 2**10
            ),
            name="schwarz",
        )(source, permeability, storage, column_depth)

    placed = (P("gz", "gx", "gy"), P("gz", "gx", "gy"), P("gz", "gx", "gy"), P("gx", "gy"))
    return jax.shard_map(
        per_device,
        mesh=mesh,
        in_specs=placed,
        out_specs=(P("gz", "gx", "gy"), P()),
        check_vma=False,
    )
```
